32 devices in a mesh: ty: 4 (over x, core), tx: 8 (over z, y).
Axes of the slice: x: 2, y: 2, z: 4, core: 2. Of those that a mesh axis runs over, the one named last changes fastest.
Arguments:
- latent: float32 [384, 768], P('ty', 'tx'), may hold values from -6 to 6
- kernels: float32 [2, 12, 129, 129], replicated, may hold values from -0.046875 to 0.046875
- socs_weights: float32 [12], replicated, may hold values from 0.01 to 0.1
- dose_scale: float32 [8], replicated, may hold values from 0.8 to 1.25
- inv_slope: float32 [4, 2048], P('ty', 'tx'), may hold values from 1 to 8
- edge_pixels: int32 [4, 2048], P('ty', 'tx'), may hold values from 0 to 9215
- threshold_pick: int32 [1], replicated, may hold values from 0 to 65535
Outputs:
- steering: float32 [384, 768], P('ty', 'tx')
- tail_mean: float32 [1], replicated
The draws below stay inside these ranges and needn't reach their ends.
Inputs may be any that keep to these rules, and one draw needn't show every extreme that they name: `edge_pixels`: each entry names a pixel of its own tile, numbered row by row.
All inputs are finite; a program needn't handle non-finite values.
Results may differ from the reference program's by a relative error of at most 0.0003.
Values sent between devices are 32-bit elements; how exact they have to be, the bound alone decides.
No kernel may reach another device: no remote copies, remote signals or barrier semaphores. Data moves between devices by JAX's collectives and lax.ppermute only.
A program may use at most 64 MiB of HBM per device.

```python
import math
import jax
import jax.numpy as jnp
from jax import lax

TILE = 96
KW = 129
KERNELS = 12
CORNERS = 8
SAMP = 256
NY = 384
NX = 768
N_TY = 4
N_TX = 8


def plant(values, own_key, smallest, high):
    longest = values.shape.index(max(values.shape))
    spots = []
    for shift in (0, 1):
        where = [jax.random.randint(jax.random.fold_in(own_key, axis), (), 0, length) for axis, length in enumerate(values.shape)]
        where[longest] = (where[longest] + shift) % values.shape[longest]
        spots.append(tuple(where))
    return values.at[spots[0]].set(smallest).at[spots[1]].set(high)


def block_scale(key, dims, split, smallest, top_value):
    factor_of, own = 1.0, jax.random.fold_in(key, 6)
    for axis_at, shards_of in split:
        heights = jnp.exp(jax.random.uniform(jax.random.fold_in(own, axis_at), (shards_of,), jnp.float32, smallest / len(split), top_value / len(split)))
        factor_of = factor_of * jnp.repeat(heights, dims[axis_at] // shards_of).reshape([-1 if axis == axis_at else 1 for axis in range(len(dims))])
    return factor_of


def normal_values(stream_key, shape, spread, limit, pieces=(), kind=jnp.bfloat16):
    array = jax.random.normal(stream_key, shape, jnp.float32) * spread
    if len(pieces) > 0:
        array = block_scale(stream_key, shape, pieces, -0.22, 0.18) * array
    return jnp.clip(array, min=-limit, max=limit).astype(kind)


def setup_inputs(seed: int = 0) -> dict:
    seeds = jax.random.split(jax.random.key(seed), 8)
    latent = normal_values(seeds[0], (NY, NX), 1.5, 6.0, ((0, 4), (1, 8)), jnp.float32)
    kernels = normal_values(seeds[1], (2, KERNELS, KW, KW), (KW * KW) ** -0.5, 0.046875, (), jnp.float32)
    socs_weights = jnp.clip(jnp.exp(jax.random.uniform(seeds[2], (KERNELS,), jnp.float32, math.log(0.01), math.log(0.1))), 0.01, 0.1)
    dose_scale = jnp.clip(jax.random.uniform(seeds[3], (CORNERS,), jnp.float32, 0.8, 1.25), 0.8, 1.25)
    inv_slope = jnp.clip(jnp.exp(math.log(8.0) - 2.0794415 * jax.random.uniform(seeds[4], (N_TY, N_TX * SAMP), jnp.float32) ** block_scale(seeds[4], (N_TY, N_TX * SAMP), ((0, 4), (1, 8)), -0.2, 0.2)), 1.0, 8.0)
    edge_pixels = plant(jax.random.randint(seeds[5], (N_TY, N_TX * SAMP), 0, TILE * TILE), jax.random.fold_in(seeds[5], 1), 0, (TILE * TILE) - 1).astype(jnp.int32)
    threshold_pick = jax.random.randint(seeds[6], (1,), 0, CORNERS * N_TY * N_TX * SAMP).astype(jnp.int32)
    return {"latent": latent, "kernels": kernels, "socs_weights": socs_weights, "dose_scale": dose_scale, "inv_slope": inv_slope, "edge_pixels": edge_pixels, "threshold_pick": threshold_pick}


STEEPNESS = 4.0
RESIST_LEVEL = 0.7
SOFTNESS = 0.25

def reference(latent, kernels, socs_weights, dose_scale, inv_slope, edge_pixels, threshold_pick):
    rows_all, cols_all = latent.shape
    radius = (KW - 1) // 2
    len_rows = rows_all + 2 * radius
    len_cols = cols_all + 2 * radius
    complex_kern = lax.complex(kernels[0], kernels[1])
    norm_weights = socs_weights / jnp.sum(socs_weights)

    def image(transmit):
        padded = jnp.pad(transmit, radius)
        mask_hat = jnp.fft.fft2(padded)

        def add_kernel(total, item):
            kern_one, weight_one = item
            spectrum = jnp.fft.ifft2(kern_one, s=(len_rows, len_cols)) * (len_rows * len_cols)
            field = jnp.fft.ifft2(mask_hat * spectrum)[:rows_all, :cols_all]
            return (total + weight_one * (field.real * field.real + field.imag * field.imag), None)
        total, unused = lax.scan(add_kernel, jnp.zeros_like(transmit), (complex_kern, norm_weights))
        return total
    sample_col = jnp.arange(N_TX * SAMP, dtype=jnp.int32)
    tile_top = (jnp.arange(N_TY, dtype=jnp.int32) * TILE)[:, None]
    pixel_row = tile_top + edge_pixels // TILE
    pixel_col = (sample_col // SAMP * TILE)[None, :] + edge_pixels % TILE

    def tail_loss(latent_in):
        transmit = 0.5 * (1.0 + jnp.tanh(latent_in))
        intensity = image(transmit)
        resist = jax.nn.sigmoid(STEEPNESS * (dose_scale[:, None, None] * intensity[None] - RESIST_LEVEL))
        sampled = resist[:, pixel_row, pixel_col]
        offset_err = (sampled - 0.5) * inv_slope[None]
        error = offset_err * offset_err
        threshold = lax.stop_gradient(error.reshape(-1)[threshold_pick[0]])
        soft = jax.nn.sigmoid((error - threshold) / SOFTNESS)
        return jnp.sum(error * soft) / jnp.sum(soft)
    tail_value, pullback = jax.vjp(tail_loss, latent)
    gradient = pullback(jnp.ones_like(tail_value))[0]
    count_all = CORNERS * N_TY * N_TX * SAMP
    return (gradient * count_all, tail_value.reshape(1))
```

```python
import functools
import math

import jax
import jax.numpy as jnp
import ml_dtypes
import numpy as np
from jax import lax
from jax.experimental import pallas as pl
from jax.experimental.pallas import tpu as pltpu
from jax.sharding import PartitionSpec as P

STEEPNESS = 4.0
RESIST_LEVEL = 0.7
SOFTNESS = 0.25
LANES = 128
F32 = jnp.float32
BF16 = jnp.bfloat16


def split(x):
    high = x.astype(BF16)
    return high, (x - high.astype(F32)).astype(BF16)


def split_table(table):
    high = table.astype(ml_dtypes.bfloat16)
    low = (table - high.astype(np.float64)).astype(ml_dtypes.bfloat16)
    return high, low


def dot(a, b):
    return jnp.dot(a, b, preferred_element_type=F32)


def dot3(a, b):
    return dot(a[0], b[0]) + dot(a[0], b[1]) + dot(a[1], b[0])


def load(pair):
    return pair[0][...], pair[1][...]


def waves(count, period):
    half = period // 2
    angle = (np.arange(half)[None, :] + 0.5) * np.arange(count)[:, None]
    angle = angle * (2.0 * math.pi / period)
    return np.cos(angle), np.sin(angle)


def on_lanes(count, period, rows):
    cos, sin = waves(count, period)
    half = period // 2
    out = np.zeros((rows, 2 * LANES))
    out[:count, :half] = cos
    out[:count, LANES : LANES + half] = sin
    return out


def on_rows(count, period):
    cos, sin = waves(count, period)
    return np.concatenate([cos, sin], axis=1).T


def halves(x):
    return x[:, :LANES], x[:, LANES:]


def spectra_kernel(kern, cb_hi, cb_lo, ca_hi, ca_lo, out_re, out_im):
    half = out_re.shape[1] // 2
    cols = load((cb_hi, cb_lo))
    rows = load((ca_hi, ca_lo))

    def step(k, carry):
        real_cos, real_sin = halves(dot3(split(kern[0, k]), cols))
        imag_cos, imag_sin = halves(dot3(split(kern[1, k]), cols))
        wide_re = jnp.concatenate([real_cos - imag_sin, real_cos + imag_sin], axis=1)
        wide_im = jnp.concatenate([real_sin + imag_cos, imag_cos - real_sin], axis=1)
        tall_re = dot3(rows, split(wide_re))
        tall_im = dot3(rows, split(wide_im))
        out_re[k, :half] = tall_re[:half] - tall_im[half:]
        out_re[k, half:] = tall_re[:half] + tall_im[half:]
        out_im[k, :half] = tall_im[:half] + tall_re[half:]
        out_im[k, half:] = tall_im[:half] - tall_re[half:]
        return carry

    lax.fori_loop(0, out_re.shape[0], step, 0)


def total_weight(weights, kernels):
    total = weights[0]
    for k in range(1, kernels):
        total = total + weights[k]
    return jnp.full((1, 1), total, F32)


def sample_places(pixels, tile):
    row = ((pixels.astype(F32) + 0.5) * (1.0 / tile)).astype(jnp.int32)
    return row, pixels - row * tile


def field_kernel(
    weights, spec_re, spec_im, middle, above, below, left, right, pixels, slopes,
    fj_hi, fj_lo, fi_hi, fi_lo, up_hi, up_lo, side_hi, side_lo,
    field_re, field_im, sampled, framed, mask,
):
    kernels, period, _ = spec_re.shape
    half = period // 2
    tile = field_re.shape[1]
    radius = above.shape[0]
    framed[:, period:] = jnp.zeros((period, 2 * LANES - period), F32)
    framed[:, :radius] = left[...]
    framed[:, radius + tile : period] = right[...]
    framed[:radius, radius : radius + tile] = above[...]
    framed[radius : radius + tile, radius : radius + tile] = middle[...]
    framed[radius + tile :, radius : radius + tile] = below[...]
    wide = dot3(split(framed[...]), load((fj_hi, fj_lo)))
    tall = dot3(load((fi_hi, fi_lo)), split(wide)) * (1.0 / (period * period))
    cos_cos, cos_sin = halves(tall[:half])
    sin_cos, sin_sin = halves(tall[half:])
    same, other = cos_cos - sin_sin, cos_cos + sin_sin
    joint, cross = sin_cos + cos_sin, sin_cos - cos_sin
    mask[0, :, :LANES], mask[0, :, LANES:] = same, other
    mask[1, :, :LANES], mask[1, :, LANES:] = -joint, -cross
    mask[2, :, :LANES], mask[2, :, LANES:] = other, same
    mask[3, :, :LANES], mask[3, :, LANES:] = cross, joint
    lift = load((up_hi, up_lo))
    across = load((side_hi, side_lo))

    def step(k, intensity):
        pos_re, pos_im = spec_re[k, :half], spec_im[k, :half]
        neg_re, neg_im = spec_re[k, half:], spec_im[k, half:]
        up_re = mask[0] * pos_re - mask[1] * pos_im
        up_im = mask[0] * pos_im + mask[1] * pos_re
        down_re = mask[2] * neg_re - mask[3] * neg_im
        down_im = mask[2] * neg_im + mask[3] * neg_re
        for_re = jnp.concatenate([up_re + down_re, down_im - up_im], axis=0)
        for_im = jnp.concatenate([up_im + down_im, up_re - down_re], axis=0)
        re_pos, re_neg = halves(dot3(lift, split(for_re)))
        im_pos, im_neg = halves(dot3(lift, split(for_im)))
        rows_re = jnp.concatenate([re_pos + re_neg, im_neg - im_pos], axis=1)
        rows_im = jnp.concatenate([im_pos + im_neg, re_pos - re_neg], axis=1)
        real = dot3(split(rows_re), across)
        imag = dot3(split(rows_im), across)
        field_re[k] = real
        field_im[k] = imag
        return intensity + weights[k] * (real * real + imag * imag)

    intensity = lax.fori_loop(0, kernels, step, jnp.zeros((tile, LANES), F32))
    intensity = intensity / total_weight(weights, kernels)
    samples = pixels.shape[1]
    row, col = sample_places(pixels[...], tile)
    in_col = lax.broadcasted_iota(jnp.int32, (LANES, samples), 0) == col
    one_hot = jnp.where(in_col, 1.0, 0.0).astype(BF16)
    high, rest = split(intensity)
    low = intensity - high.astype(F32) - rest.astype(F32)
    picked = dot(high, one_hot) + dot(rest, one_hot) + dot(low.astype(BF16), one_hot)
    in_row = lax.broadcasted_iota(jnp.int32, (tile, samples), 0) == row
    sampled[:, :samples] = jnp.sum(jnp.where(in_row, picked, 0.0), axis=0, keepdims=True)
    sampled[:, samples:] = slopes[...]


def sigmoid(x):
    return 1.0 / (1.0 + jnp.exp(-x))


def errors(intensity, slope, dose):
    resist = sigmoid(STEEPNESS * (dose * intensity - RESIST_LEVEL))
    offset = (resist - 0.5) * slope
    return resist, offset, offset * offset


def gradient_kernel(
    weights, doses, pick, me, gathered, pixels, spec_re, spec_im, field_re, field_im,
    sj_hi, sj_lo, si_hi, si_lo, bi_hi, bi_lo, bj_hi, bj_lo,
    left, middle, right, tail, total_re, total_im,
):
    kernels, period, _ = spec_re.shape
    half = period // 2
    tile = field_re.shape[1]
    radius = (period - tile) // 2
    samples = pixels.shape[1]
    devices = gathered.shape[0]
    corners = doses.shape[0]
    per_corner = devices * samples
    everyone, every_slope = gathered[:, :samples], gathered[:, samples:]
    pick_corner = pick[0] // per_corner
    remain = pick[0] - pick_corner * per_corner
    owner = lax.broadcasted_iota(jnp.int32, (devices, samples), 0) ^ me[0]
    place = owner * samples + lax.broadcasted_iota(jnp.int32, (devices, samples), 1)
    _, _, picked = errors(everyone, every_slope, doses[pick_corner])
    threshold = jnp.sum(jnp.where(place == remain, picked, 0.0), keepdims=True)

    def corner(c, sums):
        _, _, error = errors(everyone, every_slope, doses[c])
        soft = sigmoid((error - threshold) * (1.0 / SOFTNESS))
        return sums[0] + soft, sums[1] + error * soft

    zero = jnp.zeros((devices, samples), F32)
    soft_sum, error_sum = lax.fori_loop(0, corners, corner, (zero, zero))
    soft_total = jnp.sum(soft_sum, keepdims=True)
    tail_mean = jnp.sum(error_sum, keepdims=True) / soft_total
    tail[...] = tail_mean

    own, slope = gathered[:1, :samples], gathered[:1, samples:]
    which = lax.broadcasted_iota(jnp.int32, (corners, samples), 0)
    dose = jnp.zeros((corners, samples), F32)
    for c in range(corners):
        dose = jnp.where(which == c, doses[c], dose)
    resist, offset, error = errors(own, slope, dose)
    soft = sigmoid((error - threshold) * (1.0 / SOFTNESS))
    slope_soft = soft * (1.0 - soft) * (1.0 / SOFTNESS)
    chain = 2.0 * STEEPNESS * offset * slope * dose * resist * (1.0 - resist)
    coefficient = (soft + (error - tail_mean) * slope_soft) * (corners * per_corner / soft_total)
    summed = jnp.sum(coefficient * chain, axis=0, keepdims=True)
    summed = summed / total_weight(weights, kernels)

    row, col = sample_places(pixels[...], tile)
    in_row = lax.broadcasted_iota(jnp.int32, (tile, samples), 0) == row
    in_col = lax.broadcasted_iota(jnp.int32, (LANES, samples), 0) == col
    one_hot = jnp.where(in_col, 1.0, 0.0).astype(BF16)
    placed = jnp.where(in_row, summed, 0.0)
    high, rest = split(placed)
    low = (placed - high.astype(F32) - rest.astype(F32)).astype(BF16)
    grid = jnp.zeros((tile, LANES), F32)
    for part in (high, rest, low):
        grid = grid + lax.dot_general(
            part, one_hot, (((1,), (1,)), ((), ())), preferred_element_type=F32
        )

    cols = load((sj_hi, sj_lo))
    rows = load((si_hi, si_lo))
    total_re[...] = jnp.zeros((period, 2 * LANES), F32)
    total_im[...] = jnp.zeros((period, 2 * LANES), F32)

    def step(k, carry):
        weighted = grid * weights[k]
        real_cos, real_sin = halves(dot3(split(weighted * field_re[k]), cols))
        imag_cos, imag_sin = halves(dot3(split(weighted * field_im[k]), cols))
        wide_re = jnp.concatenate([real_cos + imag_sin, real_cos - imag_sin], axis=1)
        wide_im = jnp.concatenate([imag_cos - real_sin, imag_cos + real_sin], axis=1)
        tall_re = dot3(rows, split(wide_re))
        tall_im = dot3(rows, split(wide_im))
        for first, sign in ((0, 1.0), (half, -1.0)):
            part = slice(first, first + half)
            wave_re = tall_re[:half] + sign * tall_im[half:]
            wave_im = tall_im[:half] - sign * tall_re[half:]
            own_re, own_im = spec_re[k, part], spec_im[k, part]
            total_re[part] += own_re * wave_re + own_im * wave_im
            total_im[part] += own_re * wave_im - own_im * wave_re
        return carry

    lax.fori_loop(0, kernels, step, 0)
    pos_re, neg_re = total_re[:half], total_re[half:]
    pos_im, neg_im = total_im[:half], total_im[half:]
    back_rows = load((bi_hi, bi_lo))
    for_re = jnp.concatenate([pos_re + neg_re, neg_im - pos_im], axis=0)
    for_im = jnp.concatenate([pos_im + neg_im, pos_re - neg_re], axis=0)
    re_pos, re_neg = halves(dot3(back_rows, split(for_re)))
    im_pos, im_neg = halves(dot3(back_rows, split(for_im)))
    last = jnp.concatenate([re_pos + re_neg, im_neg - im_pos], axis=1)
    grad = dot3(split(last), load((bj_hi, bj_lo))) * (2.0 / (period * period))
    left[...] = grad[:, :radius]
    middle[...] = grad[:, radius : radius + tile]
    right[...] = grad[:, radius + tile : period]


VMEM = pl.BlockSpec(memory_space=pltpu.VMEM)
SMEM = pl.BlockSpec(memory_space=pltpu.SMEM)
PARAMS = pltpu.CompilerParams(vmem_limit_bytes=32 * 1024 * 1024)


def shape(*dims):
    return jax.ShapeDtypeStruct(dims, F32)


def shifted(x, axis, by):
    peers = lax.axis_size(axis)
    pairs = [(i, i + by) for i in range(peers) if 0 <= i + by < peers]
    return lax.ppermute(x, axis, pairs)


def gather_all(x):
    axes = ("ty", "tx")
    count = lax.axis_size("ty") * lax.axis_size("tx")
    step = 1
    while step < count:
        other = lax.ppermute(x, axes, [(i, i ^ step) for i in range(count)])
        x = jnp.concatenate([x, other], axis=0)
        step *= 2
    return x


def body(latent, kernels, socs_weights, dose_scale, inv_slope, edge_pixels, threshold_pick):
    tile = latent.shape[0]
    count, taps = kernels.shape[1], kernels.shape[-1]
    samples = edge_pixels.shape[1]
    radius = (taps - 1) // 2
    period = tile + 2 * radius
    half = period // 2

    transmit = 0.5 * (1.0 + jnp.tanh(latent))
    above = shifted(transmit[tile - radius :], "ty", 1)
    below = shifted(transmit[:radius], "ty", -1)

    spec_re, spec_im = pl.pallas_call(
        spectra_kernel,
        out_shape=[shape(count, period, 2 * LANES)] * 2,
        in_specs=[VMEM] * 5,
        out_specs=[VMEM] * 2,
        compiler_params=PARAMS,
        name="spectra",
    )(
        kernels,
        *split_table(on_lanes(taps, period, taps)),
        *split_table(on_rows(taps, period)),
    )

    column = jnp.concatenate([above, transmit, below], axis=0)
    left = shifted(column[:, tile - radius :], "tx", 1)
    right = shifted(column[:, :radius], "tx", -1)

    lift = on_rows(tile, period).T
    across = np.zeros((2 * LANES, LANES))
    across[:, :tile] = on_lanes(tile, period, tile).T
    field_re, field_im, sampled = pl.pallas_call(
        field_kernel,
        out_shape=[shape(count, tile, LANES)] * 2 + [shape(1, 2 * samples)],
        in_specs=[SMEM] + [VMEM] * 17,
        out_specs=[VMEM] * 3,
        scratch_shapes=[
            pltpu.VMEM((period, 2 * LANES), F32),
            pltpu.VMEM((4, half, 2 * LANES), F32),
        ],
        compiler_params=PARAMS,
        name="field",
    )(
        socs_weights, spec_re, spec_im, transmit, above, below, left, right,
        edge_pixels, inv_slope,
        *split_table(on_lanes(period, period, 2 * LANES)),
        *split_table(on_rows(period, period)),
        *split_table(lift),
        *split_table(across),
    )

    gathered = gather_all(sampled)
    me = lax.axis_index("ty") * lax.axis_size("tx") + lax.axis_index("tx")
    grad_left, grad_middle, grad_right, tail_mean = pl.pallas_call(
        gradient_kernel,
        out_shape=[shape(period, radius), shape(period, tile), shape(period, radius), shape(1, 1)],
        in_specs=[SMEM] * 4 + [VMEM] * 14,
        out_specs=[VMEM] * 4,
        scratch_shapes=[pltpu.VMEM((period, 2 * LANES), F32)] * 2,
        compiler_params=PARAMS,
        name="gradient",
    )(
        socs_weights, dose_scale, threshold_pick, me.astype(jnp.int32).reshape(1),
        gathered, edge_pixels, spec_re, spec_im, field_re, field_im,
        *split_table(on_lanes(tile, period, LANES)),
        *split_table(on_rows(tile, period)),
        *split_table(on_rows(period, period).T),
        *split_table(on_lanes(period, period, 2 * LANES).T),
    )

    from_left = shifted(grad_right, "tx", 1)
    from_right = shifted(grad_left, "tx", -1)
    rest = tile - radius
    column = (
        grad_middle
        + jnp.pad(from_left, ((0, 0), (0, rest)))
        + jnp.pad(from_right, ((0, 0), (rest, 0)))
    )
    from_above = shifted(column[radius + tile :], "ty", 1)
    from_below = shifted(column[:radius], "ty", -1)
    mask_grad = (
        column[radius : radius + tile]
        + jnp.pad(from_above, ((0, rest), (0, 0)))
        + jnp.pad(from_below, ((rest, 0), (0, 0)))
    )
    tanh_value = jnp.tanh(latent)
    steering = mask_grad * 0.5 * (1.0 - tanh_value * tanh_value)
    return (steering, tail_mean.reshape(1))


def solution(mesh):
    placed = (P("ty", "tx"), P(), P(), P(), P("ty", "tx"), P("ty", "tx"), P())
    return jax.shard_map(
        body, mesh=mesh, in_specs=placed, out_specs=(P("ty", "tx"), P()), check_vma=False
    )
```

```python
import functools
import math

import jax
import jax.numpy as jnp
import numpy as np
from jax import lax
from jax.experimental import pallas as pl
from jax.experimental.pallas import tpu as pltpu
from jax.sharding import PartitionSpec as P

STEEPNESS = 4.0
RESIST_LEVEL = 0.7
SOFTNESS = 0.25
LANES = 128
F32 = jnp.float32
BF16 = jnp.bfloat16


def split(x):
    high = x.astype(BF16)
    return high, (x - high.astype(F32)).astype(BF16)


def dot(a, b):
    return jnp.dot(a, b, preferred_element_type=F32)


def dot3(a, b):
    return dot(a[0], b[0]) + dot(a[0], b[1]) + dot(a[1], b[0])


def wave_tables(period):
    half = period // 2
    place = np.arange(period)
    angle = (np.arange(half)[None, :] + 0.5) * place[:, None] * (2.0 * math.pi / period)
    cos, sin = np.cos(angle), np.sin(angle)
    out = np.zeros((4, 2 * LANES, 2 * LANES))
    out[0, :period, :half] = cos
    out[0, :period, LANES : LANES + half] = sin
    out[1] = out[0].T
    out[2, :half, :period] = cos.T
    out[2, half:period, :period] = sin.T
    out[3] = out[2].T
    return out.astype(np.float32)


def halves(x):
    return x[:, :LANES], x[:, LANES:]


def edge_flags(axis):
    index, count = lax.axis_index(axis), lax.axis_size(axis)
    return lax.rem(index, 2) == 0, index > 0, index < count - 1


def sides(axis, first, second):
    even, lower, higher = edge_flags(axis)
    from_lower = jnp.where(lower, jnp.where(even, second, first), 0.0)
    from_higher = jnp.where(higher, jnp.where(even, first, second), 0.0)
    return from_lower, from_higher


def ordered(axis, for_lower, for_higher):
    even = lax.rem(lax.axis_index(axis), 2) == 0
    return jnp.where(even, for_higher, for_lower), jnp.where(even, for_lower, for_higher)


def exchange(axis, first, second):
    count = lax.axis_size(axis)
    out = []
    for offset, value in ((0, first), (1, second)):
        pairs = [(i, i) for i in range(count)]
        for low in range(offset, count - 1, 2):
            pairs[low], pairs[low + 1] = (low, low + 1), (low + 1, low)
        out.append(lax.ppermute(value, axis, pairs))
    return out


def spectra_kernel(start, kern, tables, *rest):
    out_re, out_im, token, planes, sems = rest[-5:]
    period = out_re.shape[1]
    half = period // 2
    taps = kern.shape[-1]
    parts = planes.shape[0]

    def fetch(k):
        return pltpu.make_async_copy(kern.at[:, start + k], planes.at[k], sems.at[k])

    for k in range(parts):
        fetch(k).start()
    cols = split(tables[0, :taps, :])
    rows = split(tables[2, :period, :taps])
    token[...] = jnp.zeros(token.shape, F32)

    def step(k, carry):
        fetch(k).wait()
        real_cos, real_sin = halves(dot3(split(planes[k, 0]), cols))
        imag_cos, imag_sin = halves(dot3(split(planes[k, 1]), cols))
        wide_re = jnp.concatenate([real_cos - imag_sin, real_cos + imag_sin], axis=1)
        wide_im = jnp.concatenate([real_sin + imag_cos, imag_cos - real_sin], axis=1)
        tall_re = dot3(rows, split(wide_re))
        tall_im = dot3(rows, split(wide_im))
        out_re[start + k, :half] = tall_re[:half] - tall_im[half:]
        out_re[start + k, half:] = tall_re[:half] + tall_im[half:]
        out_im[start + k, :half] = tall_im[:half] + tall_re[half:]
        out_im[start + k, half:] = tall_im[:half] - tall_re[half:]
        return carry

    lax.fori_loop(0, parts, step, 0)


def column_kernel(middle, first, second, after, column, next_first, next_second, token):
    tile = middle.shape[0]
    radius = first.shape[0]
    above, below = sides("ty", first[...], second[...])
    column[:radius] = above
    column[radius : radius + tile] = middle[...]
    column[radius + tile :] = below
    next_first[...], next_second[...] = ordered(
        "tx", column[:, :radius], column[:, tile - radius :]
    )
    token[...] = jnp.zeros(token.shape, F32)


def total_weight(weights, kernels):
    total = weights[0]
    for k in range(1, kernels):
        total = total + weights[k]
    return jnp.full((1, 1), total, F32)


def sample_places(pixels, tile):
    row = ((pixels.astype(F32) + 0.5) * (1.0 / tile)).astype(jnp.int32)
    return row, pixels - row * tile


def field_kernel(
    weights, spec_re, spec_im, column, first, second, pixels, slopes, tables,
    field_re, field_im, sampled, framed, mask,
):
    kernels, period, _ = spec_re.shape
    half = period // 2
    tile = field_re.shape[1]
    radius = first.shape[1]
    left, right = sides("tx", first[...], second[...])
    framed[:, period:] = jnp.zeros((period, 2 * LANES - period), F32)
    framed[:, :radius] = left
    framed[:, radius + tile : period] = right
    framed[:, radius : radius + tile] = column[...]
    wide = dot3(split(framed[...]), split(tables[0]))
    tall = dot3(split(tables[2, :period, :period]), split(wide)) * (1.0 / (period * period))
    cos_cos, cos_sin = halves(tall[:half])
    sin_cos, sin_sin = halves(tall[half:])
    same, other = cos_cos - sin_sin, cos_cos + sin_sin
    joint, cross = sin_cos + cos_sin, sin_cos - cos_sin
    mask[0, :, :LANES], mask[0, :, LANES:] = same, other
    mask[1, :, :LANES], mask[1, :, LANES:] = -joint, -cross
    mask[2, :, :LANES], mask[2, :, LANES:] = other, same
    mask[3, :, :LANES], mask[3, :, LANES:] = cross, joint
    lift = split(tables[3, :tile, :period])
    across = split(tables[1, :, :LANES])

    def step(k, intensity):
        pos_re, pos_im = spec_re[k, :half], spec_im[k, :half]
        neg_re, neg_im = spec_re[k, half:], spec_im[k, half:]
        up_re = mask[0] * pos_re - mask[1] * pos_im
        up_im = mask[0] * pos_im + mask[1] * pos_re
        down_re = mask[2] * neg_re - mask[3] * neg_im
        down_im = mask[2] * neg_im + mask[3] * neg_re
        for_re = jnp.concatenate([up_re + down_re, down_im - up_im], axis=0)
        for_im = jnp.concatenate([up_im + down_im, up_re - down_re], axis=0)
        re_pos, re_neg = halves(dot3(lift, split(for_re)))
        im_pos, im_neg = halves(dot3(lift, split(for_im)))
        rows_re = jnp.concatenate([re_pos + re_neg, im_neg - im_pos], axis=1)
        rows_im = jnp.concatenate([im_pos + im_neg, re_pos - re_neg], axis=1)
        real = dot3(split(rows_re), across)
        imag = dot3(split(rows_im), across)
        field_re[k] = real
        field_im[k] = imag
        return intensity + weights[k] * (real * real + imag * imag)

    intensity = lax.fori_loop(0, kernels, step, jnp.zeros((tile, LANES), F32))
    intensity = intensity / total_weight(weights, kernels)
    samples = pixels.shape[1]
    row, col = sample_places(pixels[...], tile)
    in_col = lax.broadcasted_iota(jnp.int32, (LANES, samples), 0) == col
    one_hot = jnp.where(in_col, 1.0, 0.0).astype(BF16)
    high, rest = split(intensity)
    low = intensity - high.astype(F32) - rest.astype(F32)
    picked = dot(high, one_hot) + dot(rest, one_hot) + dot(low.astype(BF16), one_hot)
    in_row = lax.broadcasted_iota(jnp.int32, (tile, samples), 0) == row
    sampled[:, :samples] = jnp.sum(jnp.where(in_row, picked, 0.0), axis=0, keepdims=True)
    sampled[:, samples:] = slopes[...]


def sigmoid(x):
    return 1.0 / (1.0 + jnp.exp(-x))


def errors(intensity, slope, dose):
    resist = sigmoid(STEEPNESS * (dose * intensity - RESIST_LEVEL))
    offset = (resist - 0.5) * slope
    return resist, offset, offset * offset


def gradient_kernel(
    weights, doses, pick, gathered, sampled, pixels, spec_re, spec_im, field_re, field_im,
    tables, middle, first, second, tail, total_re, total_im,
):
    kernels, period, _ = spec_re.shape
    half = period // 2
    tile = field_re.shape[1]
    radius = (period - tile) // 2
    samples = pixels.shape[1]
    devices = gathered.shape[0]
    corners = doses.shape[0]
    per_corner = devices * samples
    everyone, every_slope = gathered[:, :samples], gathered[:, samples:]
    pick_corner = pick[0] // per_corner
    remain = pick[0] - pick_corner * per_corner
    place = lax.broadcasted_iota(jnp.int32, (devices, samples), 0) * samples
    place = place + lax.broadcasted_iota(jnp.int32, (devices, samples), 1)
    _, _, picked = errors(everyone, every_slope, doses[pick_corner])
    threshold = jnp.sum(jnp.where(place == remain, picked, 0.0), keepdims=True)

    def corner(c, sums):
        _, _, error = errors(everyone, every_slope, doses[c])
        soft = sigmoid((error - threshold) * (1.0 / SOFTNESS))
        return sums[0] + soft, sums[1] + error * soft

    zero = jnp.zeros((devices, samples), F32)
    soft_sum, error_sum = lax.fori_loop(0, corners, corner, (zero, zero))
    soft_total = jnp.sum(soft_sum, keepdims=True)
    tail_mean = jnp.sum(error_sum, keepdims=True) / soft_total
    tail[...] = tail_mean

    own, slope = sampled[:, :samples], sampled[:, samples:]
    which = lax.broadcasted_iota(jnp.int32, (corners, samples), 0)
    dose = jnp.zeros((corners, samples), F32)
    for c in range(corners):
        dose = jnp.where(which == c, doses[c], dose)
    resist, offset, error = errors(own, slope, dose)
    soft = sigmoid((error - threshold) * (1.0 / SOFTNESS))
    slope_soft = soft * (1.0 - soft) * (1.0 / SOFTNESS)
    chain = 2.0 * STEEPNESS * offset * slope * dose * resist * (1.0 - resist)
    coefficient = (soft + (error - tail_mean) * slope_soft) * (corners * per_corner / soft_total)
    summed = jnp.sum(coefficient * chain, axis=0, keepdims=True)
    summed = summed / total_weight(weights, kernels)

    row, col = sample_places(pixels[...], tile)
    in_row = lax.broadcasted_iota(jnp.int32, (tile, samples), 0) == row
    in_col = lax.broadcasted_iota(jnp.int32, (LANES, samples), 0) == col
    one_hot = jnp.where(in_col, 1.0, 0.0).astype(BF16)
    placed = jnp.where(in_row, summed, 0.0)
    high, rest = split(placed)
    low = (placed - high.astype(F32) - rest.astype(F32)).astype(BF16)
    grid = jnp.zeros((tile, LANES), F32)
    for part in (high, rest, low):
        grid = grid + lax.dot_general(
            part, one_hot, (((1,), (1,)), ((), ())), preferred_element_type=F32
        )

    cols = split(tables[0, :LANES])
    rows = split(tables[2, :period, :tile])
    total_re[...] = jnp.zeros((period, 2 * LANES), F32)
    total_im[...] = jnp.zeros((period, 2 * LANES), F32)

    def step(k, carry):
        weighted = grid * weights[k]
        real_cos, real_sin = halves(dot3(split(weighted * field_re[k]), cols))
        imag_cos, imag_sin = halves(dot3(split(weighted * field_im[k]), cols))
        wide_re = jnp.concatenate([real_cos + imag_sin, real_cos - imag_sin], axis=1)
        wide_im = jnp.concatenate([imag_cos - real_sin, imag_cos + real_sin], axis=1)
        tall_re = dot3(rows, split(wide_re))
        tall_im = dot3(rows, split(wide_im))
        for start, sign in ((0, 1.0), (half, -1.0)):
            part = slice(start, start + half)
            wave_re = tall_re[:half] + sign * tall_im[half:]
            wave_im = tall_im[:half] - sign * tall_re[half:]
            own_re, own_im = spec_re[k, part], spec_im[k, part]
            total_re[part] += own_re * wave_re + own_im * wave_im
            total_im[part] += own_re * wave_im - own_im * wave_re
        return carry

    lax.fori_loop(0, kernels, step, 0)
    pos_re, neg_re = total_re[:half], total_re[half:]
    pos_im, neg_im = total_im[:half], total_im[half:]
    back_rows = split(tables[3, :period, :period])
    for_re = jnp.concatenate([pos_re + neg_re, neg_im - pos_im], axis=0)
    for_im = jnp.concatenate([pos_im + neg_im, pos_re - neg_re], axis=0)
    re_pos, re_neg = halves(dot3(back_rows, split(for_re)))
    im_pos, im_neg = halves(dot3(back_rows, split(for_im)))
    last = jnp.concatenate([re_pos + re_neg, im_neg - im_pos], axis=1)
    grad = dot3(split(last), split(tables[1])) * (2.0 / (period * period))
    middle[...] = grad[:, radius : radius + tile]
    first[...], second[...] = ordered("tx", grad[:, :radius], grad[:, radius + tile : period])


VMEM = pl.BlockSpec(memory_space=pltpu.VMEM)
SMEM = pl.BlockSpec(memory_space=pltpu.SMEM)
ANY = pl.BlockSpec(memory_space=pl.ANY)


def shape(*dims):
    return jax.ShapeDtypeStruct(dims, F32)


def call(kernel, name, out_shape, in_specs, scratch=(), aliases=None, micros=1):
    return pl.pallas_call(
        kernel,
        out_shape=out_shape,
        in_specs=in_specs,
        out_specs=[VMEM] * len(out_shape),
        scratch_shapes=scratch,
        input_output_aliases=aliases or {},
        compiler_params=pltpu.CompilerParams(vmem_limit_bytes=10 * 1024 * 1024),
        cost_estimate=pl.CostEstimate(
            flops=micros * 10**9, bytes_accessed=2**20, transcendentals=0
        ),
        name=name,
    )


def gather_all(x):
    return lax.all_gather(x, ("ty", "tx"), axis=0, tiled=True)


def body(latent, kernels, socs_weights, dose_scale, inv_slope, edge_pixels, threshold_pick):
    tile = latent.shape[0]
    count, taps = kernels.shape[1], kernels.shape[-1]
    samples = edge_pixels.shape[1]
    radius = (taps - 1) // 2
    period = tile + 2 * radius
    half = period // 2
    tables = jnp.asarray(wave_tables(period))
    token = shape(8, LANES)

    transmit = 0.5 * (1.0 + jnp.tanh(latent))
    rims = exchange("ty", *ordered("ty", transmit[:radius], transmit[tile - radius :]))

    parts = count // 2
    spec = []
    after = []
    for part in range(2):
        given = spec + after
        *spec, done = call(
            functools.partial(spectra_kernel, part * parts),
            "spectra",
            [shape(count, period, 2 * LANES)] * 2 + [token],
            [ANY, VMEM] + [ANY] * len(given),
            scratch=[
                pltpu.VMEM((parts, 2, taps, taps), F32),
                pltpu.SemaphoreType.DMA((parts,)),
            ],
            aliases={2: 0, 3: 1} if spec else None,
            micros=3,
        )(kernels, tables, *given)
        if part == 0:
            column, *rims, done = call(
                column_kernel,
                "column",
                [shape(period, tile)] + [shape(period, radius)] * 2 + [token],
                [VMEM] * 3 + [ANY],
            )(transmit, *rims, done)
            after = [done]
            rims = exchange("tx", *rims)

    field_re, field_im, sampled = call(
        field_kernel,
        "field",
        [shape(count, tile, LANES)] * 2 + [shape(1, 2 * samples)],
        [SMEM] + [VMEM] * 8,
        scratch=[
            pltpu.VMEM((period, 2 * LANES), F32),
            pltpu.VMEM((4, half, 2 * LANES), F32),
        ],
        micros=7,
    )(socs_weights, *spec, column, *rims, edge_pixels, inv_slope, tables)

    gathered = gather_all(sampled)
    grad_middle, first, second, tail_mean = call(
        gradient_kernel,
        "gradient",
        [shape(period, tile)] + [shape(period, radius)] * 2 + [shape(1, 1)],
        [SMEM] * 3 + [VMEM] * 8,
        scratch=[pltpu.VMEM((period, 2 * LANES), F32)] * 2,
        micros=9,
    )(
        socs_weights, dose_scale, threshold_pick, gathered, sampled, edge_pixels,
        *spec, field_re, field_im, tables,
    )

    rest = tile - radius
    from_left, from_right = sides("tx", *exchange("tx", first, second))
    column = (
        grad_middle
        + jnp.pad(from_left, ((0, 0), (0, rest)))
        + jnp.pad(from_right, ((0, 0), (rest, 0)))
    )
    rims = exchange("ty", *ordered("ty", column[:radius], column[radius + tile :]))
    from_above, from_below = sides("ty", *rims)
    mask_grad = (
        column[radius : radius + tile]
        + jnp.pad(from_above, ((0, rest), (0, 0)))
        + jnp.pad(from_below, ((rest, 0), (0, 0)))
    )
    tanh_value = jnp.tanh(latent)
    steering = mask_grad * 0.5 * (1.0 - tanh_value * tanh_value)
    return (steering, tail_mean.reshape(1))


def solution(mesh):
    placed = (P("ty", "tx"), P(), P(), P(), P("ty", "tx"), P("ty", "tx"), P())
    return jax.shard_map(
        body, mesh=mesh, in_specs=placed, out_specs=(P("ty", "tx"), P()), check_vma=False
    )
```

```python
import functools
import math

import jax
import jax.numpy as jnp
import numpy as np
from jax import lax
from jax.experimental import pallas as pl
from jax.experimental.pallas import tpu as pltpu
from jax.sharding import PartitionSpec as P

STEEPNESS = 4.0
RESIST_LEVEL = 0.7
SOFTNESS = 0.25
LANES = 128
F32 = jnp.float32
BF16 = jnp.bfloat16


def split(x):
    high = x.astype(BF16)
    return high, (x - high.astype(F32)).astype(BF16)


def dot(a, b):
    return jnp.dot(a, b, preferred_element_type=F32)


def dot3(a, b):
    return dot(a[0], b[0]) + dot(a[0], b[1]) + dot(a[1], b[0])


def wave_tables(period):
    half = period // 2
    place = np.arange(period)
    angle = (np.arange(half)[None, :] + 0.5) * place[:, None] * (2.0 * math.pi / period)
    cos, sin = np.cos(angle), np.sin(angle)
    out = np.zeros((4, 2 * LANES, 2 * LANES))
    out[0, :period, :half] = cos
    out[0, :period, LANES : LANES + half] = sin
    out[1] = out[0].T
    out[2, :half, :period] = cos.T
    out[2, half:period, :period] = sin.T
    out[3] = out[2].T
    return out.astype(np.float32)


def halves(x):
    return x[:, :LANES], x[:, LANES:]


def edge_flags(axis):
    index, count = lax.axis_index(axis), lax.axis_size(axis)
    return lax.rem(index, 2) == 0, index > 0, index < count - 1


def sides(axis, first, second):
    even, lower, higher = edge_flags(axis)
    from_lower = jnp.where(lower, jnp.where(even, second, first), 0.0)
    from_higher = jnp.where(higher, jnp.where(even, first, second), 0.0)
    return from_lower, from_higher


def ordered(axis, for_lower, for_higher):
    even = lax.rem(lax.axis_index(axis), 2) == 0
    return jnp.where(even, for_higher, for_lower), jnp.where(even, for_lower, for_higher)


def exchange(axis, first, second):
    count = lax.axis_size(axis)
    out = []
    for offset, value in ((0, first), (1, second)):
        pairs = [(i, i) for i in range(count)]
        for low in range(offset, count - 1, 2):
            pairs[low], pairs[low + 1] = (low, low + 1), (low + 1, low)
        out.append(lax.ppermute(value, axis, pairs))
    return out


def spectra_kernel(start, kern, tables, *rest):
    out_re, out_im, token, planes, sems = rest[-5:]
    period = out_re.shape[1]
    half = period // 2
    taps = kern.shape[-1]
    parts = planes.shape[0]

    def fetch(k):
        return pltpu.make_async_copy(kern.at[:, start + k], planes.at[k], sems.at[k])

    for k in range(parts):
        fetch(k).start()
    cols = split(tables[0, :taps, :])
    rows = split(tables[2, :period, :taps])
    token[...] = jnp.zeros(token.shape, F32)

    def step(k, carry):
        fetch(k).wait()
        real_cos, real_sin = halves(dot3(split(planes[k, 0]), cols))
        imag_cos, imag_sin = halves(dot3(split(planes[k, 1]), cols))
        wide_re = jnp.concatenate([real_cos - imag_sin, real_cos + imag_sin], axis=1)
        wide_im = jnp.concatenate([real_sin + imag_cos, imag_cos - real_sin], axis=1)
        tall_re = dot3(rows, split(wide_re))
        tall_im = dot3(rows, split(wide_im))
        out_re[start + k, :half] = tall_re[:half] - tall_im[half:]
        out_re[start + k, half:] = tall_re[:half] + tall_im[half:]
        out_im[start + k, :half] = tall_im[:half] + tall_re[half:]
        out_im[start + k, half:] = tall_im[:half] - tall_re[half:]
        return carry

    lax.fori_loop(0, parts, step, 0)


def column_kernel(middle, first, second, after, column, next_first, next_second, token):
    tile = middle.shape[0]
    radius = first.shape[0]
    above, below = sides("ty", first[...], second[...])
    column[:radius] = above
    column[radius : radius + tile] = middle[...]
    column[radius + tile :] = below
    next_first[...], next_second[...] = ordered(
        "tx", column[:, :radius], column[:, tile - radius :]
    )
    token[...] = jnp.zeros(token.shape, F32)


def total_weight(weights, kernels):
    total = weights[0]
    for k in range(1, kernels):
        total = total + weights[k]
    return jnp.full((1, 1), total, F32)


def sample_places(pixels, tile):
    row = ((pixels.astype(F32) + 0.5) * (1.0 / tile)).astype(jnp.int32)
    return row, pixels - row * tile


def field_kernel(
    weights, spec_re, spec_im, column, first, second, pixels, slopes, tables,
    field_re, field_im, sampled, framed, mask,
):
    kernels, period, _ = spec_re.shape
    half = period // 2
    tile = field_re.shape[1]
    radius = first.shape[1]
    left, right = sides("tx", first[...], second[...])
    framed[:, period:] = jnp.zeros((period, 2 * LANES - period), F32)
    framed[:, :radius] = left
    framed[:, radius + tile : period] = right
    framed[:, radius : radius + tile] = column[...]
    wide = dot3(split(framed[...]), split(tables[0]))
    tall = dot3(split(tables[2, :period, :period]), split(wide)) * (1.0 / (period * period))
    cos_cos, cos_sin = halves(tall[:half])
    sin_cos, sin_sin = halves(tall[half:])
    same, other = cos_cos - sin_sin, cos_cos + sin_sin
    joint, cross = sin_cos + cos_sin, sin_cos - cos_sin
    mask[0, :, :LANES], mask[0, :, LANES:] = same, other
    mask[1, :, :LANES], mask[1, :, LANES:] = -joint, -cross
    mask[2, :, :LANES], mask[2, :, LANES:] = other, same
    mask[3, :, :LANES], mask[3, :, LANES:] = cross, joint
    lift = split(tables[3, :tile, :period])
    across = split(tables[1, :, :LANES])

    def step(k, intensity):
        pos_re, pos_im = spec_re[k, :half], spec_im[k, :half]
        neg_re, neg_im = spec_re[k, half:], spec_im[k, half:]
        up_re = mask[0] * pos_re - mask[1] * pos_im
        up_im = mask[0] * pos_im + mask[1] * pos_re
        down_re = mask[2] * neg_re - mask[3] * neg_im
        down_im = mask[2] * neg_im + mask[3] * neg_re
        for_re = jnp.concatenate([up_re + down_re, down_im - up_im], axis=0)
        for_im = jnp.concatenate([up_im + down_im, up_re - down_re], axis=0)
        re_pos, re_neg = halves(dot3(lift, split(for_re)))
        im_pos, im_neg = halves(dot3(lift, split(for_im)))
        rows_re = jnp.concatenate([re_pos + re_neg, im_neg - im_pos], axis=1)
        rows_im = jnp.concatenate([im_pos + im_neg, re_pos - re_neg], axis=1)
        real = dot3(split(rows_re), across)
        imag = dot3(split(rows_im), across)
        field_re[k] = real
        field_im[k] = imag
        return intensity + weights[k] * (real * real + imag * imag)

    intensity = lax.fori_loop(0, kernels, step, jnp.zeros((tile, LANES), F32))
    intensity = intensity / total_weight(weights, kernels)
    samples = pixels.shape[1]
    row, col = sample_places(pixels[...], tile)
    in_col = lax.broadcasted_iota(jnp.int32, (LANES, samples), 0) == col
    one_hot = jnp.where(in_col, 1.0, 0.0).astype(BF16)
    high, rest = split(intensity)
    low = intensity - high.astype(F32) - rest.astype(F32)
    picked = dot(high, one_hot) + dot(rest, one_hot) + dot(low.astype(BF16), one_hot)
    in_row = lax.broadcasted_iota(jnp.int32, (tile, samples), 0) == row
    sampled[:, :samples] = jnp.sum(jnp.where(in_row, picked, 0.0), axis=0, keepdims=True)
    sampled[:, samples:] = slopes[...]


def sigmoid(x):
    return 1.0 / (1.0 + jnp.exp(-x))


def errors(intensity, slope, dose):
    resist = sigmoid(STEEPNESS * (dose * intensity - RESIST_LEVEL))
    offset = (resist - 0.5) * slope
    return resist, offset, offset * offset


def gradient_kernel(
    weights, doses, pick, gathered, sampled, pixels, spec_re, spec_im, field_re, field_im,
    tables, middle, first, second, tail, total_re, total_im,
):
    kernels, period, _ = spec_re.shape
    half = period // 2
    tile = field_re.shape[1]
    radius = (period - tile) // 2
    samples = pixels.shape[1]
    devices = gathered.shape[0]
    corners = doses.shape[0]
    per_corner = devices * samples
    everyone, every_slope = gathered[:, :samples], gathered[:, samples:]
    pick_corner = pick[0] // per_corner
    remain = pick[0] - pick_corner * per_corner
    place = lax.broadcasted_iota(jnp.int32, (devices, samples), 0) * samples
    place = place + lax.broadcasted_iota(jnp.int32, (devices, samples), 1)
    _, _, picked = errors(everyone, every_slope, doses[pick_corner])
    threshold = jnp.sum(jnp.where(place == remain, picked, 0.0), keepdims=True)

    def corner(c, sums):
        _, _, error = errors(everyone, every_slope, doses[c])
        soft = sigmoid((error - threshold) * (1.0 / SOFTNESS))
        return sums[0] + soft, sums[1] + error * soft

    zero = jnp.zeros((devices, samples), F32)
    soft_sum, error_sum = lax.fori_loop(0, corners, corner, (zero, zero))
    soft_total = jnp.sum(soft_sum, keepdims=True)
    tail_mean = jnp.sum(error_sum, keepdims=True) / soft_total
    tail[...] = tail_mean

    own, slope = sampled[:, :samples], sampled[:, samples:]
    which = lax.broadcasted_iota(jnp.int32, (corners, samples), 0)
    dose = jnp.zeros((corners, samples), F32)
    for c in range(corners):
        dose = jnp.where(which == c, doses[c], dose)
    resist, offset, error = errors(own, slope, dose)
    soft = sigmoid((error - threshold) * (1.0 / SOFTNESS))
    slope_soft = soft * (1.0 - soft) * (1.0 / SOFTNESS)
    chain = 2.0 * STEEPNESS * offset * slope * dose * resist * (1.0 - resist)
    coefficient = (soft + (error - tail_mean) * slope_soft) * (corners * per_corner / soft_total)
    summed = jnp.sum(coefficient * chain, axis=0, keepdims=True)
    summed = summed / total_weight(weights, kernels)

    row, col = sample_places(pixels[...], tile)
    in_row = lax.broadcasted_iota(jnp.int32, (tile, samples), 0) == row
    in_col = lax.broadcasted_iota(jnp.int32, (LANES, samples), 0) == col
    one_hot = jnp.where(in_col, 1.0, 0.0).astype(BF16)
    placed = jnp.where(in_row, summed, 0.0)
    high, rest = split(placed)
    low = (placed - high.astype(F32) - rest.astype(F32)).astype(BF16)
    grid = jnp.zeros((tile, LANES), F32)
    for part in (high, rest, low):
        grid = grid + lax.dot_general(
            part, one_hot, (((1,), (1,)), ((), ())), preferred_element_type=F32
        )

    cols = split(tables[0, :LANES])
    rows = split(tables[2, :period, :tile])
    total_re[...] = jnp.zeros((period, 2 * LANES), F32)
    total_im[...] = jnp.zeros((period, 2 * LANES), F32)

    def step(k, carry):
        weighted = grid * weights[k]
        real_cos, real_sin = halves(dot3(split(weighted * field_re[k]), cols))
        imag_cos, imag_sin = halves(dot3(split(weighted * field_im[k]), cols))
        wide_re = jnp.concatenate([real_cos + imag_sin, real_cos - imag_sin], axis=1)
        wide_im = jnp.concatenate([imag_cos - real_sin, imag_cos + real_sin], axis=1)
        tall_re = dot3(rows, split(wide_re))
        tall_im = dot3(rows, split(wide_im))
        for start, sign in ((0, 1.0), (half, -1.0)):
            part = slice(start, start + half)
            wave_re = tall_re[:half] + sign * tall_im[half:]
            wave_im = tall_im[:half] - sign * tall_re[half:]
            own_re, own_im = spec_re[k, part], spec_im[k, part]
            total_re[part] += own_re * wave_re + own_im * wave_im
            total_im[part] += own_re * wave_im - own_im * wave_re
        return carry

    lax.fori_loop(0, kernels, step, 0)
    pos_re, neg_re = total_re[:half], total_re[half:]
    pos_im, neg_im = total_im[:half], total_im[half:]
    back_rows = split(tables[3, :period, :period])
    for_re = jnp.concatenate([pos_re + neg_re, neg_im - pos_im], axis=0)
    for_im = jnp.concatenate([pos_im + neg_im, pos_re - neg_re], axis=0)
    re_pos, re_neg = halves(dot3(back_rows, split(for_re)))
    im_pos, im_neg = halves(dot3(back_rows, split(for_im)))
    last = jnp.concatenate([re_pos + re_neg, im_neg - im_pos], axis=1)
    grad = dot3(split(last), split(tables[1])) * (2.0 / (period * period))
    middle[...] = grad[:, radius : radius + tile]
    first[...], second[...] = ordered("tx", grad[:, :radius], grad[:, radius + tile : period])


VMEM = pl.BlockSpec(memory_space=pltpu.VMEM)
SMEM = pl.BlockSpec(memory_space=pltpu.SMEM)
ANY = pl.BlockSpec(memory_space=pl.ANY)


def shape(*dims):
    return jax.ShapeDtypeStruct(dims, F32)


def call(kernel, name, out_shape, in_specs, scratch=(), aliases=None, micros=1):
    return pl.pallas_call(
        kernel,
        out_shape=out_shape,
        in_specs=in_specs,
        out_specs=[VMEM] * len(out_shape),
        scratch_shapes=scratch,
        input_output_aliases=aliases or {},
        compiler_params=pltpu.CompilerParams(vmem_limit_bytes=10 * 1024 * 1024),
        cost_estimate=pl.CostEstimate(
            flops=micros * 10**9, bytes_accessed=2**20, transcendentals=0
        ),
        name=name,
    )


def gather_all(x):
    count = lax.axis_size("ty") * lax.axis_size("tx")
    copies = jnp.broadcast_to(x, (count, x.shape[1]))
    return lax.all_to_all(copies, ("ty", "tx"), 0, 0, tiled=True)


def body(latent, kernels, socs_weights, dose_scale, inv_slope, edge_pixels, threshold_pick):
    tile = latent.shape[0]
    count, taps = kernels.shape[1], kernels.shape[-1]
    samples = edge_pixels.shape[1]
    radius = (taps - 1) // 2
    period = tile + 2 * radius
    half = period // 2
    tables = jnp.asarray(wave_tables(period))
    token = shape(8, LANES)

    transmit = 0.5 * (1.0 + jnp.tanh(latent))
    rims = exchange("ty", *ordered("ty", transmit[:radius], transmit[tile - radius :]))

    parts = count // 2
    spec = []
    after = []
    for part in range(2):
        given = spec + after
        *spec, done = call(
            functools.partial(spectra_kernel, part * parts),
            "spectra",
            [shape(count, period, 2 * LANES)] * 2 + [token],
            [ANY, VMEM] + [ANY] * len(given),
            scratch=[
                pltpu.VMEM((parts, 2, taps, taps), F32),
                pltpu.SemaphoreType.DMA((parts,)),
            ],
            aliases={2: 0, 3: 1} if spec else None,
            micros=3,
        )(kernels, tables, *given)
        if part == 0:
            column, *rims, done = call(
                column_kernel,
                "column",
                [shape(period, tile)] + [shape(period, radius)] * 2 + [token],
                [VMEM] * 3 + [ANY],
            )(transmit, *rims, done)
            after = [done]
            rims = exchange("tx", *rims)

    field_re, field_im, sampled = call(
        field_kernel,
        "field",
        [shape(count, tile, LANES)] * 2 + [shape(1, 2 * samples)],
        [SMEM] + [VMEM] * 8,
        scratch=[
            pltpu.VMEM((period, 2 * LANES), F32),
            pltpu.VMEM((4, half, 2 * LANES), F32),
        ],
        micros=7,
    )(socs_weights, *spec, column, *rims, edge_pixels, inv_slope, tables)

    gathered = gather_all(sampled)
    grad_middle, first, second, tail_mean = call(
        gradient_kernel,
        "gradient",
        [shape(period, tile)] + [shape(period, radius)] * 2 + [shape(1, 1)],
        [SMEM] * 3 + [VMEM] * 8,
        scratch=[pltpu.VMEM((period, 2 * LANES), F32)] * 2,
        micros=9,
    )(
        socs_weights, dose_scale, threshold_pick, gathered, sampled, edge_pixels,
        *spec, field_re, field_im, tables,
    )

    rest = tile - radius
    from_left, from_right = sides("tx", *exchange("tx", first, second))
    column = (
        grad_middle
        + jnp.pad(from_left, ((0, 0), (0, rest)))
        + jnp.pad(from_right, ((0, 0), (rest, 0)))
    )
    rims = exchange("ty", *ordered("ty", column[:radius], column[radius + tile :]))
    from_above, from_below = sides("ty", *rims)
    mask_grad = (
        column[radius : radius + tile]
        + jnp.pad(from_above, ((0, rest), (0, 0)))
        + jnp.pad(from_below, ((rest, 0), (0, 0)))
    )
    tanh_value = jnp.tanh(latent)
    steering = mask_grad * 0.5 * (1.0 - tanh_value * tanh_value)
    return (steering, tail_mean.reshape(1))


def solution(mesh):
    placed = (P("ty", "tx"), P(), P(), P(), P("ty", "tx"), P("ty", "tx"), P())
    return jax.shard_map(
        body, mesh=mesh, in_specs=placed, out_specs=(P("ty", "tx"), P()), check_vma=False
    )
```

```python
import functools
import math

import jax
import jax.numpy as jnp
import numpy as np
from jax import lax
from jax.experimental import pallas as pl
from jax.experimental.pallas import tpu as pltpu
from jax.sharding import PartitionSpec as P

STEEPNESS = 4.0
RESIST_LEVEL = 0.7
SOFTNESS = 0.25
LANES = 128
UNROLL = 3
F32 = jnp.float32
BF16 = jnp.bfloat16


def split(x):
    high = x.astype(BF16)
    return high, (x - high.astype(F32)).astype(BF16)


def dot(a, b):
    return jnp.dot(a, b, preferred_element_type=F32)


def dot3(a, b):
    return dot(a[0], b[0]) + dot(a[0], b[1]) + dot(a[1], b[0])


def stacked(pair):
    return jnp.concatenate(pair, axis=0)


def dot3_stacked(a, b):
    high, both = a
    count = high.shape[0]
    tall = dot(both, b[0])
    return tall[:count] + tall[count:] + dot(high, b[1])


def wave_tables(period):
    half = period // 2
    place = np.arange(period)
    angle = (np.arange(half)[None, :] + 0.5) * place[:, None] * (2.0 * math.pi / period)
    cos, sin = np.cos(angle), np.sin(angle)
    out = np.zeros((4, 2 * LANES, 2 * LANES))
    out[0, :period, :half] = cos
    out[0, :period, LANES : LANES + half] = sin
    out[1] = out[0].T
    out[2, :half, :period] = cos.T
    out[2, half:period, :period] = sin.T
    out[3] = out[2].T
    return out.astype(np.float32)


def halves(x):
    return x[:, :LANES], x[:, LANES:]


def edge_flags(axis):
    index, count = lax.axis_index(axis), lax.axis_size(axis)
    return lax.rem(index, 2) == 0, index > 0, index < count - 1


def sides(axis, first, second):
    even, lower, higher = edge_flags(axis)
    from_lower = jnp.where(lower, jnp.where(even, second, first), 0.0)
    from_higher = jnp.where(higher, jnp.where(even, first, second), 0.0)
    return from_lower, from_higher


def ordered(axis, for_lower, for_higher):
    even = lax.rem(lax.axis_index(axis), 2) == 0
    return jnp.where(even, for_higher, for_lower), jnp.where(even, for_lower, for_higher)


def exchange(axis, first, second):
    count = lax.axis_size(axis)
    out = []
    for offset, value in ((0, first), (1, second)):
        pairs = [(i, i) for i in range(count)]
        for low in range(offset, count - 1, 2):
            pairs[low], pairs[low + 1] = (low, low + 1), (low + 1, low)
        out.append(lax.ppermute(value, axis, pairs))
    return out


def spectra_kernel(start, parts, kern, tables, *rest):
    out_re, out_im, token = rest[-3:]
    period = out_re.shape[1]
    half = period // 2
    taps = kern.shape[-1]
    cols = split(tables[0, :taps, :])
    rows = split(tables[2, :period, :taps])
    rows = (rows[0], stacked(rows))
    token[...] = jnp.zeros(token.shape, F32)

    def step(k, carry):
        real_cos, real_sin = halves(dot3(split(kern[0, start + k]), cols))
        imag_cos, imag_sin = halves(dot3(split(kern[1, start + k]), cols))
        wide_re = jnp.concatenate([real_cos - imag_sin, real_cos + imag_sin], axis=1)
        wide_im = jnp.concatenate([real_sin + imag_cos, imag_cos - real_sin], axis=1)
        tall_re = dot3_stacked(rows, split(wide_re))
        tall_im = dot3_stacked(rows, split(wide_im))
        out_re[start + k, :half] = tall_re[:half] - tall_im[half:]
        out_re[start + k, half:] = tall_re[:half] + tall_im[half:]
        out_im[start + k, :half] = tall_im[:half] + tall_re[half:]
        out_im[start + k, half:] = tall_im[:half] - tall_re[half:]
        return carry

    lax.fori_loop(0, parts, step, 0, unroll=UNROLL)


def pack(x):
    count = x.shape[0] // 2
    return jnp.concatenate([x[:count], x[count:]], axis=1)


def unpack(x):
    width = x.shape[1] // 2
    return jnp.concatenate([x[:, :width], x[:, width:]], axis=0)


def start_kernel(latent, transmit, first, second):
    tile = latent.shape[0]
    radius = first.shape[1] // 2
    value = 0.5 * (1.0 + jnp.tanh(latent[...]))
    transmit[...] = value
    first[...], second[...] = ordered(
        "tx", pack(value[:, :radius]), pack(value[:, tile - radius :])
    )


def band_kernel(middle, first, second, after, band, next_first, next_second, token):
    tile = middle.shape[0]
    radius = first.shape[1] // 2
    left, right = sides("tx", first[...], second[...])
    band[:, :radius] = unpack(left)
    band[:, radius : radius + tile] = middle[...]
    band[:, radius + tile :] = unpack(right)
    next_first[...], next_second[...] = ordered(
        "ty", band[:radius], band[tile - radius :]
    )
    token[...] = jnp.zeros(token.shape, F32)


def join_kernel(own, other, out):
    count = own.shape[0]
    out[:count] = own[...]
    out[count:] = other[...]


def fold_kernel(grad, first, second, band, next_first, next_second):
    tile = band.shape[0]
    radius = first.shape[0]
    above, below = sides("ty", first[...], second[...])
    band[...] = grad[radius : radius + tile]
    band[:radius] += above
    band[tile - radius :] += below
    period = band.shape[1]
    next_first[...], next_second[...] = ordered(
        "tx", pack(band[:, :radius]), pack(band[:, period - radius :])
    )


def finish_kernel(band, first, second, latent, steering):
    tile = latent.shape[0]
    radius = first.shape[1] // 2
    left, right = sides("tx", first[...], second[...])
    steering[...] = band[:, radius : radius + tile]
    steering[:, :radius] += unpack(left)
    steering[:, tile - radius :] += unpack(right)
    value = jnp.tanh(latent[...])
    steering[...] = steering[...] * 0.5 * (1.0 - value * value)


def total_weight(weights, kernels):
    total = weights[0]
    for k in range(1, kernels):
        total = total + weights[k]
    return jnp.full((1, 1), total, F32)


def sample_places(pixels, tile):
    row = ((pixels.astype(F32) + 0.5) * (1.0 / tile)).astype(jnp.int32)
    return row, pixels - row * tile


def field_kernel(
    weights, spec_re, spec_im, band, first, second, pixels, slopes, tables,
    field_re, field_im, sampled, framed, mask,
):
    kernels, period, _ = spec_re.shape
    half = period // 2
    tile = field_re.shape[1]
    radius = first.shape[0]
    above, below = sides("ty", first[...], second[...])
    framed[:radius] = above
    framed[radius + tile :] = below
    framed[radius : radius + tile] = band[...]
    wide = dot3(split(framed[...]), split(tables[0, :period]))
    tall = dot3(split(tables[2, :period, :period]), split(wide)) * (1.0 / (period * period))
    cos_cos, cos_sin = halves(tall[:half])
    sin_cos, sin_sin = halves(tall[half:])
    same, other = cos_cos - sin_sin, cos_cos + sin_sin
    joint, cross = sin_cos + cos_sin, sin_cos - cos_sin
    mask[0, :, :LANES], mask[0, :, LANES:] = same, other
    mask[1, :, :LANES], mask[1, :, LANES:] = -joint, -cross
    mask[2, :, :LANES], mask[2, :, LANES:] = other, same
    mask[3, :, :LANES], mask[3, :, LANES:] = cross, joint
    lift = split(tables[3, :tile, :period])
    lift = (lift[0], stacked(lift))
    across = split(tables[1, :, :LANES])

    def step(k, intensity):
        pos_re, pos_im = spec_re[k, :half], spec_im[k, :half]
        neg_re, neg_im = spec_re[k, half:], spec_im[k, half:]
        up_re = mask[0] * pos_re - mask[1] * pos_im
        up_im = mask[0] * pos_im + mask[1] * pos_re
        down_re = mask[2] * neg_re - mask[3] * neg_im
        down_im = mask[2] * neg_im + mask[3] * neg_re
        for_re = jnp.concatenate([up_re + down_re, down_im - up_im], axis=0)
        for_im = jnp.concatenate([up_im + down_im, up_re - down_re], axis=0)
        re_pos, re_neg = halves(dot3_stacked(lift, split(for_re)))
        im_pos, im_neg = halves(dot3_stacked(lift, split(for_im)))
        rows_re = jnp.concatenate([re_pos + re_neg, im_neg - im_pos], axis=1)
        rows_im = jnp.concatenate([im_pos + im_neg, re_pos - re_neg], axis=1)
        both = dot3(split(stacked((rows_re, rows_im))), across)
        real, imag = both[:tile], both[tile:]
        field_re[k] = real
        field_im[k] = imag
        return intensity + weights[k] * (real * real + imag * imag)

    intensity = lax.fori_loop(
        0, kernels, step, jnp.zeros((tile, LANES), F32), unroll=UNROLL
    )
    intensity = intensity / total_weight(weights, kernels)
    samples = pixels.shape[1]
    row, col = sample_places(pixels[...], tile)
    in_col = lax.broadcasted_iota(jnp.int32, (LANES, samples), 0) == col
    one_hot = jnp.where(in_col, 1.0, 0.0).astype(BF16)
    high, rest = split(intensity)
    low = intensity - high.astype(F32) - rest.astype(F32)
    picked = dot(high, one_hot) + dot(rest, one_hot) + dot(low.astype(BF16), one_hot)
    in_row = lax.broadcasted_iota(jnp.int32, (tile, samples), 0) == row
    sampled[:, :samples] = jnp.sum(jnp.where(in_row, picked, 0.0), axis=0, keepdims=True)
    sampled[:, samples:] = slopes[...]


def sigmoid(x):
    return 1.0 / (1.0 + jnp.exp(-x))


def errors(intensity, slope, dose):
    resist = sigmoid(STEEPNESS * (dose * intensity - RESIST_LEVEL))
    offset = (resist - 0.5) * slope
    return resist, offset, offset * offset


def gradient_kernel(
    weights, doses, pick, gathered, sampled, pixels, spec_re, spec_im, field_re, field_im,
    tables, grad, first, second, tail, total_re, total_im,
):
    kernels, period, _ = spec_re.shape
    half = period // 2
    tile = field_re.shape[1]
    radius = (period - tile) // 2
    samples = pixels.shape[1]
    devices = gathered.shape[0]
    corners = doses.shape[0]
    per_corner = devices * samples
    everyone, every_slope = gathered[:, :samples], gathered[:, samples:]
    pick_corner = pick[0] // per_corner
    remain = pick[0] - pick_corner * per_corner
    me = lax.axis_index("ty") * lax.axis_size("tx") + lax.axis_index("tx")
    place = (lax.broadcasted_iota(jnp.int32, (devices, samples), 0) ^ me) * samples
    place = place + lax.broadcasted_iota(jnp.int32, (devices, samples), 1)
    _, _, picked = errors(everyone, every_slope, doses[pick_corner])
    threshold = jnp.sum(jnp.where(place == remain, picked, 0.0), keepdims=True)

    def corner(c, sums):
        _, _, error = errors(everyone, every_slope, doses[c])
        soft = sigmoid((error - threshold) * (1.0 / SOFTNESS))
        return sums[0] + soft, sums[1] + error * soft

    zero = jnp.zeros((devices, samples), F32)
    soft_sum, error_sum = lax.fori_loop(
        0, corners, corner, (zero, zero), unroll=4 if devices <= 32 else 1
    )
    soft_total = jnp.sum(soft_sum, keepdims=True)
    tail_mean = jnp.sum(error_sum, keepdims=True) / soft_total
    tail[...] = tail_mean

    own, slope = sampled[:, :samples], sampled[:, samples:]
    which = lax.broadcasted_iota(jnp.int32, (corners, samples), 0)
    dose = jnp.zeros((corners, samples), F32)
    for c in range(corners):
        dose = jnp.where(which == c, doses[c], dose)
    resist, offset, error = errors(own, slope, dose)
    soft = sigmoid((error - threshold) * (1.0 / SOFTNESS))
    slope_soft = soft * (1.0 - soft) * (1.0 / SOFTNESS)
    chain = 2.0 * STEEPNESS * offset * slope * dose * resist * (1.0 - resist)
    coefficient = (soft + (error - tail_mean) * slope_soft) * (corners * per_corner / soft_total)
    summed = jnp.sum(coefficient * chain, axis=0, keepdims=True)
    summed = summed / total_weight(weights, kernels)

    row, col = sample_places(pixels[...], tile)
    in_row = lax.broadcasted_iota(jnp.int32, (tile, samples), 0) == row
    in_col = lax.broadcasted_iota(jnp.int32, (LANES, samples), 0) == col
    one_hot = jnp.where(in_col, 1.0, 0.0).astype(BF16)
    placed = jnp.where(in_row, summed, 0.0)
    high, rest = split(placed)
    low = (placed - high.astype(F32) - rest.astype(F32)).astype(BF16)
    grid = jnp.zeros((tile, LANES), F32)
    for part in (high, rest, low):
        grid = grid + lax.dot_general(
            part, one_hot, (((1,), (1,)), ((), ())), preferred_element_type=F32
        )

    cols = split(tables[0, :LANES])
    rows = split(tables[2, :period, :tile])
    rows = (rows[0], stacked(rows))
    total_re[...] = jnp.zeros((period, 2 * LANES), F32)
    total_im[...] = jnp.zeros((period, 2 * LANES), F32)

    def step(k, carry):
        weighted = grid * weights[k]
        source = stacked((weighted * field_re[k], weighted * field_im[k]))
        both = dot3(split(source), cols)
        real_cos, real_sin = halves(both[:tile])
        imag_cos, imag_sin = halves(both[tile:])
        wide_re = jnp.concatenate([real_cos + imag_sin, real_cos - imag_sin], axis=1)
        wide_im = jnp.concatenate([imag_cos - real_sin, imag_cos + real_sin], axis=1)
        tall_re = dot3_stacked(rows, split(wide_re))
        tall_im = dot3_stacked(rows, split(wide_im))
        for start, sign in ((0, 1.0), (half, -1.0)):
            part = slice(start, start + half)
            wave_re = tall_re[:half] + sign * tall_im[half:]
            wave_im = tall_im[:half] - sign * tall_re[half:]
            own_re, own_im = spec_re[k, part], spec_im[k, part]
            total_re[part] += own_re * wave_re + own_im * wave_im
            total_im[part] += own_re * wave_im - own_im * wave_re
        return carry

    lax.fori_loop(0, kernels, step, 0, unroll=UNROLL)
    pos_re, neg_re = total_re[:half], total_re[half:]
    pos_im, neg_im = total_im[:half], total_im[half:]
    back_rows = split(tables[3, :period, :period])
    for_re = jnp.concatenate([pos_re + neg_re, neg_im - pos_im], axis=0)
    for_im = jnp.concatenate([pos_im + neg_im, pos_re - neg_re], axis=0)
    re_pos, re_neg = halves(dot3(back_rows, split(for_re)))
    im_pos, im_neg = halves(dot3(back_rows, split(for_im)))
    last = jnp.concatenate([re_pos + re_neg, im_neg - im_pos], axis=1)
    framed = dot3(split(last), split(tables[1, :, :period])) * (2.0 / (period * period))
    grad[...] = framed
    first[...], second[...] = ordered("ty", framed[:radius], framed[radius + tile :])


VMEM = pl.BlockSpec(memory_space=pltpu.VMEM)
SMEM = pl.BlockSpec(memory_space=pltpu.SMEM)
ANY = pl.BlockSpec(memory_space=pl.ANY)


def shape(*dims):
    return jax.ShapeDtypeStruct(dims, F32)


def call(kernel, name, out_shape, in_specs, scratch=(), aliases=None, micros=1):
    return pl.pallas_call(
        kernel,
        out_shape=out_shape,
        in_specs=in_specs,
        out_specs=[VMEM] * len(out_shape),
        scratch_shapes=scratch,
        input_output_aliases=aliases or {},
        compiler_params=pltpu.CompilerParams(vmem_limit_bytes=10 * 1024 * 1024),
        cost_estimate=pl.CostEstimate(
            flops=micros * 10**9, bytes_accessed=2**20, transcendentals=0
        ),
        name=name,
    )


def gather_all(x):
    count = lax.axis_size("ty") * lax.axis_size("tx")
    step = 1
    while step < count:
        other = lax.ppermute(x, ("ty", "tx"), [(i, i ^ step) for i in range(count)])
        joined = [shape(2 * step, x.shape[1])]
        (x,) = call(join_kernel, "join", joined, [VMEM] * 2)(x, other)
        step *= 2
    return x


def body(latent, kernels, socs_weights, dose_scale, inv_slope, edge_pixels, threshold_pick):
    tile = latent.shape[0]
    count, taps = kernels.shape[1], kernels.shape[-1]
    samples = edge_pixels.shape[1]
    radius = (taps - 1) // 2
    period = tile + 2 * radius
    half = period // 2
    tables = jnp.asarray(wave_tables(period))
    token = shape(8, LANES)
    packed = [shape(tile // 2, 2 * radius)] * 2
    rim = [shape(radius, period)] * 2

    transmit, *rims = call(
        start_kernel, "start", [shape(tile, tile)] + packed, [VMEM]
    )(latent)
    rims = exchange("tx", *rims)

    parts = count // 2
    spec = []
    after = []
    for part in range(2):
        given = spec + after
        *spec, done = call(
            functools.partial(spectra_kernel, part * parts, parts),
            "spectra",
            [shape(count, period, 2 * LANES)] * 2 + [token],
            [VMEM] * 2 + [ANY] * len(given),
            aliases={2: 0, 3: 1} if spec else None,
            micros=3,
        )(kernels, tables, *given)
        if part == 0:
            band, *rims, done = call(
                band_kernel,
                "band",
                [shape(tile, period)] + rim + [token],
                [VMEM] * 3 + [ANY],
            )(transmit, *rims, done)
            after = [done]
            rims = exchange("ty", *rims)

    field_re, field_im, sampled = call(
        field_kernel,
        "field",
        [shape(count, tile, LANES)] * 2 + [shape(1, 2 * samples)],
        [SMEM] + [VMEM] * 8,
        scratch=[
            pltpu.VMEM((period, period), F32),
            pltpu.VMEM((4, half, 2 * LANES), F32),
        ],
        micros=7,
    )(socs_weights, *spec, band, *rims, edge_pixels, inv_slope, tables)

    gathered = gather_all(sampled)
    grad, *rims, tail_mean = call(
        gradient_kernel,
        "gradient",
        [shape(period, period)] + rim + [shape(1, 1)],
        [SMEM] * 3 + [VMEM] * 8,
        scratch=[pltpu.VMEM((period, 2 * LANES), F32)] * 2,
        micros=9,
    )(
        socs_weights, dose_scale, threshold_pick, gathered, sampled, edge_pixels,
        *spec, field_re, field_im, tables,
    )

    rims = exchange("ty", *rims)
    band, *rims = call(
        fold_kernel, "fold", [shape(tile, period)] + packed, [VMEM] * 3
    )(grad, *rims)
    rims = exchange("tx", *rims)
    (steering,) = call(
        finish_kernel, "finish", [shape(tile, tile)], [VMEM] * 4
    )(band, *rims, latent)
    return (steering, tail_mean.reshape(1))


def solution(mesh):
    placed = (P("ty", "tx"), P(), P(), P(), P("ty", "tx"), P("ty", "tx"), P())
    return jax.shard_map(
        body, mesh=mesh, in_specs=placed, out_specs=(P("ty", "tx"), P()), check_vma=False
    )
```

```python
import functools
import math

import jax
import jax.numpy as jnp
import numpy as np
from jax import lax
from jax.experimental import pallas as pl
from jax.experimental.pallas import tpu as pltpu
from jax.sharding import PartitionSpec as P

STEEPNESS = 4.0
RESIST_LEVEL = 0.7
SOFTNESS = 0.25
LANES = 128
UNROLL = 3
F32 = jnp.float32
BF16 = jnp.bfloat16


def split(x):
    high = x.astype(BF16)
    return high, (x - high.astype(F32)).astype(BF16)


def dot(a, b):
    return jnp.dot(a, b, preferred_element_type=F32)


def dot3(a, b):
    return dot(a[0], b[0]) + dot(a[0], b[1]) + dot(a[1], b[0])


def stacked(pair):
    return jnp.concatenate(pair, axis=0)


def dot3_stacked(a, b):
    high, both = a
    count = high.shape[0]
    tall = dot(both, b[0])
    return tall[:count] + tall[count:] + dot(high, b[1])


def wave_tables(period):
    half = period // 2
    place = np.arange(period)
    angle = (np.arange(half)[None, :] + 0.5) * place[:, None] * (2.0 * math.pi / period)
    cos, sin = np.cos(angle), np.sin(angle)
    out = np.zeros((4, 2 * LANES, 2 * LANES))
    out[0, :period, :half] = cos
    out[0, :period, LANES : LANES + half] = sin
    out[1] = out[0].T
    out[2, :half, :period] = cos.T
    out[2, half:period, :period] = sin.T
    out[3] = out[2].T
    return out.astype(np.float32)


def halves(x):
    return x[:, :LANES], x[:, LANES:]


def edge_flags(axis):
    index, count = lax.axis_index(axis), lax.axis_size(axis)
    return lax.rem(index, 2) == 0, index > 0, index < count - 1


def sides(axis, first, second):
    even, lower, higher = edge_flags(axis)
    from_lower = jnp.where(lower, jnp.where(even, second, first), 0.0)
    from_higher = jnp.where(higher, jnp.where(even, first, second), 0.0)
    return from_lower, from_higher


def ordered(axis, for_lower, for_higher):
    even = lax.rem(lax.axis_index(axis), 2) == 0
    return jnp.where(even, for_higher, for_lower), jnp.where(even, for_lower, for_higher)


def exchange(axis, first, second):
    count = lax.axis_size(axis)
    out = []
    for offset, value in ((0, first), (1, second)):
        pairs = [(i, i) for i in range(count)]
        for low in range(offset, count - 1, 2):
            pairs[low], pairs[low + 1] = (low, low + 1), (low + 1, low)
        out.append(lax.ppermute(value, axis, pairs))
    return out


def spectra_kernel(start, parts, kern, tables, *rest):
    out_re, out_im, token = rest[-3:]
    period = out_re.shape[1]
    half = period // 2
    taps = kern.shape[-1]
    cols = split(tables[0, :taps, :])
    rows = split(tables[2, :period, :taps])
    rows = (rows[0], stacked(rows))
    token[...] = jnp.zeros(token.shape, F32)

    def step(k, carry):
        real_cos, real_sin = halves(dot3(split(kern[0, start + k]), cols))
        imag_cos, imag_sin = halves(dot3(split(kern[1, start + k]), cols))
        wide_re = jnp.concatenate([real_cos - imag_sin, real_cos + imag_sin], axis=1)
        wide_im = jnp.concatenate([real_sin + imag_cos, imag_cos - real_sin], axis=1)
        tall_re = dot3_stacked(rows, split(wide_re))
        tall_im = dot3_stacked(rows, split(wide_im))
        out_re[start + k, :half] = tall_re[:half] - tall_im[half:]
        out_re[start + k, half:] = tall_re[:half] + tall_im[half:]
        out_im[start + k, :half] = tall_im[:half] + tall_re[half:]
        out_im[start + k, half:] = tall_im[:half] - tall_re[half:]
        return carry

    lax.fori_loop(0, parts, step, 0, unroll=UNROLL)


def pack(x):
    count = x.shape[0] // 2
    return jnp.concatenate([x[:count], x[count:]], axis=1)


def unpack(x):
    width = x.shape[1] // 2
    return jnp.concatenate([x[:, :width], x[:, width:]], axis=0)


def start_kernel(latent, transmit, first, second):
    tile = latent.shape[0]
    radius = first.shape[1] // 2
    value = 0.5 * (1.0 + jnp.tanh(latent[...]))
    transmit[...] = value
    first[...], second[...] = ordered(
        "tx", pack(value[:, :radius]), pack(value[:, tile - radius :])
    )


def band_kernel(middle, first, second, after, band, next_first, next_second, token):
    tile = middle.shape[0]
    radius = first.shape[1] // 2
    left, right = sides("tx", first[...], second[...])
    band[:, :radius] = unpack(left)
    band[:, radius : radius + tile] = middle[...]
    band[:, radius + tile :] = unpack(right)
    next_first[...], next_second[...] = ordered(
        "ty", band[:radius], band[tile - radius :]
    )
    token[...] = jnp.zeros(token.shape, F32)


def repeat_kernel(rows, out):
    for r in range(rows.shape[0]):
        out[:, r] = jnp.broadcast_to(rows[r], (out.shape[0], out.shape[2]))


def fold_kernel(grad, first, second, band, next_first, next_second):
    tile = band.shape[0]
    radius = first.shape[0]
    above, below = sides("ty", first[...], second[...])
    band[...] = grad[radius : radius + tile]
    band[:radius] += above
    band[tile - radius :] += below
    period = band.shape[1]
    next_first[...], next_second[...] = ordered(
        "tx", pack(band[:, :radius]), pack(band[:, period - radius :])
    )


def finish_kernel(band, first, second, latent, steering):
    tile = latent.shape[0]
    radius = first.shape[1] // 2
    left, right = sides("tx", first[...], second[...])
    steering[...] = band[:, radius : radius + tile]
    steering[:, :radius] += unpack(left)
    steering[:, tile - radius :] += unpack(right)
    value = jnp.tanh(latent[...])
    steering[...] = steering[...] * 0.5 * (1.0 - value * value)


def total_weight(weights, kernels):
    total = weights[0]
    for k in range(1, kernels):
        total = total + weights[k]
    return jnp.full((1, 1), total, F32)


def sample_places(pixels, tile):
    row = ((pixels.astype(F32) + 0.5) * (1.0 / tile)).astype(jnp.int32)
    return row, pixels - row * tile


def field_kernel(
    weights, spec_re, spec_im, band, first, second, pixels, slopes, tables,
    field_re, field_im, sampled, copies, framed, mask,
):
    kernels, period, _ = spec_re.shape
    half = period // 2
    tile = field_re.shape[1]
    radius = first.shape[0]
    above, below = sides("ty", first[...], second[...])
    framed[:radius] = above
    framed[radius + tile :] = below
    framed[radius : radius + tile] = band[...]
    wide = dot3(split(framed[...]), split(tables[0, :period]))
    tall = dot3(split(tables[2, :period, :period]), split(wide)) * (1.0 / (period * period))
    cos_cos, cos_sin = halves(tall[:half])
    sin_cos, sin_sin = halves(tall[half:])
    same, other = cos_cos - sin_sin, cos_cos + sin_sin
    joint, cross = sin_cos + cos_sin, sin_cos - cos_sin
    mask[0, :, :LANES], mask[0, :, LANES:] = same, other
    mask[1, :, :LANES], mask[1, :, LANES:] = -joint, -cross
    mask[2, :, :LANES], mask[2, :, LANES:] = other, same
    mask[3, :, :LANES], mask[3, :, LANES:] = cross, joint
    lift = split(tables[3, :tile, :period])
    lift = (lift[0], stacked(lift))
    across = split(tables[1, :, :LANES])

    def step(k, intensity):
        pos_re, pos_im = spec_re[k, :half], spec_im[k, :half]
        neg_re, neg_im = spec_re[k, half:], spec_im[k, half:]
        up_re = mask[0] * pos_re - mask[1] * pos_im
        up_im = mask[0] * pos_im + mask[1] * pos_re
        down_re = mask[2] * neg_re - mask[3] * neg_im
        down_im = mask[2] * neg_im + mask[3] * neg_re
        for_re = jnp.concatenate([up_re + down_re, down_im - up_im], axis=0)
        for_im = jnp.concatenate([up_im + down_im, up_re - down_re], axis=0)
        re_pos, re_neg = halves(dot3_stacked(lift, split(for_re)))
        im_pos, im_neg = halves(dot3_stacked(lift, split(for_im)))
        rows_re = jnp.concatenate([re_pos + re_neg, im_neg - im_pos], axis=1)
        rows_im = jnp.concatenate([im_pos + im_neg, re_pos - re_neg], axis=1)
        both = dot3(split(stacked((rows_re, rows_im))), across)
        real, imag = both[:tile], both[tile:]
        field_re[k] = real
        field_im[k] = imag
        return intensity + weights[k] * (real * real + imag * imag)

    intensity = lax.fori_loop(
        0, kernels, step, jnp.zeros((tile, LANES), F32), unroll=UNROLL
    )
    intensity = intensity / total_weight(weights, kernels)
    samples = pixels.shape[1]
    row, col = sample_places(pixels[...], tile)
    in_col = lax.broadcasted_iota(jnp.int32, (LANES, samples), 0) == col
    one_hot = jnp.where(in_col, 1.0, 0.0).astype(BF16)
    high, rest = split(intensity)
    low = intensity - high.astype(F32) - rest.astype(F32)
    picked = dot(high, one_hot) + dot(rest, one_hot) + dot(low.astype(BF16), one_hot)
    in_row = lax.broadcasted_iota(jnp.int32, (tile, samples), 0) == row
    own = jnp.sum(jnp.where(in_row, picked, 0.0), axis=0, keepdims=True)
    sampled[...] = jnp.concatenate([own, slopes[...]], axis=1)
    copies[...] = jnp.broadcast_to(sampled[...][None], copies.shape)


def sigmoid(x):
    return 1.0 / (1.0 + jnp.exp(-x))


def errors(intensity, slope, dose):
    resist = sigmoid(STEEPNESS * (dose * intensity - RESIST_LEVEL))
    offset = (resist - 0.5) * slope
    return resist, offset, offset * offset


def gradient_kernel(
    weights, doses, pick, gathered, sampled, pixels, spec_re, spec_im, field_re, field_im,
    tables, grad, first, second, tail, total_re, total_im,
):
    kernels, period, _ = spec_re.shape
    half = period // 2
    tile = field_re.shape[1]
    radius = (period - tile) // 2
    samples = pixels.shape[1]
    groups, members, _ = gathered.shape
    devices = groups * members
    corners = doses.shape[0]
    per_corner = devices * samples
    rows = gathered[...].reshape(devices, 2 * samples)
    everyone, every_slope = rows[:, :samples], rows[:, samples:]
    pick_corner = pick[0] // per_corner
    remain = pick[0] - pick_corner * per_corner
    place = lax.broadcasted_iota(jnp.int32, (devices, samples), 0) * samples
    place = place + lax.broadcasted_iota(jnp.int32, (devices, samples), 1)
    _, _, picked = errors(everyone, every_slope, doses[pick_corner])
    threshold = jnp.sum(jnp.where(place == remain, picked, 0.0), keepdims=True)

    def corner(c, sums):
        _, _, error = errors(everyone, every_slope, doses[c])
        soft = sigmoid((error - threshold) * (1.0 / SOFTNESS))
        return sums[0] + soft, sums[1] + error * soft

    zero = jnp.zeros((devices, samples), F32)
    soft_sum, error_sum = lax.fori_loop(
        0, corners, corner, (zero, zero), unroll=4 if devices <= 32 else 1
    )
    soft_total = jnp.sum(soft_sum, keepdims=True)
    tail_mean = jnp.sum(error_sum, keepdims=True) / soft_total
    tail[...] = tail_mean

    own, slope = sampled[:, :samples], sampled[:, samples:]
    which = lax.broadcasted_iota(jnp.int32, (corners, samples), 0)
    dose = jnp.zeros((corners, samples), F32)
    for c in range(corners):
        dose = jnp.where(which == c, doses[c], dose)
    resist, offset, error = errors(own, slope, dose)
    soft = sigmoid((error - threshold) * (1.0 / SOFTNESS))
    slope_soft = soft * (1.0 - soft) * (1.0 / SOFTNESS)
    chain = 2.0 * STEEPNESS * offset * slope * dose * resist * (1.0 - resist)
    coefficient = (soft + (error - tail_mean) * slope_soft) * (corners * per_corner / soft_total)
    summed = jnp.sum(coefficient * chain, axis=0, keepdims=True)
    summed = summed / total_weight(weights, kernels)

    row, col = sample_places(pixels[...], tile)
    in_row = lax.broadcasted_iota(jnp.int32, (tile, samples), 0) == row
    in_col = lax.broadcasted_iota(jnp.int32, (LANES, samples), 0) == col
    one_hot = jnp.where(in_col, 1.0, 0.0).astype(BF16)
    placed = jnp.where(in_row, summed, 0.0)
    high, rest = split(placed)
    low = (placed - high.astype(F32) - rest.astype(F32)).astype(BF16)
    grid = jnp.zeros((tile, LANES), F32)
    for part in (high, rest, low):
        grid = grid + lax.dot_general(
            part, one_hot, (((1,), (1,)), ((), ())), preferred_element_type=F32
        )

    cols = split(tables[0, :LANES])
    rows = split(tables[2, :period, :tile])
    rows = (rows[0], stacked(rows))
    total_re[...] = jnp.zeros((period, 2 * LANES), F32)
    total_im[...] = jnp.zeros((period, 2 * LANES), F32)

    def step(k, carry):
        weighted = grid * weights[k]
        source = stacked((weighted * field_re[k], weighted * field_im[k]))
        both = dot3(split(source), cols)
        real_cos, real_sin = halves(both[:tile])
        imag_cos, imag_sin = halves(both[tile:])
        wide_re = jnp.concatenate([real_cos + imag_sin, real_cos - imag_sin], axis=1)
        wide_im = jnp.concatenate([imag_cos - real_sin, imag_cos + real_sin], axis=1)
        tall_re = dot3_stacked(rows, split(wide_re))
        tall_im = dot3_stacked(rows, split(wide_im))
        for start, sign in ((0, 1.0), (half, -1.0)):
            part = slice(start, start + half)
            wave_re = tall_re[:half] + sign * tall_im[half:]
            wave_im = tall_im[:half] - sign * tall_re[half:]
            own_re, own_im = spec_re[k, part], spec_im[k, part]
            total_re[part] += own_re * wave_re + own_im * wave_im
            total_im[part] += own_re * wave_im - own_im * wave_re
        return carry

    lax.fori_loop(0, kernels, step, 0, unroll=UNROLL)
    pos_re, neg_re = total_re[:half], total_re[half:]
    pos_im, neg_im = total_im[:half], total_im[half:]
    back_rows = split(tables[3, :period, :period])
    for_re = jnp.concatenate([pos_re + neg_re, neg_im - pos_im], axis=0)
    for_im = jnp.concatenate([pos_im + neg_im, pos_re - neg_re], axis=0)
    re_pos, re_neg = halves(dot3(back_rows, split(for_re)))
    im_pos, im_neg = halves(dot3(back_rows, split(for_im)))
    last = jnp.concatenate([re_pos + re_neg, im_neg - im_pos], axis=1)
    framed = dot3(split(last), split(tables[1, :, :period])) * (2.0 / (period * period))
    grad[...] = framed
    first[...], second[...] = ordered("ty", framed[:radius], framed[radius + tile :])


VMEM = pl.BlockSpec(memory_space=pltpu.VMEM)
SMEM = pl.BlockSpec(memory_space=pltpu.SMEM)
ANY = pl.BlockSpec(memory_space=pl.ANY)


def shape(*dims):
    return jax.ShapeDtypeStruct(dims, F32)


def call(kernel, name, out_shape, in_specs, scratch=(), aliases=None, micros=1):
    return pl.pallas_call(
        kernel,
        out_shape=out_shape,
        in_specs=in_specs,
        out_specs=[VMEM] * len(out_shape),
        scratch_shapes=scratch,
        input_output_aliases=aliases or {},
        compiler_params=pltpu.CompilerParams(vmem_limit_bytes=10 * 1024 * 1024),
        cost_estimate=pl.CostEstimate(
            flops=micros * 10**9, bytes_accessed=2**20, transcendentals=0
        ),
        name=name,
    )


def gather_all(copies):
    group = lax.all_to_all(copies, "tx", 0, 0, tiled=True)
    repeated = [shape(lax.axis_size("ty"), group.shape[0], group.shape[2])]
    (groups,) = call(repeat_kernel, "repeat", repeated, [VMEM])(group)
    return lax.all_to_all(groups, "ty", 0, 0, tiled=True)


def body(latent, kernels, socs_weights, dose_scale, inv_slope, edge_pixels, threshold_pick):
    tile = latent.shape[0]
    count, taps = kernels.shape[1], kernels.shape[-1]
    samples = edge_pixels.shape[1]
    radius = (taps - 1) // 2
    period = tile + 2 * radius
    half = period // 2
    tables = jnp.asarray(wave_tables(period))
    token = shape(8, LANES)
    packed = [shape(tile // 2, 2 * radius)] * 2
    rim = [shape(radius, period)] * 2

    transmit, *rims = call(
        start_kernel, "start", [shape(tile, tile)] + packed, [VMEM]
    )(latent)
    rims = exchange("tx", *rims)

    parts = count // 2
    spec = []
    after = []
    for part in range(2):
        given = spec + after
        *spec, done = call(
            functools.partial(spectra_kernel, part * parts, parts),
            "spectra",
            [shape(count, period, 2 * LANES)] * 2 + [token],
            [VMEM] * 2 + [ANY] * len(given),
            aliases={2: 0, 3: 1} if spec else None,
            micros=3,
        )(kernels, tables, *given)
        if part == 0:
            band, *rims, done = call(
                band_kernel,
                "band",
                [shape(tile, period)] + rim + [token],
                [VMEM] * 3 + [ANY],
            )(transmit, *rims, done)
            after = [done]
            rims = exchange("ty", *rims)

    across = lax.axis_size("tx")
    field_re, field_im, sampled, copies = call(
        field_kernel,
        "field",
        [shape(count, tile, LANES)] * 2
        + [shape(1, 2 * samples), shape(across, 1, 2 * samples)],
        [SMEM] + [VMEM] * 8,
        scratch=[
            pltpu.VMEM((period, period), F32),
            pltpu.VMEM((4, half, 2 * LANES), F32),
        ],
        micros=7,
    )(socs_weights, *spec, band, *rims, edge_pixels, inv_slope, tables)

    gathered = gather_all(copies)
    grad, *rims, tail_mean = call(
        gradient_kernel,
        "gradient",
        [shape(period, period)] + rim + [shape(1, 1)],
        [SMEM] * 3 + [VMEM] * 8,
        scratch=[pltpu.VMEM((period, 2 * LANES), F32)] * 2,
        micros=9,
    )(
        socs_weights, dose_scale, threshold_pick, gathered, sampled, edge_pixels,
        *spec, field_re, field_im, tables,
    )

    rims = exchange("ty", *rims)
    band, *rims = call(
        fold_kernel, "fold", [shape(tile, period)] + packed, [VMEM] * 3
    )(grad, *rims)
    rims = exchange("tx", *rims)
    (steering,) = call(
        finish_kernel, "finish", [shape(tile, tile)], [VMEM] * 4
    )(band, *rims, latent)
    return (steering, tail_mean.reshape(1))


def solution(mesh):
    placed = (P("ty", "tx"), P(), P(), P(), P("ty", "tx"), P("ty", "tx"), P())
    return jax.shard_map(
        body, mesh=mesh, in_specs=placed, out_specs=(P("ty", "tx"), P()), check_vma=False
    )
```

```python
import functools
import math

import jax
import jax.numpy as jnp
import ml_dtypes
import numpy as np
from jax import lax
from jax.experimental import pallas as pl
from jax.experimental.pallas import tpu as pltpu
from jax.sharding import PartitionSpec as P

STEEPNESS = 4.0
RESIST_LEVEL = 0.7
SOFTNESS = 0.25
LANES = 128
UNROLL = 3
F32 = jnp.float32
BF16 = jnp.bfloat16


def split(x):
    high = x.astype(BF16)
    return high, (x - high.astype(F32)).astype(BF16)


def dot(a, b):
    return jnp.dot(a, b, preferred_element_type=F32)


def dot3(a, b):
    return dot(a[0], b[0]) + dot(a[0], b[1]) + dot(a[1], b[0])


def stacked(pair):
    return jnp.concatenate(pair, axis=0)


def dot3_stacked(a, b):
    high, both = a
    count = high.shape[0]
    tall = dot(both, b[0])
    return tall[:count] + tall[count:] + dot(high, b[1])


def wave_tables(period, tile):
    half = period // 2
    place = np.arange(period)
    angle = (np.arange(half)[None, :] + 0.5) * place[:, None] * (2.0 * math.pi / period)
    cos, sin = np.cos(angle), np.sin(angle)
    wide = np.zeros((2 * LANES, 2 * LANES))
    tall = np.zeros((2 * LANES, 2 * LANES))
    wide[:period, :half] = cos
    wide[:period, LANES : LANES + half] = sin
    tall[:half, :period] = cos.T
    tall[half:period, :period] = sin.T
    out = np.zeros((10, 2 * LANES, 2 * LANES), ml_dtypes.bfloat16)
    for first, table in ((0, wide), (2, tall), (4, wide.T), (6, tall.T)):
        out[first] = table.astype(ml_dtypes.bfloat16)
        out[first + 1] = (table - out[first].astype(np.float64)).astype(ml_dtypes.bfloat16)
    out[8, :, :tile] = out[2, :, :tile]
    out[8, :, tile : 2 * tile] = out[2, :, :tile]
    out[9, :, :tile] = out[3, :, :tile]
    return out


def pair(tables, first, rows, cols):
    return tables[first, :rows, :cols], tables[first + 1, :rows, :cols]


def whole(parts):
    return parts[0].astype(F32) + parts[1].astype(F32)


def halves(x):
    return x[:, :LANES], x[:, LANES:]


def edge_flags(axis):
    index, count = lax.axis_index(axis), lax.axis_size(axis)
    return lax.rem(index, 2) == 0, index > 0, index < count - 1


def sides(axis, first, second):
    even, lower, higher = edge_flags(axis)
    from_lower = jnp.where(lower, jnp.where(even, second, first), 0.0)
    from_higher = jnp.where(higher, jnp.where(even, first, second), 0.0)
    return from_lower, from_higher


def ordered(axis, for_lower, for_higher):
    even = lax.rem(lax.axis_index(axis), 2) == 0
    return jnp.where(even, for_higher, for_lower), jnp.where(even, for_lower, for_higher)


def exchange(axis, first, second):
    count = lax.axis_size(axis)
    out = []
    for offset, value in ((0, first), (1, second)):
        pairs = [(i, i) for i in range(count)]
        for low in range(offset, count - 1, 2):
            pairs[low], pairs[low + 1] = (low, low + 1), (low + 1, low)
        out.append(lax.ppermute(value, axis, pairs))
    return out


def spectra_kernel(start, parts, kern, tables, *rest):
    out_re, out_im, token, edge = rest[-4:]
    period = out_re.shape[1]
    half = period // 2
    last = kern.shape[-1] - 1
    cols = pair(tables, 0, last, 2 * LANES)
    cols = (stacked((cols[0], cols[0])), cols[1])
    end_row = whole((tables[0, last : last + 16, :], tables[1, last : last + 16, :]))[:1]
    high, low = pair(tables, 2, period, last)
    rows = stacked(
        (
            jnp.concatenate([high, high], axis=1),
            jnp.concatenate([low, jnp.zeros_like(low)], axis=1),
        )
    )
    end_col = whole(pair(tables, 2, period, 2 * LANES))[:, last : last + 1]
    edge[...] = jnp.broadcast_to(end_col, edge.shape)

    def along_lanes(plane):
        high, low = split(plane[:, :last])
        out = dot(jnp.concatenate([high, low], axis=1), cols[0]) + dot(high, cols[1])
        return halves(out + plane[:, last:] * end_row)

    def along_rows(wide):
        tall = dot(rows, stacked(split(wide[:last])))
        tail = wide[last:]
        outer = [edge[...] * tail[:, :LANES], edge[...] * tail[:, LANES:]]
        return tall[:period] + tall[period:] + jnp.concatenate(outer, axis=1)

    token[...] = jnp.zeros(token.shape, F32)

    def step(k, carry):
        real_cos, real_sin = along_lanes(kern[0, start + k])
        imag_cos, imag_sin = along_lanes(kern[1, start + k])
        wide_re = jnp.concatenate([real_cos - imag_sin, real_cos + imag_sin], axis=1)
        wide_im = jnp.concatenate([real_sin + imag_cos, imag_cos - real_sin], axis=1)
        tall_re = along_rows(wide_re)
        tall_im = along_rows(wide_im)
        out_re[start + k, :half] = tall_re[:half] - tall_im[half:]
        out_re[start + k, half:] = tall_re[:half] + tall_im[half:]
        out_im[start + k, :half] = tall_im[:half] + tall_re[half:]
        out_im[start + k, half:] = tall_im[:half] - tall_re[half:]
        return carry

    lax.fori_loop(0, parts, step, 0, unroll=UNROLL)


def pack(x):
    count = x.shape[0] // 2
    return jnp.concatenate([x[:count], x[count:]], axis=1)


def unpack(x):
    width = x.shape[1] // 2
    return jnp.concatenate([x[:, :width], x[:, width:]], axis=0)


def start_kernel(latent, transmit, first, second):
    tile = latent.shape[0]
    radius = first.shape[1] // 2
    value = 0.5 * (1.0 + jnp.tanh(latent[...]))
    transmit[...] = value
    first[...], second[...] = ordered(
        "tx", pack(value[:, :radius]), pack(value[:, tile - radius :])
    )


def band_kernel(middle, first, second, after, band, next_first, next_second, token):
    tile = middle.shape[0]
    radius = first.shape[1] // 2
    left, right = sides("tx", first[...], second[...])
    band[:, :radius] = unpack(left)
    band[:, radius : radius + tile] = middle[...]
    band[:, radius + tile :] = unpack(right)
    next_first[...], next_second[...] = ordered(
        "ty", band[:radius], band[tile - radius :]
    )
    token[...] = jnp.zeros(token.shape, F32)


def fold_kernel(grad, first, second, band, next_first, next_second):
    tile = band.shape[0]
    radius = first.shape[0]
    above, below = sides("ty", first[...], second[...])
    band[...] = grad[radius : radius + tile]
    band[:radius] += above
    band[tile - radius :] += below
    period = band.shape[1]
    next_first[...], next_second[...] = ordered(
        "tx", pack(band[:, :radius]), pack(band[:, period - radius :])
    )


def finish_kernel(band, first, second, latent, steering):
    tile = latent.shape[0]
    radius = first.shape[1] // 2
    left, right = sides("tx", first[...], second[...])
    steering[...] = band[:, radius : radius + tile]
    steering[:, :radius] += unpack(left)
    steering[:, tile - radius :] += unpack(right)
    value = jnp.tanh(latent[...])
    steering[...] = steering[...] * 0.5 * (1.0 - value * value)


def total_weight(weights, kernels):
    total = weights[0]
    for k in range(1, kernels):
        total = total + weights[k]
    return jnp.full((1, 1), total, F32)


def sample_places(pixels, tile):
    row = ((pixels.astype(F32) + 0.5) * (1.0 / tile)).astype(jnp.int32)
    return row, pixels - row * tile


def field_kernel(
    weights, spec_re, spec_im, band, first, second, pixels, slopes, tables,
    field_re, field_im, sampled, copies, framed, mask,
):
    kernels, period, _ = spec_re.shape
    half = period // 2
    tile = field_re.shape[1]
    radius = first.shape[0]
    above, below = sides("ty", first[...], second[...])
    framed[:radius] = above
    framed[radius + tile :] = below
    framed[radius : radius + tile] = band[...]
    wide = dot3(split(framed[...]), pair(tables, 0, period, 2 * LANES))
    tall = dot3(pair(tables, 2, period, period), split(wide)) * (1.0 / (period * period))
    cos_cos, cos_sin = halves(tall[:half])
    sin_cos, sin_sin = halves(tall[half:])
    same, other = cos_cos - sin_sin, cos_cos + sin_sin
    joint, cross = sin_cos + cos_sin, sin_cos - cos_sin
    mask[0, :, :LANES], mask[0, :, LANES:] = same, other
    mask[1, :, :LANES], mask[1, :, LANES:] = -joint, -cross
    mask[2, :, :LANES], mask[2, :, LANES:] = other, same
    mask[3, :, :LANES], mask[3, :, LANES:] = cross, joint
    lift = pair(tables, 6, tile, period)
    lift = (lift[0], stacked(lift))
    across = pair(tables, 4, 2 * LANES, LANES)
    across = (across[0], jnp.concatenate(across, axis=1))

    def step(k, intensity):
        pos_re, pos_im = spec_re[k, :half], spec_im[k, :half]
        neg_re, neg_im = spec_re[k, half:], spec_im[k, half:]
        up_re = mask[0] * pos_re - mask[1] * pos_im
        up_im = mask[0] * pos_im + mask[1] * pos_re
        down_re = mask[2] * neg_re - mask[3] * neg_im
        down_im = mask[2] * neg_im + mask[3] * neg_re
        for_re = jnp.concatenate([up_re + down_re, down_im - up_im], axis=0)
        for_im = jnp.concatenate([up_im + down_im, up_re - down_re], axis=0)
        re_pos, re_neg = halves(dot3_stacked(lift, split(for_re)))
        im_pos, im_neg = halves(dot3_stacked(lift, split(for_im)))
        rows_re = jnp.concatenate([re_pos + re_neg, im_neg - im_pos], axis=1)
        rows_im = jnp.concatenate([im_pos + im_neg, re_pos - re_neg], axis=1)
        high, low = split(stacked((rows_re, rows_im)))
        first, second = halves(dot(high, across[1]))
        both = first + second + dot(low, across[0])
        real, imag = both[:tile], both[tile:]
        field_re[k] = real
        field_im[k] = imag
        return intensity + weights[k] * (real * real + imag * imag)

    intensity = lax.fori_loop(
        0, kernels, step, jnp.zeros((tile, LANES), F32), unroll=UNROLL
    )
    intensity = intensity / total_weight(weights, kernels)
    samples = pixels.shape[1]
    row, col = sample_places(pixels[...], tile)
    in_col = lax.broadcasted_iota(jnp.int32, (LANES, samples), 0) == col
    one_hot = jnp.where(in_col, 1.0, 0.0).astype(BF16)
    high, rest = split(intensity)
    low = intensity - high.astype(F32) - rest.astype(F32)
    picked = dot(high, one_hot) + dot(rest, one_hot) + dot(low.astype(BF16), one_hot)
    in_row = lax.broadcasted_iota(jnp.int32, (tile, samples), 0) == row
    own = jnp.sum(jnp.where(in_row, picked, 0.0), axis=0, keepdims=True)
    sampled[...] = jnp.concatenate([own, slopes[...]], axis=1)
    copies[...] = jnp.broadcast_to(sampled[...][None], copies.shape)


def sigmoid(x):
    return 1.0 / (1.0 + jnp.exp(-x))


def errors(intensity, slope, dose):
    resist = 0.5 * jnp.tanh(0.5 * STEEPNESS * (dose * intensity - RESIST_LEVEL))
    offset = resist * slope
    return resist, offset, offset * offset


def gradient_kernel(
    weights, doses, pick, gathered, sampled, pixels, spec_re, spec_im, field_re, field_im,
    tables, grad, first, second, tail, total_re, total_im, held, sems,
):
    kernels, period, _ = spec_re.shape

    def fetch(k):
        return [
            pltpu.make_async_copy(source.at[k], held.at[i, k], sems.at[i, k])
            for i, source in enumerate((spec_re, spec_im))
        ]

    for k in range(kernels):
        for copy in fetch(k):
            copy.start()
    half = period // 2
    tile = field_re.shape[1]
    radius = (period - tile) // 2
    samples = pixels.shape[1]
    devices = gathered.shape[0]
    corners = doses.shape[0]
    per_corner = devices * samples
    everyone, every_slope = gathered[:, :samples], gathered[:, samples:]
    pick_corner = pick[0] // per_corner
    remain = pick[0] - pick_corner * per_corner
    place = lax.broadcasted_iota(jnp.int32, (devices, samples), 0) * samples
    place = place + lax.broadcasted_iota(jnp.int32, (devices, samples), 1)
    _, _, picked = errors(everyone, every_slope, doses[pick_corner])
    threshold = jnp.sum(jnp.where(place == remain, picked, 0.0), keepdims=True)

    def corner(c, sums):
        _, _, error = errors(everyone, every_slope, doses[c])
        soft = sigmoid((error - threshold) * (1.0 / SOFTNESS))
        return sums[0] + soft, sums[1] + error * soft

    zero = jnp.zeros((devices, samples), F32)
    soft_sum, error_sum = lax.fori_loop(
        0, corners, corner, (zero, zero), unroll=4 if devices <= 32 else 1
    )
    soft_total = jnp.sum(soft_sum, keepdims=True)
    tail_mean = jnp.sum(error_sum, keepdims=True) / soft_total
    tail[...] = tail_mean

    own, slope = sampled[:, :samples], sampled[:, samples:]
    which = lax.broadcasted_iota(jnp.int32, (corners, samples), 0)
    dose = jnp.zeros((corners, samples), F32)
    for c in range(corners):
        dose = jnp.where(which == c, doses[c], dose)
    resist, offset, error = errors(own, slope, dose)
    soft = sigmoid((error - threshold) * (1.0 / SOFTNESS))
    slope_soft = soft * (1.0 - soft) * (1.0 / SOFTNESS)
    chain = 2.0 * STEEPNESS * offset * slope * dose * (0.25 - resist * resist)
    coefficient = (soft + (error - tail_mean) * slope_soft) * (corners * per_corner / soft_total)
    summed = jnp.sum(coefficient * chain, axis=0, keepdims=True)
    summed = summed / total_weight(weights, kernels)

    row, col = sample_places(pixels[...], tile)
    in_row = lax.broadcasted_iota(jnp.int32, (tile, samples), 0) == row
    in_col = lax.broadcasted_iota(jnp.int32, (LANES, samples), 0) == col
    one_hot = jnp.where(in_col, 1.0, 0.0).astype(BF16)
    placed = jnp.where(in_row, summed, 0.0)
    high, rest = split(placed)
    low = (placed - high.astype(F32) - rest.astype(F32)).astype(BF16)
    grid = jnp.zeros((tile, LANES), F32)
    for part in (high, rest, low):
        grid = grid + lax.dot_general(
            part, one_hot, (((1,), (1,)), ((), ())), preferred_element_type=F32
        )

    cols = pair(tables, 0, LANES, 2 * LANES)
    cols = (stacked((cols[0], cols[0])), cols[1])
    rows = stacked(pair(tables, 8, period, 2 * tile))
    total_re[...] = jnp.zeros((period, 2 * LANES), F32)
    total_im[...] = jnp.zeros((period, 2 * LANES), F32)

    def step(k, carry):
        weighted = grid * weights[k]
        source = stacked((weighted * field_re[k], weighted * field_im[k]))
        high, low = split(source)
        both = dot(jnp.concatenate([high, low], axis=1), cols[0]) + dot(high, cols[1])
        real_cos, real_sin = halves(both[:tile])
        imag_cos, imag_sin = halves(both[tile:])
        wide_re = jnp.concatenate([real_cos + imag_sin, real_cos - imag_sin], axis=1)
        wide_im = jnp.concatenate([imag_cos - real_sin, imag_cos + real_sin], axis=1)
        tall_re = dot(rows, stacked(split(wide_re)))
        tall_im = dot(rows, stacked(split(wide_im)))
        tall_re = tall_re[:period] + tall_re[period:]
        tall_im = tall_im[:period] + tall_im[period:]
        for copy in fetch(k):
            copy.wait()
        for start, sign in ((0, 1.0), (half, -1.0)):
            part = slice(start, start + half)
            wave_re = tall_re[:half] + sign * tall_im[half:]
            wave_im = tall_im[:half] - sign * tall_re[half:]
            own_re, own_im = held[0, k, part], held[1, k, part]
            total_re[part] += own_re * wave_re + own_im * wave_im
            total_im[part] += own_re * wave_im - own_im * wave_re
        return carry

    lax.fori_loop(0, kernels, step, 0, unroll=UNROLL)
    pos_re, neg_re = total_re[:half], total_re[half:]
    pos_im, neg_im = total_im[:half], total_im[half:]
    back_rows = pair(tables, 6, period, period)
    back_rows = (back_rows[0], stacked(back_rows))
    for_re = jnp.concatenate([pos_re + neg_re, neg_im - pos_im], axis=0)
    for_im = jnp.concatenate([pos_im + neg_im, pos_re - neg_re], axis=0)
    re_pos, re_neg = halves(dot3_stacked(back_rows, split(for_re)))
    im_pos, im_neg = halves(dot3_stacked(back_rows, split(for_im)))
    last = jnp.concatenate([re_pos + re_neg, im_neg - im_pos], axis=1)
    framed = dot3(split(last), pair(tables, 4, 2 * LANES, period)) * (2.0 / (period * period))
    grad[...] = framed
    first[...], second[...] = ordered("ty", framed[:radius], framed[radius + tile :])


VMEM = pl.BlockSpec(memory_space=pltpu.VMEM)
SMEM = pl.BlockSpec(memory_space=pltpu.SMEM)
ANY = pl.BlockSpec(memory_space=pl.ANY)
HBM = pl.BlockSpec(memory_space=pltpu.HBM)


def shape(*dims):
    return jax.ShapeDtypeStruct(dims, F32)


def call(kernel, name, out_shape, in_specs, scratch=(), aliases=None, micros=1):
    return pl.pallas_call(
        kernel,
        out_shape=out_shape,
        in_specs=in_specs,
        out_specs=[VMEM] * len(out_shape),
        scratch_shapes=scratch,
        input_output_aliases=aliases or {},
        compiler_params=pltpu.CompilerParams(vmem_limit_bytes=16 * 1024 * 1024),
        cost_estimate=pl.CostEstimate(
            flops=micros * 10**9, bytes_accessed=2**20, transcendentals=0
        ),
        name=name,
    )


def gather_all(copies):
    return lax.all_to_all(copies, ("ty", "tx"), 0, 0, tiled=True)


def body(latent, kernels, socs_weights, dose_scale, inv_slope, edge_pixels, threshold_pick):
    tile = latent.shape[0]
    count, taps = kernels.shape[1], kernels.shape[-1]
    samples = edge_pixels.shape[1]
    radius = (taps - 1) // 2
    period = tile + 2 * radius
    half = period // 2
    tables = jnp.asarray(wave_tables(period, tile))
    token = shape(8, LANES)
    packed = [shape(tile // 2, 2 * radius)] * 2
    rim = [shape(radius, period)] * 2

    transmit, *rims = call(
        start_kernel, "start", [shape(tile, tile)] + packed, [VMEM]
    )(latent)
    rims = exchange("tx", *rims)

    parts = count // 2
    spec = []
    after = []
    for part in range(2):
        given = spec + after
        *spec, done = call(
            functools.partial(spectra_kernel, part * parts, parts),
            "spectra",
            [shape(count, period, 2 * LANES)] * 2 + [token],
            [VMEM] * 2 + [ANY] * len(given),
            scratch=[pltpu.VMEM((period, LANES), F32)],
            aliases={2: 0, 3: 1} if spec else None,
            micros=3,
        )(kernels, tables, *given)
        if part == 0:
            band, *rims, done = call(
                band_kernel,
                "band",
                [shape(tile, period)] + rim + [token],
                [VMEM] * 3 + [ANY],
            )(transmit, *rims, done)
            after = [done]
            rims = exchange("ty", *rims)

    devices = lax.axis_size("ty") * lax.axis_size("tx")
    field_re, field_im, sampled, copies = call(
        field_kernel,
        "field",
        [shape(count, tile, LANES)] * 2
        + [shape(1, 2 * samples), shape(devices, 1, 2 * samples)],
        [SMEM] + [VMEM] * 8,
        scratch=[
            pltpu.VMEM((period, period), F32),
            pltpu.VMEM((4, half, 2 * LANES), F32),
        ],
        micros=7,
    )(socs_weights, *spec, band, *rims, edge_pixels, inv_slope, tables)

    gathered = gather_all(copies).reshape(devices, 2 * samples)
    grad, *rims, tail_mean = call(
        gradient_kernel,
        "gradient",
        [shape(period, period)] + rim + [shape(1, 1)],
        [SMEM] * 3 + [VMEM] * 3 + [HBM] * 2 + [VMEM] * 3,
        scratch=[pltpu.VMEM((period, 2 * LANES), F32)] * 2
        + [
            pltpu.VMEM((2, count, period, 2 * LANES), F32),
            pltpu.SemaphoreType.DMA((2, count)),
        ],
        micros=9,
    )(
        socs_weights, dose_scale, threshold_pick, gathered, sampled, edge_pixels,
        *spec, field_re, field_im, tables,
    )

    rims = exchange("ty", *rims)
    band, *rims = call(
        fold_kernel, "fold", [shape(tile, period)] + packed, [VMEM] * 3
    )(grad, *rims)
    rims = exchange("tx", *rims)
    (steering,) = call(
        finish_kernel, "finish", [shape(tile, tile)], [VMEM] * 4
    )(band, *rims, latent)
    return (steering, tail_mean.reshape(1))


def solution(mesh):
    placed = (P("ty", "tx"), P(), P(), P(), P("ty", "tx"), P("ty", "tx"), P())
    return jax.shard_map(
        body, mesh=mesh, in_specs=placed, out_specs=(P("ty", "tx"), P()), check_vma=False
    )
```

```python
import functools
import math

import jax
import jax.numpy as jnp
import ml_dtypes
import numpy as np
from jax import lax
from jax.experimental import pallas as pl
from jax.experimental.pallas import tpu as pltpu
from jax.sharding import PartitionSpec as P

STEEPNESS = 4.0
RESIST_LEVEL = 0.7
SOFTNESS = 0.25
LANES = 128
UNROLL = 3
F32 = jnp.float32
BF16 = jnp.bfloat16


def split(x):
    high = x.astype(BF16)
    return high, (x - high.astype(F32)).astype(BF16)


def dot(a, b):
    return jnp.dot(a, b, preferred_element_type=F32)


def dot3(a, b):
    return dot(a[0], b[0]) + dot(a[0], b[1]) + dot(a[1], b[0])


def stacked(pair):
    return jnp.concatenate(pair, axis=0)


def dot3_stacked(a, b):
    high, both = a
    count = high.shape[0]
    tall = dot(both, b[0])
    return tall[:count] + tall[count:] + dot(high, b[1])


def wave_tables(period, tile):
    half = period // 2
    place = np.arange(period)
    angle = (np.arange(half)[None, :] + 0.5) * place[:, None] * (2.0 * math.pi / period)
    cos, sin = np.cos(angle), np.sin(angle)
    wide = np.zeros((2 * LANES, 2 * LANES))
    tall = np.zeros((2 * LANES, 2 * LANES))
    wide[:period, :half] = cos
    wide[:period, LANES : LANES + half] = sin
    tall[:half, :period] = cos.T
    tall[half:period, :period] = sin.T
    out = np.zeros((10, 2 * LANES, 2 * LANES), ml_dtypes.bfloat16)
    for first, table in ((0, wide), (2, tall), (4, wide.T), (6, tall.T)):
        out[first] = table.astype(ml_dtypes.bfloat16)
        out[first + 1] = (table - out[first].astype(np.float64)).astype(ml_dtypes.bfloat16)
    out[8, :, :tile] = out[2, :, :tile]
    out[8, :, tile : 2 * tile] = out[2, :, :tile]
    out[9, :, :tile] = out[3, :, :tile]
    return out


def pair(tables, first, rows, cols):
    return tables[first, :rows, :cols], tables[first + 1, :rows, :cols]


def whole(parts):
    return parts[0].astype(F32) + parts[1].astype(F32)


def halves(x):
    return x[:, :LANES], x[:, LANES:]


def place_in_pair(axis):
    index, count = lax.axis_index(axis), lax.axis_size(axis)
    lower = lax.rem(index, 2) == 0
    return lower, jnp.where(lower, index > 0, index < count - 1)


def swap(axis, x):
    return lax.ppermute(x, axis, [(i, i ^ 1) for i in range(lax.axis_size(axis))])


def ring(axis, x, back=False):
    count = lax.axis_size(axis)
    cycle = list(range(0, count, 2)) + list(range(count - 1, 0, -2))
    pairs = list(zip(cycle, cycle[1:] + cycle[:1]))
    return lax.ppermute(x, axis, [(b, a) if back else (a, b) for a, b in pairs])


def spectra_kernel(start, parts, kern, tables, *rest):
    out_re, out_im, token, edge = rest[-4:]
    period = out_re.shape[1]
    half = period // 2
    last = kern.shape[-1] - 1
    cols = pair(tables, 0, last, 2 * LANES)
    cols = (stacked((cols[0], cols[0])), cols[1])
    end_row = whole((tables[0, last : last + 16, :], tables[1, last : last + 16, :]))[:1]
    high, low = pair(tables, 2, period, last)
    rows = stacked(
        (
            jnp.concatenate([high, high], axis=1),
            jnp.concatenate([low, jnp.zeros_like(low)], axis=1),
        )
    )
    end_col = whole(pair(tables, 2, period, 2 * LANES))[:, last : last + 1]
    edge[...] = jnp.broadcast_to(end_col, edge.shape)

    def along_lanes(plane):
        high, low = split(plane[:, :last])
        out = dot(jnp.concatenate([high, low], axis=1), cols[0]) + dot(high, cols[1])
        return halves(out + plane[:, last:] * end_row)

    def along_rows(wide):
        tall = dot(rows, stacked(split(wide[:last])))
        tail = wide[last:]
        outer = [edge[...] * tail[:, :LANES], edge[...] * tail[:, LANES:]]
        return tall[:period] + tall[period:] + jnp.concatenate(outer, axis=1)

    token[...] = jnp.zeros(token.shape, F32)

    def step(k, carry):
        real_cos, real_sin = along_lanes(kern[0, start + k])
        imag_cos, imag_sin = along_lanes(kern[1, start + k])
        wide_re = jnp.concatenate([real_cos - imag_sin, real_cos + imag_sin], axis=1)
        wide_im = jnp.concatenate([real_sin + imag_cos, imag_cos - real_sin], axis=1)
        tall_re = along_rows(wide_re)
        tall_im = along_rows(wide_im)
        out_re[start + k, :half] = tall_re[:half] - tall_im[half:]
        out_re[start + k, half:] = tall_re[:half] + tall_im[half:]
        out_im[start + k, :half] = tall_im[:half] + tall_re[half:]
        out_im[start + k, half:] = tall_im[:half] - tall_re[half:]
        return carry

    lax.fori_loop(0, parts, step, 0, unroll=UNROLL)


def pack(x):
    count = x.shape[0] // 2
    return jnp.concatenate([x[:count], x[count:]], axis=1)


def unpack(x):
    width = x.shape[1] // 2
    return jnp.concatenate([x[:, :width], x[:, width:]], axis=0)


def start_kernel(latent, transmit):
    transmit[...] = 0.5 * (1.0 + jnp.tanh(latent[...]))


def relay_columns_kernel(partner, after, rim, token):
    radius = rim.shape[1] // 2
    tile = partner.shape[1]
    lower, _ = place_in_pair("tx")
    rim[...] = jnp.where(
        lower, pack(partner[:, tile - radius :]), pack(partner[:, :radius])
    )
    token[...] = jnp.zeros(token.shape, F32)


def band_kernel(middle, partner, rim, after, band, token):
    tile = middle.shape[0]
    radius = rim.shape[1] // 2
    lower, other = place_in_pair("tx")
    outer = jnp.where(other, unpack(rim[...]), 0.0)
    band[:, :radius] = jnp.where(lower, outer, partner[:, tile - radius :])
    band[:, radius : radius + tile] = middle[...]
    band[:, radius + tile :] = jnp.where(lower, partner[:, :radius], outer)
    token[...] = jnp.zeros(token.shape, F32)


def relay_rows_kernel(partner, after, rim, token):
    radius = rim.shape[0]
    tile = partner.shape[0]
    lower, _ = place_in_pair("ty")
    rim[...] = jnp.where(lower, partner[tile - radius :], partner[:radius])
    token[...] = jnp.zeros(token.shape, F32)


def fold_rows_kernel(grad, rim, out):
    radius = rim.shape[0]
    tile = out.shape[0]
    lower, _ = place_in_pair("ty")
    count, index = lax.axis_size("ty"), lax.axis_index("ty")
    comes = jnp.where(lower, index < count - 2, index > 1)
    outer = jnp.where(comes, rim[...], 0.0)
    top = jnp.where(lower, grad[radius + tile :], outer)
    bottom = jnp.where(lower, outer, grad[:radius])
    out[:radius] = top
    out[radius:] = jnp.zeros((tile - radius, out.shape[1]), F32)
    out[tile - radius :] += bottom


def fold_band_kernel(grad, partner, band, rim):
    tile = band.shape[0]
    radius = rim.shape[1] // 2
    lower, _ = place_in_pair("tx")
    band[...] = grad[radius : radius + tile] + partner[...]
    rim[...] = jnp.where(
        lower, pack(band[:, :radius]), pack(band[:, radius + tile :])
    )


def fold_columns_kernel(band, rim, out):
    radius = rim.shape[1] // 2
    tile = out.shape[1]
    lower, _ = place_in_pair("tx")
    count, index = lax.axis_size("tx"), lax.axis_index("tx")
    comes = jnp.where(lower, index < count - 2, index > 1)
    outer = jnp.where(comes, unpack(rim[...]), 0.0)
    left = jnp.where(lower, band[:, radius + tile :], outer)
    right = jnp.where(lower, outer, band[:, :radius])
    out[:, :radius] = left
    out[:, radius:] = jnp.zeros((out.shape[0], tile - radius), F32)
    out[:, tile - radius :] += right


def finish_kernel(band, partner, latent, steering):
    tile = latent.shape[0]
    radius = (band.shape[1] - tile) // 2
    value = jnp.tanh(latent[...])
    total = band[:, radius : radius + tile] + partner[...]
    steering[...] = total * 0.5 * (1.0 - value * value)


def total_weight(weights, kernels):
    total = weights[0]
    for k in range(1, kernels):
        total = total + weights[k]
    return jnp.full((1, 1), total, F32)


def sample_places(pixels, tile):
    row = ((pixels.astype(F32) + 0.5) * (1.0 / tile)).astype(jnp.int32)
    return row, pixels - row * tile


def field_kernel(
    weights, spec_re, spec_im, band, partner, rim, pixels, slopes, tables,
    field_re, field_im, sampled, copies, framed, mask,
):
    kernels, period, _ = spec_re.shape
    half = period // 2
    tile = field_re.shape[1]
    radius = rim.shape[0]
    lower, other = place_in_pair("ty")
    outer = jnp.where(other, rim[...], 0.0)
    framed[:radius] = jnp.where(lower, outer, partner[tile - radius :])
    framed[radius + tile :] = jnp.where(lower, partner[:radius], outer)
    framed[radius : radius + tile] = band[...]
    wide = dot3(split(framed[...]), pair(tables, 0, period, 2 * LANES))
    tall = dot3(pair(tables, 2, period, period), split(wide)) * (1.0 / (period * period))
    cos_cos, cos_sin = halves(tall[:half])
    sin_cos, sin_sin = halves(tall[half:])
    same, other = cos_cos - sin_sin, cos_cos + sin_sin
    joint, cross = sin_cos + cos_sin, sin_cos - cos_sin
    mask[0, :, :LANES], mask[0, :, LANES:] = same, other
    mask[1, :, :LANES], mask[1, :, LANES:] = -joint, -cross
    mask[2, :, :LANES], mask[2, :, LANES:] = other, same
    mask[3, :, :LANES], mask[3, :, LANES:] = cross, joint
    lift = pair(tables, 6, tile, period)
    lift = (lift[0], stacked(lift))
    across = pair(tables, 4, 2 * LANES, LANES)
    across = (across[0], jnp.concatenate(across, axis=1))

    def step(k, intensity):
        pos_re, pos_im = spec_re[k, :half], spec_im[k, :half]
        neg_re, neg_im = spec_re[k, half:], spec_im[k, half:]
        up_re = mask[0] * pos_re - mask[1] * pos_im
        up_im = mask[0] * pos_im + mask[1] * pos_re
        down_re = mask[2] * neg_re - mask[3] * neg_im
        down_im = mask[2] * neg_im + mask[3] * neg_re
        for_re = jnp.concatenate([up_re + down_re, down_im - up_im], axis=0)
        for_im = jnp.concatenate([up_im + down_im, up_re - down_re], axis=0)
        re_pos, re_neg = halves(dot3_stacked(lift, split(for_re)))
        im_pos, im_neg = halves(dot3_stacked(lift, split(for_im)))
        rows_re = jnp.concatenate([re_pos + re_neg, im_neg - im_pos], axis=1)
        rows_im = jnp.concatenate([im_pos + im_neg, re_pos - re_neg], axis=1)
        high, low = split(stacked((rows_re, rows_im)))
        first, second = halves(dot(high, across[1]))
        both = first + second + dot(low, across[0])
        real, imag = both[:tile], both[tile:]
        field_re[k] = real
        field_im[k] = imag
        return intensity + weights[k] * (real * real + imag * imag)

    intensity = lax.fori_loop(
        0, kernels, step, jnp.zeros((tile, LANES), F32), unroll=UNROLL
    )
    intensity = intensity / total_weight(weights, kernels)
    samples = pixels.shape[1]
    row, col = sample_places(pixels[...], tile)
    in_col = lax.broadcasted_iota(jnp.int32, (LANES, samples), 0) == col
    one_hot = jnp.where(in_col, 1.0, 0.0).astype(BF16)
    high, rest = split(intensity)
    low = intensity - high.astype(F32) - rest.astype(F32)
    picked = dot(high, one_hot) + dot(rest, one_hot) + dot(low.astype(BF16), one_hot)
    in_row = lax.broadcasted_iota(jnp.int32, (tile, samples), 0) == row
    own = jnp.sum(jnp.where(in_row, picked, 0.0), axis=0, keepdims=True)
    sampled[...] = jnp.concatenate([own, slopes[...]], axis=1)
    copies[...] = jnp.broadcast_to(sampled[...][None], copies.shape)


def sigmoid(x):
    return 1.0 / (1.0 + jnp.exp(-x))


def errors(intensity, slope, dose):
    resist = 0.5 * jnp.tanh(0.5 * STEEPNESS * (dose * intensity - RESIST_LEVEL))
    offset = resist * slope
    return resist, offset, offset * offset


def gradient_kernel(
    weights, doses, pick, gathered, sampled, pixels, spec_re, spec_im, field_re, field_im,
    tables, grad, rim, tail, total_re, total_im, held, sems,
):
    kernels, period, _ = spec_re.shape

    def fetch(k):
        return [
            pltpu.make_async_copy(source.at[k], held.at[i, k], sems.at[i, k])
            for i, source in enumerate((spec_re, spec_im))
        ]

    for k in range(kernels):
        for copy in fetch(k):
            copy.start()
    half = period // 2
    tile = field_re.shape[1]
    radius = (period - tile) // 2
    samples = pixels.shape[1]
    devices = gathered.shape[0]
    corners = doses.shape[0]
    per_corner = devices * samples
    everyone, every_slope = gathered[:, :samples], gathered[:, samples:]
    pick_corner = pick[0] // per_corner
    remain = pick[0] - pick_corner * per_corner
    place = lax.broadcasted_iota(jnp.int32, (devices, samples), 0) * samples
    place = place + lax.broadcasted_iota(jnp.int32, (devices, samples), 1)
    _, _, picked = errors(everyone, every_slope, doses[pick_corner])
    threshold = jnp.sum(jnp.where(place == remain, picked, 0.0), keepdims=True)

    def corner(c, sums):
        _, _, error = errors(everyone, every_slope, doses[c])
        soft = sigmoid((error - threshold) * (1.0 / SOFTNESS))
        return sums[0] + soft, sums[1] + error * soft

    zero = jnp.zeros((devices, samples), F32)
    soft_sum, error_sum = lax.fori_loop(
        0, corners, corner, (zero, zero), unroll=4 if devices <= 32 else 1
    )
    soft_total = jnp.sum(soft_sum, keepdims=True)
    tail_mean = jnp.sum(error_sum, keepdims=True) / soft_total
    tail[...] = tail_mean

    own, slope = sampled[:, :samples], sampled[:, samples:]
    which = lax.broadcasted_iota(jnp.int32, (corners, samples), 0)
    dose = jnp.zeros((corners, samples), F32)
    for c in range(corners):
        dose = jnp.where(which == c, doses[c], dose)
    resist, offset, error = errors(own, slope, dose)
    soft = sigmoid((error - threshold) * (1.0 / SOFTNESS))
    slope_soft = soft * (1.0 - soft) * (1.0 / SOFTNESS)
    chain = 2.0 * STEEPNESS * offset * slope * dose * (0.25 - resist * resist)
    coefficient = (soft + (error - tail_mean) * slope_soft) * (corners * per_corner / soft_total)
    summed = jnp.sum(coefficient * chain, axis=0, keepdims=True)
    summed = summed / total_weight(weights, kernels)

    row, col = sample_places(pixels[...], tile)
    in_row = lax.broadcasted_iota(jnp.int32, (tile, samples), 0) == row
    in_col = lax.broadcasted_iota(jnp.int32, (LANES, samples), 0) == col
    one_hot = jnp.where(in_col, 1.0, 0.0).astype(BF16)
    placed = jnp.where(in_row, summed, 0.0)
    high, rest = split(placed)
    low = (placed - high.astype(F32) - rest.astype(F32)).astype(BF16)
    grid = jnp.zeros((tile, LANES), F32)
    for part in (high, rest, low):
        grid = grid + lax.dot_general(
            part, one_hot, (((1,), (1,)), ((), ())), preferred_element_type=F32
        )

    cols = pair(tables, 0, LANES, 2 * LANES)
    cols = (stacked((cols[0], cols[0])), cols[1])
    rows = stacked(pair(tables, 8, period, 2 * tile))
    total_re[...] = jnp.zeros((period, 2 * LANES), F32)
    total_im[...] = jnp.zeros((period, 2 * LANES), F32)

    def step(k, carry):
        weighted = grid * weights[k]
        source = stacked((weighted * field_re[k], weighted * field_im[k]))
        high, low = split(source)
        both = dot(jnp.concatenate([high, low], axis=1), cols[0]) + dot(high, cols[1])
        real_cos, real_sin = halves(both[:tile])
        imag_cos, imag_sin = halves(both[tile:])
        wide_re = jnp.concatenate([real_cos + imag_sin, real_cos - imag_sin], axis=1)
        wide_im = jnp.concatenate([imag_cos - real_sin, imag_cos + real_sin], axis=1)
        tall_re = dot(rows, stacked(split(wide_re)))
        tall_im = dot(rows, stacked(split(wide_im)))
        tall_re = tall_re[:period] + tall_re[period:]
        tall_im = tall_im[:period] + tall_im[period:]
        for copy in fetch(k):
            copy.wait()
        for start, sign in ((0, 1.0), (half, -1.0)):
            part = slice(start, start + half)
            wave_re = tall_re[:half] + sign * tall_im[half:]
            wave_im = tall_im[:half] - sign * tall_re[half:]
            own_re, own_im = held[0, k, part], held[1, k, part]
            total_re[part] += own_re * wave_re + own_im * wave_im
            total_im[part] += own_re * wave_im - own_im * wave_re
        return carry

    lax.fori_loop(0, kernels, step, 0, unroll=UNROLL)
    pos_re, neg_re = total_re[:half], total_re[half:]
    pos_im, neg_im = total_im[:half], total_im[half:]
    back_rows = pair(tables, 6, period, period)
    back_rows = (back_rows[0], stacked(back_rows))
    for_re = jnp.concatenate([pos_re + neg_re, neg_im - pos_im], axis=0)
    for_im = jnp.concatenate([pos_im + neg_im, pos_re - neg_re], axis=0)
    re_pos, re_neg = halves(dot3_stacked(back_rows, split(for_re)))
    im_pos, im_neg = halves(dot3_stacked(back_rows, split(for_im)))
    last = jnp.concatenate([re_pos + re_neg, im_neg - im_pos], axis=1)
    framed = dot3(split(last), pair(tables, 4, 2 * LANES, period)) * (2.0 / (period * period))
    grad[...] = framed
    lower, _ = place_in_pair("ty")
    rim[...] = jnp.where(lower, framed[:radius], framed[radius + tile :])


VMEM = pl.BlockSpec(memory_space=pltpu.VMEM)
SMEM = pl.BlockSpec(memory_space=pltpu.SMEM)
ANY = pl.BlockSpec(memory_space=pl.ANY)
HBM = pl.BlockSpec(memory_space=pltpu.HBM)


def shape(*dims):
    return jax.ShapeDtypeStruct(dims, F32)


def call(kernel, name, out_shape, in_specs, scratch=(), aliases=None, micros=1, vmem=10):
    return pl.pallas_call(
        kernel,
        out_shape=out_shape,
        in_specs=in_specs,
        out_specs=[VMEM] * len(out_shape),
        scratch_shapes=scratch,
        input_output_aliases=aliases or {},
        compiler_params=pltpu.CompilerParams(vmem_limit_bytes=vmem * 1024 * 1024),
        cost_estimate=pl.CostEstimate(
            flops=micros * 10**9, bytes_accessed=2**20, transcendentals=0
        ),
        name=name,
    )


def gather_all(copies):
    return lax.all_to_all(copies, ("ty", "tx"), 0, 0, tiled=True)


def body(latent, kernels, socs_weights, dose_scale, inv_slope, edge_pixels, threshold_pick):
    tile = latent.shape[0]
    count, taps = kernels.shape[1], kernels.shape[-1]
    samples = edge_pixels.shape[1]
    radius = (taps - 1) // 2
    period = tile + 2 * radius
    half = period // 2
    tables = jnp.asarray(wave_tables(period, tile))
    token = shape(8, LANES)
    packed = shape(tile // 2, 2 * radius)
    devices = lax.axis_size("ty") * lax.axis_size("tx")

    steps = 4
    parts = count // steps
    spec = []

    def spectra(step, *after):
        given = spec + list(after)
        *out, done = call(
            functools.partial(spectra_kernel, step * parts, parts),
            "spectra",
            [shape(count, period, 2 * LANES)] * 2 + [token],
            [VMEM] * 2 + [ANY] * len(given),
            scratch=[pltpu.VMEM((period, LANES), F32)],
            aliases={2: 0, 3: 1} if spec else None,
            micros=2,
        )(kernels, tables, *given)
        spec[:] = out
        return done

    (transmit,) = call(start_kernel, "start", [shape(tile, tile)], [VMEM])(latent)
    partner = swap("tx", transmit)
    done = spectra(0)
    rim, done = call(relay_columns_kernel, "relay", [packed, token], [VMEM, ANY])(
        partner, done
    )
    rim = ring("tx", rim)
    done = spectra(1, done)
    band, done = call(
        band_kernel, "band", [shape(tile, period), token], [VMEM] * 3 + [ANY]
    )(transmit, partner, rim, done)
    partner = swap("ty", band)
    done = spectra(2, done)
    rim, done = call(
        relay_rows_kernel, "relay", [shape(radius, period), token], [VMEM, ANY]
    )(partner, done)
    rim = ring("ty", rim)
    spectra(3, done)

    field_re, field_im, sampled, copies = call(
        field_kernel,
        "field",
        [shape(count, tile, LANES)] * 2
        + [shape(1, 2 * samples), shape(devices, 1, 2 * samples)],
        [SMEM] + [VMEM] * 8,
        scratch=[
            pltpu.VMEM((period, period), F32),
            pltpu.VMEM((4, half, 2 * LANES), F32),
        ],
        micros=7,
    )(socs_weights, *spec, band, partner, rim, edge_pixels, inv_slope, tables)

    gathered = gather_all(copies).reshape(devices, 2 * samples)
    grad, rim, tail_mean = call(
        gradient_kernel,
        "gradient",
        [shape(period, period), shape(radius, period), shape(1, 1)],
        [SMEM] * 3 + [VMEM] * 3 + [HBM] * 2 + [VMEM] * 3,
        scratch=[pltpu.VMEM((period, 2 * LANES), F32)] * 2
        + [
            pltpu.VMEM((2, count, period, 2 * LANES), F32),
            pltpu.SemaphoreType.DMA((2, count)),
        ],
        micros=9,
        vmem=60,
    )(
        socs_weights, dose_scale, threshold_pick, gathered, sampled, edge_pixels,
        *spec, field_re, field_im, tables,
    )

    rim = ring("ty", rim, back=True)
    (partner,) = call(fold_rows_kernel, "fold", [shape(tile, period)], [VMEM] * 2)(
        grad, rim
    )
    partner = swap("ty", partner)
    band, rim = call(
        fold_band_kernel, "fold", [shape(tile, period), packed], [VMEM] * 2
    )(grad, partner)
    rim = ring("tx", rim, back=True)
    (partner,) = call(fold_columns_kernel, "fold", [shape(tile, tile)], [VMEM] * 2)(
        band, rim
    )
    partner = swap("tx", partner)
    (steering,) = call(finish_kernel, "finish", [shape(tile, tile)], [VMEM] * 3)(
        band, partner, latent
    )
    return (steering, tail_mean.reshape(1))


def solution(mesh):
    placed = (P("ty", "tx"), P(), P(), P(), P("ty", "tx"), P("ty", "tx"), P())
    return jax.shard_map(
        body, mesh=mesh, in_specs=placed, out_specs=(P("ty", "tx"), P()), check_vma=False
    )
```

```python
import functools
import math

import jax
import jax.numpy as jnp
import ml_dtypes
import numpy as np
from jax import lax
from jax.experimental import pallas as pl
from jax.experimental.pallas import tpu as pltpu
from jax.sharding import PartitionSpec as P

STEEPNESS = 4.0
RESIST_LEVEL = 0.7
SOFTNESS = 0.25
LANES = 128
BATCH = 3
F32 = jnp.float32
BF16 = jnp.bfloat16


def split(x):
    high = x.astype(BF16)
    return high, (x - high.astype(F32)).astype(BF16)


def dot(a, b):
    return jnp.dot(a, b, preferred_element_type=F32)


def dot3(a, b):
    return dot(a[0], b[0]) + dot(a[0], b[1]) + dot(a[1], b[0])


def stacked(pair):
    return jnp.concatenate(pair, axis=0)


def dot3_stacked(a, b):
    high, both = a
    count = high.shape[0]
    tall = dot(both, b[0])
    return tall[:count] + tall[count:] + dot(high, b[1])


def wave_tables(period, tile):
    half = period // 2
    place = np.arange(period)
    angle = (np.arange(half)[None, :] + 0.5) * place[:, None] * (2.0 * math.pi / period)
    cos, sin = np.cos(angle), np.sin(angle)
    wide = np.zeros((2 * LANES, 2 * LANES))
    tall = np.zeros((2 * LANES, 2 * LANES))
    wide[:period, :half] = cos
    wide[:period, LANES : LANES + half] = sin
    tall[:half, :period] = cos.T
    tall[half:period, :period] = sin.T
    out = np.zeros((10, 2 * LANES, 2 * LANES), ml_dtypes.bfloat16)
    for first, table in ((0, wide), (2, tall), (4, wide.T), (6, tall.T)):
        out[first] = table.astype(ml_dtypes.bfloat16)
        out[first + 1] = (table - out[first].astype(np.float64)).astype(ml_dtypes.bfloat16)
    out[8, :, :tile] = out[2, :, :tile]
    out[8, :, tile : 2 * tile] = out[2, :, :tile]
    out[9, :, :tile] = out[3, :, :tile]
    return out


def pair(tables, first, rows, cols):
    return tables[first, :rows, :cols], tables[first + 1, :rows, :cols]


def whole(parts):
    return parts[0].astype(F32) + parts[1].astype(F32)


def halves(x):
    return x[:, :LANES], x[:, LANES:]


def place_in_pair(axis):
    index, count = lax.axis_index(axis), lax.axis_size(axis)
    lower = lax.rem(index, 2) == 0
    return lower, jnp.where(lower, index > 0, index < count - 1)


def swap(axis, x):
    return lax.ppermute(x, axis, [(i, i ^ 1) for i in range(lax.axis_size(axis))])


def swap_outside(axis, x):
    count = lax.axis_size(axis)
    pairs = [(0, 0), (count - 1, count - 1)]
    for low in range(1, count - 1, 2):
        pairs += [(low, low + 1), (low + 1, low)]
    return lax.ppermute(x, axis, pairs)


def ring(axis, x, back=False):
    count = lax.axis_size(axis)
    cycle = list(range(0, count, 2)) + list(range(count - 1, 0, -2))
    pairs = list(zip(cycle, cycle[1:] + cycle[:1]))
    return lax.ppermute(x, axis, [(b, a) if back else (a, b) for a, b in pairs])


def spectra_kernel(start, parts, kern, tables, *rest):
    out_re, out_im, token, edge = rest[-4:]
    period = out_re.shape[1]
    half = period // 2
    last = kern.shape[-1] - 1
    cols = pair(tables, 0, last, 2 * LANES)
    cols = (stacked((cols[0], cols[0])), cols[1])
    end_row = whole((tables[0, last : last + 16, :], tables[1, last : last + 16, :]))[:1]
    high, low = pair(tables, 2, period, last)
    rows = stacked(
        (
            jnp.concatenate([high, high], axis=1),
            jnp.concatenate([low, jnp.zeros_like(low)], axis=1),
        )
    )
    end_col = whole(pair(tables, 2, period, 2 * LANES))[:, last : last + 1]
    edge[...] = jnp.broadcast_to(end_col, edge.shape)

    def along_lanes(planes):
        main = stacked([plane[:last] for plane in planes])
        tail = stacked([plane[last:] for plane in planes])
        tail = jnp.concatenate([tail, jnp.zeros((-tail.shape[0] % 16, last + 1), F32)], axis=0)
        both = stacked((main, tail))
        high, low = split(both[:, :last])
        out = dot(jnp.concatenate([high, low], axis=1), cols[0]) + dot(high, cols[1])
        out = out + both[:, last:] * end_row
        first = len(planes) * last
        return [
            (out[i * last : (i + 1) * last], out[first + i : first + i + 1])
            for i in range(len(planes))
        ]

    def along_rows(wide, tail):
        tall = dot(rows, stacked(split(wide)))
        outer = [edge[...] * tail[:, :LANES], edge[...] * tail[:, LANES:]]
        return tall[:period] + tall[period:] + jnp.concatenate(outer, axis=1)

    def mixed(real, imag):
        real_cos, real_sin = halves(real)
        imag_cos, imag_sin = halves(imag)
        return (
            jnp.concatenate([real_cos - imag_sin, real_cos + imag_sin], axis=1),
            jnp.concatenate([real_sin + imag_cos, imag_cos - real_sin], axis=1),
        )

    def step(group, carry):
        first = start + group * BATCH
        planes = along_lanes([kern[c, first + i] for i in range(BATCH) for c in range(2)])
        for i in range(BATCH):
            k = first + i
            (real, real_tail), (imag, imag_tail) = planes[2 * i : 2 * i + 2]
            wide_re, wide_im = mixed(real, imag)
            tail_re, tail_im = mixed(real_tail, imag_tail)
            tall_re = along_rows(wide_re, tail_re)
            tall_im = along_rows(wide_im, tail_im)
            out_re[k, :half] = tall_re[:half] - tall_im[half:]
            out_re[k, half:] = tall_re[:half] + tall_im[half:]
            out_im[k, :half] = tall_im[:half] + tall_re[half:]
            out_im[k, half:] = tall_im[:half] - tall_re[half:]
        return carry

    lax.fori_loop(0, parts // BATCH, step, 0)


def pack(x):
    count = x.shape[0] // 2
    return jnp.concatenate([x[:count], x[count:]], axis=1)


def unpack(x):
    width = x.shape[1] // 2
    return jnp.concatenate([x[:, :width], x[:, width:]], axis=0)


def band_kernel(middle, partner, outside, after, band, token):
    tile = middle.shape[0]
    radius = (band.shape[1] - tile) // 2
    lower, other = place_in_pair("tx")

    def transmit(x):
        return 0.5 * (1.0 + jnp.tanh(x))

    near = transmit(jnp.where(lower, partner[:, :radius], partner[:, tile - radius :]))
    far = transmit(jnp.where(lower, outside[:, tile - radius :], outside[:, :radius]))
    far = jnp.where(other, far, 0.0)
    band[:, :radius] = jnp.where(lower, far, near)
    band[:, radius : radius + tile] = transmit(middle[...])
    band[:, radius + tile :] = jnp.where(lower, near, far)
    token[...] = jnp.zeros(token.shape, F32)


def relay_rows_kernel(partner, after, rim, token):
    radius = rim.shape[0]
    tile = partner.shape[0]
    lower, _ = place_in_pair("ty")
    rim[...] = jnp.where(lower, partner[tile - radius :], partner[:radius])
    token[...] = jnp.zeros(token.shape, F32)


def fold_rows_kernel(grad, rim, out):
    radius = rim.shape[0]
    tile = out.shape[0]
    lower, _ = place_in_pair("ty")
    count, index = lax.axis_size("ty"), lax.axis_index("ty")
    comes = jnp.where(lower, index < count - 2, index > 1)
    outer = jnp.where(comes, rim[...], 0.0)
    top = jnp.where(lower, grad[radius + tile :], outer)
    bottom = jnp.where(lower, outer, grad[:radius])
    out[:radius] = top
    out[radius:] = jnp.zeros((tile - radius, out.shape[1]), F32)
    out[tile - radius :] += bottom


def fold_band_kernel(grad, partner, band, near, far):
    tile = band.shape[0]
    radius = near.shape[1] // 2
    lower, _ = place_in_pair("tx")
    band[...] = grad[radius : radius + tile] + partner[...]
    left, right = pack(band[:, :radius]), pack(band[:, radius + tile :])
    near[...] = jnp.where(lower, right, left)
    far[...] = jnp.where(lower, left, right)


def finish_kernel(band, near, far, latent, steering):
    tile = latent.shape[0]
    radius = (band.shape[1] - tile) // 2
    lower, other = place_in_pair("tx")
    inner = unpack(near[...])
    outer = jnp.where(other, unpack(far[...]), 0.0)
    steering[...] = band[:, radius : radius + tile]
    steering[:, :radius] += jnp.where(lower, outer, inner)
    steering[:, tile - radius :] += jnp.where(lower, inner, outer)
    value = jnp.tanh(latent[...])
    steering[...] = steering[...] * 0.5 * (1.0 - value * value)


def total_weight(weights, kernels):
    total = weights[0]
    for k in range(1, kernels):
        total = total + weights[k]
    return jnp.full((1, 1), total, F32)


def sample_places(pixels, tile):
    row = ((pixels.astype(F32) + 0.5) * (1.0 / tile)).astype(jnp.int32)
    return row, pixels - row * tile


def field_kernel(
    weights, spec_re, spec_im, band, partner, rim, pixels, slopes, tables,
    field_re, field_im, sampled, copies, framed, mask,
):
    kernels, period, _ = spec_re.shape
    half = period // 2
    tile = field_re.shape[1]
    radius = rim.shape[0]
    lower, other = place_in_pair("ty")
    outer = jnp.where(other, rim[...], 0.0)
    framed[:radius] = jnp.where(lower, outer, partner[tile - radius :])
    framed[radius + tile :] = jnp.where(lower, partner[:radius], outer)
    framed[radius : radius + tile] = band[...]
    wide = dot3(split(framed[...]), pair(tables, 0, period, 2 * LANES))
    tall = dot3(pair(tables, 2, period, period), split(wide)) * (1.0 / (period * period))
    cos_cos, cos_sin = halves(tall[:half])
    sin_cos, sin_sin = halves(tall[half:])
    same, other = cos_cos - sin_sin, cos_cos + sin_sin
    joint, cross = sin_cos + cos_sin, sin_cos - cos_sin
    mask[0, :, :LANES], mask[0, :, LANES:] = same, other
    mask[1, :, :LANES], mask[1, :, LANES:] = -joint, -cross
    mask[2, :, :LANES], mask[2, :, LANES:] = other, same
    mask[3, :, :LANES], mask[3, :, LANES:] = cross, joint
    lift = pair(tables, 6, tile, period)
    lift = (lift[0], stacked(lift))
    across = pair(tables, 4, 2 * LANES, LANES)
    across = (across[0], jnp.concatenate(across, axis=1))

    def lifted(k):
        pos_re, pos_im = spec_re[k, :half], spec_im[k, :half]
        neg_re, neg_im = spec_re[k, half:], spec_im[k, half:]
        up_re = mask[0] * pos_re - mask[1] * pos_im
        up_im = mask[0] * pos_im + mask[1] * pos_re
        down_re = mask[2] * neg_re - mask[3] * neg_im
        down_im = mask[2] * neg_im + mask[3] * neg_re
        for_re = jnp.concatenate([up_re + down_re, down_im - up_im], axis=0)
        for_im = jnp.concatenate([up_im + down_im, up_re - down_re], axis=0)
        re_pos, re_neg = halves(dot3_stacked(lift, split(for_re)))
        im_pos, im_neg = halves(dot3_stacked(lift, split(for_im)))
        rows_re = jnp.concatenate([re_pos + re_neg, im_neg - im_pos], axis=1)
        rows_im = jnp.concatenate([im_pos + im_neg, re_pos - re_neg], axis=1)
        return [rows_re, rows_im]

    def step(group, intensity):
        first = group * BATCH
        rows = stacked([row for i in range(BATCH) for row in lifted(first + i)])
        high, low = split(rows)
        by_high, by_low = halves(dot(high, across[1]))
        both = by_high + by_low + dot(low, across[0])
        for i in range(BATCH):
            real = both[2 * i * tile : (2 * i + 1) * tile]
            imag = both[(2 * i + 1) * tile : (2 * i + 2) * tile]
            field_re[first + i] = real
            field_im[first + i] = imag
            intensity = intensity + weights[first + i] * (real * real + imag * imag)
        return intensity

    intensity = lax.fori_loop(
        0, kernels // BATCH, step, jnp.zeros((tile, LANES), F32)
    )
    intensity = intensity / total_weight(weights, kernels)
    samples = pixels.shape[1]
    row, col = sample_places(pixels[...], tile)
    in_col = lax.broadcasted_iota(jnp.int32, (LANES, samples), 0) == col
    one_hot = jnp.where(in_col, 1.0, 0.0).astype(BF16)
    high, rest = split(intensity)
    low = intensity - high.astype(F32) - rest.astype(F32)
    picked = dot(high, one_hot) + dot(rest, one_hot) + dot(low.astype(BF16), one_hot)
    in_row = lax.broadcasted_iota(jnp.int32, (tile, samples), 0) == row
    own = jnp.sum(jnp.where(in_row, picked, 0.0), axis=0, keepdims=True)
    sampled[...] = jnp.concatenate([own, slopes[...]], axis=1)
    copies[...] = jnp.broadcast_to(sampled[...][None], copies.shape)


def sigmoid(x):
    return 1.0 / (1.0 + jnp.exp(-x))


def errors(intensity, slope, dose):
    resist = 0.5 * jnp.tanh(0.5 * STEEPNESS * (dose * intensity - RESIST_LEVEL))
    offset = resist * slope
    return resist, offset, offset * offset


def source_kernel(weights, doses, pick, gathered, sampled, pixels, placed_sum, tail):
    kernels = weights.shape[0]
    tile = placed_sum.shape[0]
    samples = pixels.shape[1]
    devices = gathered.shape[0]
    corners = doses.shape[0]
    per_corner = devices * samples
    everyone, every_slope = gathered[:, :samples], gathered[:, samples:]
    pick_corner = pick[0] // per_corner
    remain = pick[0] - pick_corner * per_corner
    place = lax.broadcasted_iota(jnp.int32, (devices, samples), 0) * samples
    place = place + lax.broadcasted_iota(jnp.int32, (devices, samples), 1)
    _, _, picked = errors(everyone, every_slope, doses[pick_corner])
    threshold = jnp.sum(jnp.where(place == remain, picked, 0.0), keepdims=True)

    def corner(c, sums):
        _, _, error = errors(everyone, every_slope, doses[c])
        soft = sigmoid((error - threshold) * (1.0 / SOFTNESS))
        return sums[0] + soft, sums[1] + error * soft

    zero = jnp.zeros((devices, samples), F32)
    soft_sum, error_sum = lax.fori_loop(
        0, corners, corner, (zero, zero), unroll=4 if devices <= 32 else 1
    )
    soft_total = jnp.sum(soft_sum, keepdims=True)
    tail_mean = jnp.sum(error_sum, keepdims=True) / soft_total
    tail[...] = tail_mean

    own, slope = sampled[:, :samples], sampled[:, samples:]
    which = lax.broadcasted_iota(jnp.int32, (corners, samples), 0)
    dose = jnp.zeros((corners, samples), F32)
    for c in range(corners):
        dose = jnp.where(which == c, doses[c], dose)
    resist, offset, error = errors(own, slope, dose)
    soft = sigmoid((error - threshold) * (1.0 / SOFTNESS))
    slope_soft = soft * (1.0 - soft) * (1.0 / SOFTNESS)
    chain = 2.0 * STEEPNESS * offset * slope * dose * (0.25 - resist * resist)
    coefficient = (soft + (error - tail_mean) * slope_soft) * (corners * per_corner / soft_total)
    summed = jnp.sum(coefficient * chain, axis=0, keepdims=True)
    summed = summed / total_weight(weights, kernels)

    row, col = sample_places(pixels[...], tile)
    in_row = lax.broadcasted_iota(jnp.int32, (tile, samples), 0) == row
    in_col = lax.broadcasted_iota(jnp.int32, (LANES, samples), 0) == col
    one_hot = jnp.where(in_col, 1.0, 0.0).astype(BF16)
    placed = jnp.where(in_row, summed, 0.0)
    high, rest = split(placed)
    low = (placed - high.astype(F32) - rest.astype(F32)).astype(BF16)
    grid = jnp.zeros((tile, LANES), F32)
    for part in (high, rest, low):
        grid = grid + lax.dot_general(
            part, one_hot, (((1,), (1,)), ((), ())), preferred_element_type=F32
        )

    placed_sum[...] = grid


def gradient_kernel(
    weights, grid, spec_re, spec_im, field_re, field_im, tables,
    grad, rim, total_re, total_im,
):
    kernels, period, _ = spec_re.shape
    half = period // 2
    tile = field_re.shape[1]
    radius = (period - tile) // 2
    cols = pair(tables, 0, LANES, 2 * LANES)
    cols = (stacked((cols[0], cols[0])), cols[1])
    rows = stacked(pair(tables, 8, period, 2 * tile))
    total_re[...] = jnp.zeros((period, 2 * LANES), F32)
    total_im[...] = jnp.zeros((period, 2 * LANES), F32)

    def step(group, carry):
        sources = []
        for i in range(BATCH):
            k = group * BATCH + i
            weighted = grid[...] * weights[k]
            sources += [weighted * field_re[k], weighted * field_im[k]]
        high, low = split(stacked(sources))
        both = dot(jnp.concatenate([high, low], axis=1), cols[0]) + dot(high, cols[1])
        for i in range(BATCH):
            k = group * BATCH + i
            real_cos, real_sin = halves(both[2 * i * tile : (2 * i + 1) * tile])
            imag_cos, imag_sin = halves(both[(2 * i + 1) * tile : (2 * i + 2) * tile])
            wide_re = jnp.concatenate([real_cos + imag_sin, real_cos - imag_sin], axis=1)
            wide_im = jnp.concatenate([imag_cos - real_sin, imag_cos + real_sin], axis=1)
            tall_re = dot(rows, stacked(split(wide_re)))
            tall_im = dot(rows, stacked(split(wide_im)))
            tall_re = tall_re[:period] + tall_re[period:]
            tall_im = tall_im[:period] + tall_im[period:]
            for start, sign in ((0, 1.0), (half, -1.0)):
                part = slice(start, start + half)
                wave_re = tall_re[:half] + sign * tall_im[half:]
                wave_im = tall_im[:half] - sign * tall_re[half:]
                own_re, own_im = spec_re[k, part], spec_im[k, part]
                total_re[part] += own_re * wave_re + own_im * wave_im
                total_im[part] += own_re * wave_im - own_im * wave_re
        return carry

    lax.fori_loop(0, kernels // BATCH, step, 0)
    pos_re, neg_re = total_re[:half], total_re[half:]
    pos_im, neg_im = total_im[:half], total_im[half:]
    back_rows = pair(tables, 6, period, period)
    back_rows = (back_rows[0], stacked(back_rows))
    for_re = jnp.concatenate([pos_re + neg_re, neg_im - pos_im], axis=0)
    for_im = jnp.concatenate([pos_im + neg_im, pos_re - neg_re], axis=0)
    re_pos, re_neg = halves(dot3_stacked(back_rows, split(for_re)))
    im_pos, im_neg = halves(dot3_stacked(back_rows, split(for_im)))
    last = jnp.concatenate([re_pos + re_neg, im_neg - im_pos], axis=1)
    framed = dot3(split(last), pair(tables, 4, 2 * LANES, period)) * (2.0 / (period * period))
    grad[...] = framed
    lower, _ = place_in_pair("ty")
    rim[...] = jnp.where(lower, framed[:radius], framed[radius + tile :])


VMEM = pl.BlockSpec(memory_space=pltpu.VMEM)
SMEM = pl.BlockSpec(memory_space=pltpu.SMEM)
ANY = pl.BlockSpec(memory_space=pl.ANY)


def shape(*dims):
    return jax.ShapeDtypeStruct(dims, F32)


def call(kernel, name, out_shape, in_specs, scratch=(), aliases=None, micros=1):
    return pl.pallas_call(
        kernel,
        out_shape=out_shape,
        in_specs=in_specs,
        out_specs=[VMEM] * len(out_shape),
        scratch_shapes=scratch,
        input_output_aliases=aliases or {},
        compiler_params=pltpu.CompilerParams(vmem_limit_bytes=10 * 1024 * 1024),
        cost_estimate=pl.CostEstimate(
            flops=micros * 10**9, bytes_accessed=2**20, transcendentals=0
        ),
        name=name,
    )


def gather_all(copies):
    return lax.all_to_all(copies, ("ty", "tx"), 0, 0, tiled=True)


def body(latent, kernels, socs_weights, dose_scale, inv_slope, edge_pixels, threshold_pick):
    tile = latent.shape[0]
    count, taps = kernels.shape[1], kernels.shape[-1]
    samples = edge_pixels.shape[1]
    radius = (taps - 1) // 2
    period = tile + 2 * radius
    half = period // 2
    tables = jnp.asarray(wave_tables(period, tile))
    token = shape(8, LANES)
    packed = shape(tile // 2, 2 * radius)
    devices = lax.axis_size("ty") * lax.axis_size("tx")

    spec = []

    def spectra(start, parts, *after):
        given = spec + list(after)
        *out, done = call(
            functools.partial(spectra_kernel, start, parts),
            "spectra",
            [shape(count, period, 2 * LANES)] * 2 + [token],
            [VMEM] * 2 + [ANY] * len(given),
            scratch=[pltpu.VMEM((period, LANES), F32)],
            aliases={2: 0, 3: 1} if spec else None,
            micros=2,
        )(kernels, tables, *given)
        spec[:] = out
        return done

    partner, outside = swap("tx", latent), swap_outside("tx", latent)
    quarter = count // 4
    done = spectra(0, quarter)
    band, done = call(
        band_kernel, "band", [shape(tile, period), token], [VMEM] * 3 + [ANY]
    )(latent, partner, outside, done)
    partner = swap("ty", band)
    done = spectra(quarter, quarter, done)
    rim, done = call(
        relay_rows_kernel, "relay", [shape(radius, period), token], [VMEM, ANY]
    )(partner, done)
    rim = ring("ty", rim)
    spectra(2 * quarter, count - 2 * quarter, done)

    field_re, field_im, sampled, copies = call(
        field_kernel,
        "field",
        [shape(count, tile, LANES)] * 2
        + [shape(1, 2 * samples), shape(devices, 1, 2 * samples)],
        [SMEM] + [VMEM] * 8,
        scratch=[
            pltpu.VMEM((period, period), F32),
            pltpu.VMEM((4, half, 2 * LANES), F32),
        ],
        micros=7,
    )(socs_weights, *spec, band, partner, rim, edge_pixels, inv_slope, tables)

    gathered = gather_all(copies).reshape(devices, 2 * samples)
    grid, tail_mean = call(
        source_kernel,
        "source",
        [shape(tile, LANES), shape(1, 1)],
        [SMEM] * 3 + [VMEM] * 3,
        micros=2,
    )(socs_weights, dose_scale, threshold_pick, gathered, sampled, edge_pixels)
    grad, rim = call(
        gradient_kernel,
        "gradient",
        [shape(period, period), shape(radius, period)],
        [SMEM] + [VMEM] * 6,
        scratch=[pltpu.VMEM((period, 2 * LANES), F32)] * 2,
        micros=6,
    )(socs_weights, grid, *spec, field_re, field_im, tables)

    rim = ring("ty", rim, back=True)
    (partner,) = call(fold_rows_kernel, "fold", [shape(tile, period)], [VMEM] * 2)(
        grad, rim
    )
    partner = swap("ty", partner)
    band, near, far = call(
        fold_band_kernel, "fold", [shape(tile, period)] + [packed] * 2, [VMEM] * 2
    )(grad, partner)
    near, far = swap("tx", near), swap_outside("tx", far)
    (steering,) = call(finish_kernel, "finish", [shape(tile, tile)], [VMEM] * 4)(
        band, near, far, latent
    )
    return (steering, tail_mean.reshape(1))


def solution(mesh):
    placed = (P("ty", "tx"), P(), P(), P(), P("ty", "tx"), P("ty", "tx"), P())
    return jax.shard_map(
        body, mesh=mesh, in_specs=placed, out_specs=(P("ty", "tx"), P()), check_vma=False
    )
```

```python
import functools
import math

import jax
import jax.numpy as jnp
import ml_dtypes
import numpy as np
from jax import lax
from jax.experimental import pallas as pl
from jax.experimental.pallas import tpu as pltpu
from jax.sharding import PartitionSpec as P

STEEPNESS = 4.0
RESIST_LEVEL = 0.7
SOFTNESS = 0.25
LANES = 128
BATCH = 3
F32 = jnp.float32
BF16 = jnp.bfloat16


def split(x):
    high = x.astype(BF16)
    return high, (x - high.astype(F32)).astype(BF16)


def dot(a, b):
    return jnp.dot(a, b, preferred_element_type=F32)


def dot3(a, b):
    return dot(a[0], b[0]) + dot(a[0], b[1]) + dot(a[1], b[0])


def stacked(pair):
    return jnp.concatenate(pair, axis=0)


def dot3_stacked(a, b):
    high, both = a
    count = high.shape[0]
    tall = dot(both, b[0])
    return tall[:count] + tall[count:] + dot(high, b[1])


def wave_tables(period, tile):
    half = period // 2
    turn = (np.arange(half) + 0.5) * (2.0 * math.pi / period)
    size = 2 * LANES

    def parts(table):
        high = table.astype(ml_dtypes.bfloat16)
        return high, (table - high.astype(np.float64)).astype(ml_dtypes.bfloat16)

    def both(places):
        angle = turn[:, None] * places[None, :]
        return np.cos(angle), np.sin(angle)

    def whole_table(places, by_lane):
        cos, sin = both(places)
        out = np.zeros((size, size))
        out[:half, : len(places)] = cos
        start = LANES if by_lane else half
        out[start : start + half, : len(places)] = sin
        return out

    place = np.arange(period)
    wide = whole_table(place, True)
    tall = whole_table(place, False)
    centred = whole_table(place - (tile - 1) / 2, False)
    out = np.zeros((12, size, size), ml_dtypes.bfloat16)
    for first, table in ((0, wide.T), (2, tall), (4, wide), (6, centred), (8, centred.T)):
        out[first], out[first + 1] = parts(table)
    rows = tile // 2
    for i, table in enumerate(both(np.arange(rows) + 0.5)):
        high, low = parts(table)
        top = 2 * rows * i
        out[10, top : top + rows, :half] = high.T
        out[10, top : top + rows, half:period] = high.T
        out[10, top + rows : top + 2 * rows, :half] = low.T
        top = half * i
        out[11, top : top + half, :rows] = high
        out[11, top : top + half, rows : 2 * rows] = high
        out[11, top : top + half, 2 * rows : 3 * rows] = low
    return out


def pair(tables, first, rows, cols):
    return tables[first, :rows, :cols], tables[first + 1, :rows, :cols]


def whole(parts):
    return parts[0].astype(F32) + parts[1].astype(F32)


def halves(x):
    return x[:, :LANES], x[:, LANES:]


def place_in_pair(axis):
    index, count = lax.axis_index(axis), lax.axis_size(axis)
    lower = lax.rem(index, 2) == 0
    return lower, jnp.where(lower, index > 0, index < count - 1)


def swap(axis, x):
    return lax.ppermute(x, axis, [(i, i ^ 1) for i in range(lax.axis_size(axis))])


def swap_outside(axis, x):
    count = lax.axis_size(axis)
    pairs = [(0, 0), (count - 1, count - 1)]
    for low in range(1, count - 1, 2):
        pairs += [(low, low + 1), (low + 1, low)]
    return lax.ppermute(x, axis, pairs)


def ring(axis, x, back=False):
    count = lax.axis_size(axis)
    cycle = list(range(0, count, 2)) + list(range(count - 1, 0, -2))
    pairs = list(zip(cycle, cycle[1:] + cycle[:1]))
    return lax.ppermute(x, axis, [(b, a) if back else (a, b) for a, b in pairs])


def spectra_kernel(start, parts, kern, tables, *rest):
    out_re, out_im, token, edge = rest[-4:]
    period = out_re.shape[1]
    half = period // 2
    last = kern.shape[-1] - 1
    cols = pair(tables, 0, last, 2 * LANES)
    cols = (stacked((cols[0], cols[0])), cols[1])
    end_row = whole((tables[0, last : last + 16, :], tables[1, last : last + 16, :]))[:1]
    high, low = pair(tables, 2, period, last)
    rows = stacked(
        (
            jnp.concatenate([high, high], axis=1),
            jnp.concatenate([low, jnp.zeros_like(low)], axis=1),
        )
    )
    end_col = whole(pair(tables, 2, period, 2 * LANES))[:, last : last + 1]
    edge[...] = jnp.broadcast_to(end_col, edge.shape)

    def along_lanes(planes):
        main = stacked([plane[:last] for plane in planes])
        tail = stacked([plane[last:] for plane in planes])
        tail = jnp.concatenate([tail, jnp.zeros((-tail.shape[0] % 16, last + 1), F32)], axis=0)
        both = stacked((main, tail))
        high, low = split(both[:, :last])
        out = dot(jnp.concatenate([high, low], axis=1), cols[0]) + dot(high, cols[1])
        out = out + both[:, last:] * end_row
        first = len(planes) * last
        return [
            (out[i * last : (i + 1) * last], out[first + i : first + i + 1])
            for i in range(len(planes))
        ]

    def along_rows(wide, tail):
        tall = dot(rows, stacked(split(wide)))
        outer = [edge[...] * tail[:, :LANES], edge[...] * tail[:, LANES:]]
        return tall[:period] + tall[period:] + jnp.concatenate(outer, axis=1)

    def mixed(real, imag):
        real_cos, real_sin = halves(real)
        imag_cos, imag_sin = halves(imag)
        return (
            jnp.concatenate([real_cos - imag_sin, real_cos + imag_sin], axis=1),
            jnp.concatenate([real_sin + imag_cos, imag_cos - real_sin], axis=1),
        )

    def step(group, carry):
        first = start + group * BATCH
        planes = along_lanes([kern[c, group * BATCH + i] for i in range(BATCH) for c in range(2)])
        for i in range(BATCH):
            k = first + i
            (real, real_tail), (imag, imag_tail) = planes[2 * i : 2 * i + 2]
            wide_re, wide_im = mixed(real, imag)
            tail_re, tail_im = mixed(real_tail, imag_tail)
            tall_re = along_rows(wide_re, tail_re)
            tall_im = along_rows(wide_im, tail_im)
            out_re[k, :half] = tall_re[:half] - tall_im[half:]
            out_re[k, half:] = tall_re[:half] + tall_im[half:]
            out_im[k, :half] = tall_im[:half] + tall_re[half:]
            out_im[k, half:] = tall_im[:half] - tall_re[half:]
        return carry

    lax.fori_loop(0, parts // BATCH, step, 0)


def pack(x):
    count = x.shape[0] // 2
    return jnp.concatenate([x[:count], x[count:]], axis=1)


def unpack(x):
    width = x.shape[1] // 2
    return jnp.concatenate([x[:, :width], x[:, width:]], axis=0)


def band_kernel(middle, partner, outside, after, band, token):
    tile = middle.shape[0]
    radius = (band.shape[1] - tile) // 2
    lower, other = place_in_pair("tx")

    def transmit(x):
        return 0.5 * (1.0 + jnp.tanh(x))

    near = transmit(jnp.where(lower, partner[:, :radius], partner[:, tile - radius :]))
    far = transmit(jnp.where(lower, outside[:, tile - radius :], outside[:, :radius]))
    far = jnp.where(other, far, 0.0)
    band[:, :radius] = jnp.where(lower, far, near)
    band[:, radius : radius + tile] = transmit(middle[...])
    band[:, radius + tile :] = jnp.where(lower, near, far)
    token[...] = jnp.zeros(token.shape, F32)


def relay_rows_kernel(partner, after, rim, token):
    radius = rim.shape[0]
    tile = partner.shape[0]
    lower, _ = place_in_pair("ty")
    rim[...] = jnp.where(lower, partner[tile - radius :], partner[:radius])
    token[...] = jnp.zeros(token.shape, F32)


def fold_rows_kernel(grad, rim, out):
    radius = rim.shape[0]
    tile = out.shape[0]
    lower, _ = place_in_pair("ty")
    count, index = lax.axis_size("ty"), lax.axis_index("ty")
    comes = jnp.where(lower, index < count - 2, index > 1)
    outer = jnp.where(comes, rim[...], 0.0)
    top = jnp.where(lower, grad[radius + tile :], outer)
    bottom = jnp.where(lower, outer, grad[:radius])
    out[:radius] = top
    out[radius:] = jnp.zeros((tile - radius, out.shape[1]), F32)
    out[tile - radius :] += bottom


def fold_band_kernel(grad, partner, band, far):
    tile = band.shape[0]
    radius = far.shape[1] // 2
    lower, _ = place_in_pair("tx")
    band[...] = grad[radius : radius + tile] + partner[...]
    far[...] = jnp.where(lower, pack(band[:, :radius]), pack(band[:, radius + tile :]))


def near_rim_kernel(band, near):
    tile = band.shape[0]
    radius = near.shape[1] // 2
    lower, _ = place_in_pair("tx")
    near[...] = jnp.where(lower, pack(band[:, radius + tile :]), pack(band[:, :radius]))


def finish_kernel(band, near, far, latent, steering):
    tile = latent.shape[0]
    radius = (band.shape[1] - tile) // 2
    lower, other = place_in_pair("tx")
    inner = unpack(near[...])
    outer = jnp.where(other, unpack(far[...]), 0.0)
    steering[...] = band[:, radius : radius + tile]
    steering[:, :radius] += jnp.where(lower, outer, inner)
    steering[:, tile - radius :] += jnp.where(lower, inner, outer)
    value = jnp.tanh(latent[...])
    steering[...] = steering[...] * 0.5 * (1.0 - value * value)


def total_weight(weights, kernels):
    total = weights[0]
    for k in range(1, kernels):
        total = total + weights[k]
    return jnp.full((1, 1), total, F32)


def sample_places(pixels, tile):
    row = ((pixels.astype(F32) + 0.5) * (1.0 / tile)).astype(jnp.int32)
    held = jnp.where(row < tile // 2, tile - 1 - row, row - tile // 2)
    return held, pixels - row * tile


def field_kernel(
    weights, spec_re, spec_im, band, partner, rim, pixels, slopes, tables,
    field_re, field_im, sampled, copies, framed, mask,
):
    kernels, period, _ = spec_re.shape
    half = period // 2
    tile = field_re.shape[1]
    radius = rim.shape[0]
    lower, other = place_in_pair("ty")
    outer = jnp.where(other, rim[...], 0.0)
    framed[:radius] = jnp.where(lower, outer, partner[tile - radius :])
    framed[radius + tile :] = jnp.where(lower, partner[:radius], outer)
    framed[radius : radius + tile] = band[...]
    wide = dot3(split(framed[...]), pair(tables, 0, period, 2 * LANES))
    tall = dot3(pair(tables, 6, period, period), split(wide)) * (1.0 / (period * period))
    cos_cos, cos_sin = halves(tall[:half])
    sin_cos, sin_sin = halves(tall[half:])
    same, other = cos_cos - sin_sin, cos_cos + sin_sin
    joint, cross = sin_cos + cos_sin, sin_cos - cos_sin
    mask[0, :, :LANES], mask[0, :, LANES:] = same, other
    mask[1, :, :LANES], mask[1, :, LANES:] = -joint, -cross
    mask[2, :, :LANES], mask[2, :, LANES:] = other, same
    mask[3, :, :LANES], mask[3, :, LANES:] = cross, joint
    cos_lift = tables[10, :tile, :period]
    sin_lift = tables[10, tile : 2 * tile, :period]
    rows = tile // 2

    def lift(table, x):
        out = dot(table, stacked(split(x)))
        return out[:rows] + out[rows:]

    across = pair(tables, 4, 2 * LANES, LANES)
    across = (across[0], jnp.concatenate(across, axis=1))

    def lifted(k):
        pos_re, pos_im = spec_re[k, :half], spec_im[k, :half]
        neg_re, neg_im = spec_re[k, half:], spec_im[k, half:]
        up_re = mask[0] * pos_re - mask[1] * pos_im
        up_im = mask[0] * pos_im + mask[1] * pos_re
        down_re = mask[2] * neg_re - mask[3] * neg_im
        down_im = mask[2] * neg_im + mask[3] * neg_re
        even_re = lift(cos_lift, up_re + down_re)
        even_im = lift(cos_lift, up_im + down_im)
        odd_re = lift(sin_lift, up_im - down_im)
        odd_im = lift(sin_lift, up_re - down_re)
        re_pos, re_neg = halves(stacked((even_re - odd_re, even_re + odd_re)))
        im_pos, im_neg = halves(stacked((even_im + odd_im, even_im - odd_im)))
        rows_re = jnp.concatenate([re_pos + re_neg, im_neg - im_pos], axis=1)
        rows_im = jnp.concatenate([im_pos + im_neg, re_pos - re_neg], axis=1)
        return [rows_re, rows_im]

    def step(group, intensity):
        first = group * BATCH
        rows = stacked([row for i in range(BATCH) for row in lifted(first + i)])
        high, low = split(rows)
        by_high, by_low = halves(dot(high, across[1]))
        both = by_high + by_low + dot(low, across[0])
        for i in range(BATCH):
            real = both[2 * i * tile : (2 * i + 1) * tile]
            imag = both[(2 * i + 1) * tile : (2 * i + 2) * tile]
            field_re[first + i] = real
            field_im[first + i] = imag
            intensity = intensity + weights[first + i] * (real * real + imag * imag)
        return intensity

    intensity = lax.fori_loop(
        0, kernels // BATCH, step, jnp.zeros((tile, LANES), F32)
    )
    intensity = intensity / total_weight(weights, kernels)
    samples = pixels.shape[1]
    row, col = sample_places(pixels[...], tile)
    in_col = lax.broadcasted_iota(jnp.int32, (LANES, samples), 0) == col
    one_hot = jnp.where(in_col, 1.0, 0.0).astype(BF16)
    high, rest = split(intensity)
    low = intensity - high.astype(F32) - rest.astype(F32)
    picked = dot(high, one_hot) + dot(rest, one_hot) + dot(low.astype(BF16), one_hot)
    in_row = lax.broadcasted_iota(jnp.int32, (tile, samples), 0) == row
    own = jnp.sum(jnp.where(in_row, picked, 0.0), axis=0, keepdims=True)
    sampled[...] = jnp.concatenate([own, slopes[...]], axis=1)
    copies[...] = jnp.broadcast_to(sampled[...][None], copies.shape)


def sigmoid(x):
    return 1.0 / (1.0 + jnp.exp(-x))


def errors(intensity, slope, dose):
    resist = 0.5 * jnp.tanh(0.5 * STEEPNESS * (dose * intensity - RESIST_LEVEL))
    offset = resist * slope
    return resist, offset, offset * offset


def source_kernel(weights, doses, pick, gathered, sampled, pixels, placed_sum, tail):
    kernels = weights.shape[0]
    tile = placed_sum.shape[0]
    samples = pixels.shape[1]
    devices = gathered.shape[0]
    corners = doses.shape[0]
    per_corner = devices * samples
    everyone, every_slope = gathered[:, :samples], gathered[:, samples:]
    pick_corner = pick[0] // per_corner
    remain = pick[0] - pick_corner * per_corner
    place = lax.broadcasted_iota(jnp.int32, (devices, samples), 0) * samples
    place = place + lax.broadcasted_iota(jnp.int32, (devices, samples), 1)
    _, _, picked = errors(everyone, every_slope, doses[pick_corner])
    threshold = jnp.sum(jnp.where(place == remain, picked, 0.0), keepdims=True)

    def corner(c, sums):
        _, _, error = errors(everyone, every_slope, doses[c])
        soft = sigmoid((error - threshold) * (1.0 / SOFTNESS))
        return sums[0] + soft, sums[1] + error * soft

    zero = jnp.zeros((devices, samples), F32)
    soft_sum, error_sum = lax.fori_loop(
        0, corners, corner, (zero, zero), unroll=4 if devices <= 32 else 1
    )
    soft_total = jnp.sum(soft_sum, keepdims=True)
    tail_mean = jnp.sum(error_sum, keepdims=True) / soft_total
    tail[...] = tail_mean

    own, slope = sampled[:, :samples], sampled[:, samples:]
    which = lax.broadcasted_iota(jnp.int32, (corners, samples), 0)
    dose = jnp.zeros((corners, samples), F32)
    for c in range(corners):
        dose = jnp.where(which == c, doses[c], dose)
    resist, offset, error = errors(own, slope, dose)
    soft = sigmoid((error - threshold) * (1.0 / SOFTNESS))
    slope_soft = soft * (1.0 - soft) * (1.0 / SOFTNESS)
    chain = 2.0 * STEEPNESS * offset * slope * dose * (0.25 - resist * resist)
    coefficient = (soft + (error - tail_mean) * slope_soft) * (corners * per_corner / soft_total)
    summed = jnp.sum(coefficient * chain, axis=0, keepdims=True)
    summed = summed / total_weight(weights, kernels)

    row, col = sample_places(pixels[...], tile)
    in_row = lax.broadcasted_iota(jnp.int32, (tile, samples), 0) == row
    in_col = lax.broadcasted_iota(jnp.int32, (LANES, samples), 0) == col
    one_hot = jnp.where(in_col, 1.0, 0.0).astype(BF16)
    placed = jnp.where(in_row, summed, 0.0)
    high, rest = split(placed)
    low = (placed - high.astype(F32) - rest.astype(F32)).astype(BF16)
    grid = jnp.zeros((tile, LANES), F32)
    for part in (high, rest, low):
        grid = grid + lax.dot_general(
            part, one_hot, (((1,), (1,)), ((), ())), preferred_element_type=F32
        )

    placed_sum[...] = grid


def gradient_kernel(
    weights, grid, spec_re, spec_im, field_re, field_im, tables,
    grad, rim, total_re, total_im,
):
    kernels, period, _ = spec_re.shape
    half = period // 2
    tile = field_re.shape[1]
    radius = (period - tile) // 2
    cols = pair(tables, 0, LANES, 2 * LANES)
    cols = (stacked((cols[0], cols[0])), cols[1])
    rows = tile // 2
    cos_rows = tables[11, :half, : 3 * rows]
    sin_rows = tables[11, half:period, : 3 * rows]

    def along_rows(wide):
        out = []
        for table, x in (
            (cos_rows, wide[:rows] + wide[rows:]),
            (sin_rows, wide[:rows] - wide[rows:]),
        ):
            high, low = split(x)
            out.append(dot(table, stacked((high, low, high))))
        return out

    total_re[...] = jnp.zeros((period, 2 * LANES), F32)
    total_im[...] = jnp.zeros((period, 2 * LANES), F32)

    def step(group, carry):
        sources = []
        for i in range(BATCH):
            k = group * BATCH + i
            weighted = grid[...] * weights[k]
            sources += [weighted * field_re[k], weighted * field_im[k]]
        high, low = split(stacked(sources))
        both = dot(jnp.concatenate([high, low], axis=1), cols[0]) + dot(high, cols[1])
        for i in range(BATCH):
            k = group * BATCH + i
            real_cos, real_sin = halves(both[2 * i * tile : (2 * i + 1) * tile])
            imag_cos, imag_sin = halves(both[(2 * i + 1) * tile : (2 * i + 2) * tile])
            wide_re = jnp.concatenate([real_cos + imag_sin, real_cos - imag_sin], axis=1)
            wide_im = jnp.concatenate([imag_cos - real_sin, imag_cos + real_sin], axis=1)
            cos_re, sin_re = along_rows(wide_re)
            cos_im, sin_im = along_rows(wide_im)
            for start, sign in ((0, 1.0), (half, -1.0)):
                part = slice(start, start + half)
                wave_re = cos_re + sign * sin_im
                wave_im = cos_im - sign * sin_re
                own_re, own_im = spec_re[k, part], spec_im[k, part]
                total_re[part] += own_re * wave_re + own_im * wave_im
                total_im[part] += own_re * wave_im - own_im * wave_re
        return carry

    lax.fori_loop(0, kernels // BATCH, step, 0)
    pos_re, neg_re = total_re[:half], total_re[half:]
    pos_im, neg_im = total_im[:half], total_im[half:]
    back_rows = pair(tables, 8, period, period)
    back_rows = (back_rows[0], stacked(back_rows))
    for_re = jnp.concatenate([pos_re + neg_re, neg_im - pos_im], axis=0)
    for_im = jnp.concatenate([pos_im + neg_im, pos_re - neg_re], axis=0)
    re_pos, re_neg = halves(dot3_stacked(back_rows, split(for_re)))
    im_pos, im_neg = halves(dot3_stacked(back_rows, split(for_im)))
    last = jnp.concatenate([re_pos + re_neg, im_neg - im_pos], axis=1)
    framed = dot3(split(last), pair(tables, 4, 2 * LANES, period)) * (2.0 / (period * period))
    grad[...] = framed
    lower, _ = place_in_pair("ty")
    rim[...] = jnp.where(lower, framed[:radius], framed[radius + tile :])


VMEM = pl.BlockSpec(memory_space=pltpu.VMEM)
SMEM = pl.BlockSpec(memory_space=pltpu.SMEM)
ANY = pl.BlockSpec(memory_space=pl.ANY)


def shape(*dims):
    return jax.ShapeDtypeStruct(dims, F32)


def call(kernel, name, out_shape, in_specs, scratch=(), aliases=None, micros=1):
    return pl.pallas_call(
        kernel,
        out_shape=out_shape,
        in_specs=in_specs,
        out_specs=[VMEM] * len(out_shape),
        scratch_shapes=scratch,
        input_output_aliases=aliases or {},
        compiler_params=pltpu.CompilerParams(vmem_limit_bytes=10 * 1024 * 1024),
        cost_estimate=pl.CostEstimate(
            flops=micros * 10**9, bytes_accessed=2**20, transcendentals=0
        ),
        name=name,
    )


def gather_all(copies):
    return lax.all_to_all(copies, ("ty", "tx"), 0, 0, tiled=True)


def body(latent, kernels, socs_weights, dose_scale, inv_slope, edge_pixels, threshold_pick):
    tile = latent.shape[0]
    count, taps = kernels.shape[1], kernels.shape[-1]
    samples = edge_pixels.shape[1]
    radius = (taps - 1) // 2
    period = tile + 2 * radius
    half = period // 2
    tables = jnp.asarray(wave_tables(period, tile))
    token = shape(8, LANES)
    packed = shape(tile // 2, 2 * radius)
    devices = lax.axis_size("ty") * lax.axis_size("tx")

    spec = []

    def spectra(start, parts, *after):
        given = spec + list(after)
        *out, done = call(
            functools.partial(spectra_kernel, start, parts),
            "spectra",
            [shape(count, period, 2 * LANES)] * 2 + [token],
            [VMEM] * 2 + [ANY] * len(given),
            scratch=[pltpu.VMEM((period, LANES), F32)],
            aliases={2: 0, 3: 1} if spec else None,
            micros=2,
        )(kernels[:, start : start + parts], tables, *given)
        spec[:] = out
        return done

    partner, outside = swap("tx", latent), swap_outside("tx", latent)
    quarter = count // 4
    done = spectra(0, quarter)
    band, done = call(
        band_kernel, "band", [shape(tile, period), token], [VMEM] * 3 + [ANY]
    )(latent, partner, outside, done)
    partner = swap("ty", band)
    done = spectra(quarter, quarter, done)
    rim, done = call(
        relay_rows_kernel, "relay", [shape(radius, period), token], [VMEM, ANY]
    )(partner, done)
    rim = ring("ty", rim)
    spectra(2 * quarter, count - 2 * quarter, done)

    field_re, field_im, sampled, copies = call(
        field_kernel,
        "field",
        [shape(count, tile, LANES)] * 2
        + [shape(1, 2 * samples), shape(devices, 1, 2 * samples)],
        [SMEM] + [VMEM] * 8,
        scratch=[
            pltpu.VMEM((period, period), F32),
            pltpu.VMEM((4, half, 2 * LANES), F32),
        ],
        micros=7,
    )(socs_weights, *spec, band, partner, rim, edge_pixels, inv_slope, tables)

    gathered = gather_all(copies).reshape(devices, 2 * samples)
    grid, tail_mean = call(
        source_kernel,
        "source",
        [shape(tile, LANES), shape(1, 1)],
        [SMEM] * 3 + [VMEM] * 3,
        micros=2,
    )(socs_weights, dose_scale, threshold_pick, gathered, sampled, edge_pixels)
    grad, rim = call(
        gradient_kernel,
        "gradient",
        [shape(period, period), shape(radius, period)],
        [SMEM] + [VMEM] * 6,
        scratch=[pltpu.VMEM((period, 2 * LANES), F32)] * 2,
        micros=6,
    )(socs_weights, grid, *spec, field_re, field_im, tables)

    rim = ring("ty", rim, back=True)
    (partner,) = call(fold_rows_kernel, "fold", [shape(tile, period)], [VMEM] * 2)(
        grad, rim
    )
    partner = swap("ty", partner)
    band, far = call(
        fold_band_kernel, "fold", [shape(tile, period), packed], [VMEM] * 2
    )(grad, partner)
    far = swap_outside("tx", far)
    (near,) = call(near_rim_kernel, "near", [packed], [VMEM])(band)
    near = swap("tx", near)
    (steering,) = call(finish_kernel, "finish", [shape(tile, tile)], [VMEM] * 4)(
        band, near, far, latent
    )
    return (steering, tail_mean.reshape(1))


def solution(mesh):
    placed = (P("ty", "tx"), P(), P(), P(), P("ty", "tx"), P("ty", "tx"), P())
    return jax.shard_map(
        body, mesh=mesh, in_specs=placed, out_specs=(P("ty", "tx"), P()), check_vma=False
    )
```

```python
import functools
import math

import jax
import jax.numpy as jnp
import ml_dtypes
import numpy as np
from jax import lax
from jax.experimental import pallas as pl
from jax.experimental.pallas import tpu as pltpu
from jax.sharding import PartitionSpec as P

STEEPNESS = 4.0
RESIST_LEVEL = 0.7
SOFTNESS = 0.25
LANES = 128
BATCH = 3
F32 = jnp.float32
BF16 = jnp.bfloat16


def split(x):
    high = x.astype(BF16)
    return high, (x - high.astype(F32)).astype(BF16)


def dot(a, b):
    return jnp.dot(a, b, preferred_element_type=F32)


def dot3(a, b):
    return dot(a[0], b[0]) + dot(a[0], b[1]) + dot(a[1], b[0])


def stacked(pair):
    return jnp.concatenate(pair, axis=0)


def dot3_stacked(a, b):
    high, both = a
    count = high.shape[0]
    tall = dot(both, b[0])
    return tall[:count] + tall[count:] + dot(high, b[1])


def wave_tables(period, tile):
    half = period // 2
    turn = (np.arange(half) + 0.5) * (2.0 * math.pi / period)
    size = 2 * LANES

    def parts(table):
        high = table.astype(ml_dtypes.bfloat16)
        return high, (table - high.astype(np.float64)).astype(ml_dtypes.bfloat16)

    def both(places):
        angle = turn[:, None] * places[None, :]
        return np.cos(angle), np.sin(angle)

    def whole_table(places, by_lane):
        cos, sin = both(places)
        out = np.zeros((size, size))
        out[:half, : len(places)] = cos
        start = LANES if by_lane else half
        out[start : start + half, : len(places)] = sin
        return out

    place = np.arange(period)
    wide = whole_table(place, True)
    tall = whole_table(place, False)
    centred = whole_table(place - (tile - 1) / 2, False)
    out = np.zeros((12, size, size), ml_dtypes.bfloat16)
    for first, table in ((0, wide.T), (2, tall), (4, wide), (6, centred), (8, centred.T)):
        out[first], out[first + 1] = parts(table)
    rows = tile // 2
    for i, table in enumerate(both(np.arange(rows) + 0.5)):
        high, low = parts(table)
        top = 2 * rows * i
        out[10, top : top + rows, :half] = high.T
        out[10, top : top + rows, half:period] = high.T
        out[10, top + rows : top + 2 * rows, :half] = low.T
        top = half * i
        out[11, top : top + half, :rows] = high
        out[11, top : top + half, rows : 2 * rows] = high
        out[11, top : top + half, 2 * rows : 3 * rows] = low
    return out


def pair(tables, first, rows, cols):
    return tables[first, :rows, :cols], tables[first + 1, :rows, :cols]


def whole(parts):
    return parts[0].astype(F32) + parts[1].astype(F32)


def halves(x):
    return x[:, :LANES], x[:, LANES:]


def place_in_pair(axis):
    index, count = lax.axis_index(axis), lax.axis_size(axis)
    lower = lax.rem(index, 2) == 0
    return lower, jnp.where(lower, index > 0, index < count - 1)


def swap(axis, x):
    return lax.ppermute(x, axis, [(i, i ^ 1) for i in range(lax.axis_size(axis))])


def swap_outside(axis, x):
    count = lax.axis_size(axis)
    pairs = [(0, 0), (count - 1, count - 1)]
    for low in range(1, count - 1, 2):
        pairs += [(low, low + 1), (low + 1, low)]
    return lax.ppermute(x, axis, pairs)


def ring(axis, x, back=False):
    count = lax.axis_size(axis)
    cycle = list(range(0, count, 2)) + list(range(count - 1, 0, -2))
    pairs = list(zip(cycle, cycle[1:] + cycle[:1]))
    return lax.ppermute(x, axis, [(b, a) if back else (a, b) for a, b in pairs])


def spectra_kernel(start, groups, kern, tables, *rest):
    *outs, token, edge = rest[-2 - groups :]
    period = outs[0].shape[2]
    half = period // 2
    last = kern.shape[-1] - 1
    cols = pair(tables, 0, last, 2 * LANES)
    cols = (stacked((cols[0], cols[0])), cols[1])
    end_row = whole((tables[0, last : last + 16, :], tables[1, last : last + 16, :]))[:1]
    high, low = pair(tables, 2, period, last)
    rows = stacked(
        (
            jnp.concatenate([high, high], axis=1),
            jnp.concatenate([low, jnp.zeros_like(low)], axis=1),
        )
    )
    end_col = whole(pair(tables, 2, period, 2 * LANES))[:, last : last + 1]
    edge[...] = jnp.broadcast_to(end_col, edge.shape)

    def along_lanes(planes):
        main = stacked([plane[:last] for plane in planes])
        tail = stacked([plane[last:] for plane in planes])
        tail = jnp.concatenate([tail, jnp.zeros((-tail.shape[0] % 16, last + 1), F32)], axis=0)
        both = stacked((main, tail))
        high, low = split(both[:, :last])
        out = dot(jnp.concatenate([high, low], axis=1), cols[0]) + dot(high, cols[1])
        out = out + both[:, last:] * end_row
        first = len(planes) * last
        return [
            (out[i * last : (i + 1) * last], out[first + i : first + i + 1])
            for i in range(len(planes))
        ]

    def along_rows(wide, tail):
        tall = dot(rows, stacked(split(wide)))
        outer = [edge[...] * tail[:, :LANES], edge[...] * tail[:, LANES:]]
        return tall[:period] + tall[period:] + jnp.concatenate(outer, axis=1)

    def mixed(real, imag):
        real_cos, real_sin = halves(real)
        imag_cos, imag_sin = halves(imag)
        return (
            jnp.concatenate([real_cos - imag_sin, real_cos + imag_sin], axis=1),
            jnp.concatenate([real_sin + imag_cos, imag_cos - real_sin], axis=1),
        )

    for group, out in enumerate(outs):
        first = start + group * BATCH
        planes = along_lanes([kern[c, first + k] for k in range(BATCH) for c in range(2)])
        for k in range(BATCH):
            (real, real_tail), (imag, imag_tail) = planes[2 * k : 2 * k + 2]
            wide_re, wide_im = mixed(real, imag)
            tail_re, tail_im = mixed(real_tail, imag_tail)
            tall_re = along_rows(wide_re, tail_re)
            tall_im = along_rows(wide_im, tail_im)
            out[0, k, :half] = tall_re[:half] - tall_im[half:]
            out[0, k, half:] = tall_re[:half] + tall_im[half:]
            out[1, k, :half] = tall_im[:half] + tall_re[half:]
            out[1, k, half:] = tall_im[:half] - tall_re[half:]


def pack(x):
    count = x.shape[0] // 2
    return jnp.concatenate([x[:count], x[count:]], axis=1)


def unpack(x):
    width = x.shape[1] // 2
    return jnp.concatenate([x[:, :width], x[:, width:]], axis=0)


def own_kernel(latent, transmit, token):
    transmit[...] = 0.5 * (1.0 + jnp.tanh(latent[...]))
    token[...] = jnp.zeros(token.shape, F32)


def band_kernel(middle, partner, outside, after, band, token):
    tile = middle.shape[0]
    radius = (band.shape[1] - tile) // 2
    lower, other = place_in_pair("tx")

    def transmit(x):
        return 0.5 * (1.0 + jnp.tanh(x))

    near = transmit(jnp.where(lower, partner[:, :radius], partner[:, tile - radius :]))
    far = transmit(jnp.where(lower, outside[:, tile - radius :], outside[:, :radius]))
    far = jnp.where(other, far, 0.0)
    band[:, :radius] = jnp.where(lower, far, near)
    band[:, radius : radius + tile] = middle[...]
    band[:, radius + tile :] = jnp.where(lower, near, far)
    token[...] = jnp.zeros(token.shape, F32)


def relay_rows_kernel(partner, after, rim, token):
    radius = rim.shape[0]
    tile = partner.shape[0]
    lower, _ = place_in_pair("ty")
    rim[...] = jnp.where(lower, partner[tile - radius :], partner[:radius])
    token[...] = jnp.zeros(token.shape, F32)


def fold_rows_kernel(grad, rim, out):
    radius = rim.shape[0]
    tile = out.shape[0]
    lower, _ = place_in_pair("ty")
    count, index = lax.axis_size("ty"), lax.axis_index("ty")
    comes = jnp.where(lower, index < count - 2, index > 1)
    outer = jnp.where(comes, rim[...], 0.0)
    top = jnp.where(lower, grad[radius + tile :], outer)
    bottom = jnp.where(lower, outer, grad[:radius])
    out[:radius] = top
    out[radius:] = jnp.zeros((tile - radius, out.shape[1]), F32)
    out[tile - radius :] += bottom


def fold_band_kernel(grad, partner, band, far):
    tile = band.shape[0]
    radius = far.shape[1] // 2
    lower, _ = place_in_pair("tx")
    band[...] = grad[radius : radius + tile] + partner[...]
    far[...] = jnp.where(lower, pack(band[:, :radius]), pack(band[:, radius + tile :]))


def near_rim_kernel(band, near):
    tile = band.shape[0]
    radius = near.shape[1] // 2
    lower, _ = place_in_pair("tx")
    near[...] = jnp.where(lower, pack(band[:, radius + tile :]), pack(band[:, :radius]))


def far_side_kernel(band, far, out):
    tile = out.shape[0]
    radius = (band.shape[1] - tile) // 2
    lower, other = place_in_pair("tx")
    outer = jnp.where(other, unpack(far[...]), 0.0)
    out[...] = band[:, radius : radius + tile]
    out[:, :radius] += jnp.where(lower, outer, 0.0)
    out[:, tile - radius :] += jnp.where(lower, 0.0, outer)


def finish_kernel(total, near, latent, steering):
    tile = latent.shape[0]
    radius = near.shape[1] // 2
    lower, _ = place_in_pair("tx")
    inner = unpack(near[...])
    steering[...] = total[...]
    steering[:, :radius] += jnp.where(lower, 0.0, inner)
    steering[:, tile - radius :] += jnp.where(lower, inner, 0.0)
    value = jnp.tanh(latent[...])
    steering[...] = steering[...] * 0.5 * (1.0 - value * value)


def total_weight(weights, kernels):
    total = weights[0]
    for k in range(1, kernels):
        total = total + weights[k]
    return jnp.full((1, 1), total, F32)


def sample_places(pixels, tile):
    row = ((pixels.astype(F32) + 0.5) * (1.0 / tile)).astype(jnp.int32)
    held = jnp.where(row < tile // 2, tile - 1 - row, row - tile // 2)
    return held, pixels - row * tile


def field_kernel(weights, band, partner, rim, pixels, slopes, tables, *rest):
    *spec, field_re, field_im, sampled, copies, framed, mask = rest
    kernels = weights.shape[0]
    period = band.shape[1]
    half = period // 2
    tile = field_re.shape[1]
    radius = rim.shape[0]
    lower, other = place_in_pair("ty")
    outer = jnp.where(other, rim[...], 0.0)
    framed[:radius] = jnp.where(lower, outer, partner[tile - radius :])
    framed[radius + tile :] = jnp.where(lower, partner[:radius], outer)
    framed[radius : radius + tile] = band[...]
    wide = dot3(split(framed[...]), pair(tables, 0, period, 2 * LANES))
    tall = dot3(pair(tables, 6, period, period), split(wide)) * (1.0 / (period * period))
    cos_cos, cos_sin = halves(tall[:half])
    sin_cos, sin_sin = halves(tall[half:])
    same, other = cos_cos - sin_sin, cos_cos + sin_sin
    joint, cross = sin_cos + cos_sin, sin_cos - cos_sin
    mask[0, :, :LANES], mask[0, :, LANES:] = same, other
    mask[1, :, :LANES], mask[1, :, LANES:] = -joint, -cross
    mask[2, :, :LANES], mask[2, :, LANES:] = other, same
    mask[3, :, :LANES], mask[3, :, LANES:] = cross, joint
    cos_lift = tables[10, :tile, :period]
    sin_lift = tables[10, tile : 2 * tile, :period]
    rows = tile // 2

    def lift(table, x):
        out = dot(table, stacked(split(x)))
        return out[:rows] + out[rows:]

    across = pair(tables, 4, 2 * LANES, LANES)
    across = (across[0], jnp.concatenate(across, axis=1))

    def lifted(own, k):
        pos_re, pos_im = own[0, k, :half], own[1, k, :half]
        neg_re, neg_im = own[0, k, half:], own[1, k, half:]
        up_re = mask[0] * pos_re - mask[1] * pos_im
        up_im = mask[0] * pos_im + mask[1] * pos_re
        down_re = mask[2] * neg_re - mask[3] * neg_im
        down_im = mask[2] * neg_im + mask[3] * neg_re
        even_re = lift(cos_lift, up_re + down_re)
        even_im = lift(cos_lift, up_im + down_im)
        odd_re = lift(sin_lift, up_im - down_im)
        odd_im = lift(sin_lift, up_re - down_re)
        re_pos, re_neg = halves(stacked((even_re - odd_re, even_re + odd_re)))
        im_pos, im_neg = halves(stacked((even_im + odd_im, even_im - odd_im)))
        rows_re = jnp.concatenate([re_pos + re_neg, im_neg - im_pos], axis=1)
        rows_im = jnp.concatenate([im_pos + im_neg, re_pos - re_neg], axis=1)
        return [rows_re, rows_im]

    intensity = jnp.zeros((tile, LANES), F32)
    for group, own in enumerate(spec):
        first = group * BATCH
        lines = stacked([line for i in range(BATCH) for line in lifted(own, i)])
        high, low = split(lines)
        by_high, by_low = halves(dot(high, across[1]))
        both = by_high + by_low + dot(low, across[0])
        for i in range(BATCH):
            real = both[2 * i * tile : (2 * i + 1) * tile]
            imag = both[(2 * i + 1) * tile : (2 * i + 2) * tile]
            field_re[first + i] = real
            field_im[first + i] = imag
            intensity = intensity + weights[first + i] * (real * real + imag * imag)
    intensity = intensity / total_weight(weights, kernels)
    samples = pixels.shape[1]
    row, col = sample_places(pixels[...], tile)
    in_col = lax.broadcasted_iota(jnp.int32, (LANES, samples), 0) == col
    one_hot = jnp.where(in_col, 1.0, 0.0).astype(BF16)
    high, rest = split(intensity)
    low = intensity - high.astype(F32) - rest.astype(F32)
    picked = dot(high, one_hot) + dot(rest, one_hot) + dot(low.astype(BF16), one_hot)
    in_row = lax.broadcasted_iota(jnp.int32, (tile, samples), 0) == row
    own = jnp.sum(jnp.where(in_row, picked, 0.0), axis=0, keepdims=True)
    sampled[...] = jnp.concatenate([own, slopes[...]], axis=1)
    copies[...] = jnp.broadcast_to(sampled[...][None], copies.shape)


def sigmoid(x):
    return 1.0 / (1.0 + jnp.exp(-x))


def errors(intensity, slope, dose):
    resist = 0.5 * jnp.tanh(0.5 * STEEPNESS * (dose * intensity - RESIST_LEVEL))
    offset = resist * slope
    return resist, offset, offset * offset


def source_kernel(weights, doses, pick, gathered, sampled, pixels, placed_sum, tail):
    kernels = weights.shape[0]
    tile = placed_sum.shape[0]
    samples = pixels.shape[1]
    devices = gathered.shape[0]
    corners = doses.shape[0]
    per_corner = devices * samples
    everyone, every_slope = gathered[:, :samples], gathered[:, samples:]
    pick_corner = pick[0] // per_corner
    remain = pick[0] - pick_corner * per_corner
    place = lax.broadcasted_iota(jnp.int32, (devices, samples), 0) * samples
    place = place + lax.broadcasted_iota(jnp.int32, (devices, samples), 1)
    _, _, picked = errors(everyone, every_slope, doses[pick_corner])
    threshold = jnp.sum(jnp.where(place == remain, picked, 0.0), keepdims=True)

    def corner(c, sums):
        _, _, error = errors(everyone, every_slope, doses[c])
        soft = sigmoid((error - threshold) * (1.0 / SOFTNESS))
        return sums[0] + soft, sums[1] + error * soft

    zero = jnp.zeros((devices, samples), F32)
    soft_sum, error_sum = lax.fori_loop(
        0, corners, corner, (zero, zero), unroll=4 if devices <= 32 else 1
    )
    soft_total = jnp.sum(soft_sum, keepdims=True)
    tail_mean = jnp.sum(error_sum, keepdims=True) / soft_total
    tail[...] = tail_mean

    own, slope = sampled[:, :samples], sampled[:, samples:]
    which = lax.broadcasted_iota(jnp.int32, (corners, samples), 0)
    dose = jnp.zeros((corners, samples), F32)
    for c in range(corners):
        dose = jnp.where(which == c, doses[c], dose)
    resist, offset, error = errors(own, slope, dose)
    soft = sigmoid((error - threshold) * (1.0 / SOFTNESS))
    slope_soft = soft * (1.0 - soft) * (1.0 / SOFTNESS)
    chain = 2.0 * STEEPNESS * offset * slope * dose * (0.25 - resist * resist)
    coefficient = (soft + (error - tail_mean) * slope_soft) * (corners * per_corner / soft_total)
    summed = jnp.sum(coefficient * chain, axis=0, keepdims=True)
    summed = summed / total_weight(weights, kernels)

    row, col = sample_places(pixels[...], tile)
    in_row = lax.broadcasted_iota(jnp.int32, (tile, samples), 0) == row
    in_col = lax.broadcasted_iota(jnp.int32, (LANES, samples), 0) == col
    one_hot = jnp.where(in_col, 1.0, 0.0).astype(BF16)
    placed = jnp.where(in_row, summed, 0.0)
    high, rest = split(placed)
    low = (placed - high.astype(F32) - rest.astype(F32)).astype(BF16)
    grid = jnp.zeros((tile, LANES), F32)
    for part in (high, rest, low):
        grid = grid + lax.dot_general(
            part, one_hot, (((1,), (1,)), ((), ())), preferred_element_type=F32
        )

    placed_sum[...] = grid


def gradient_kernel(weights, grid, field_re, field_im, tables, *rest):
    *spec, grad, rim, total_re, total_im = rest
    period = grad.shape[0]
    half = period // 2
    tile = field_re.shape[1]
    radius = (period - tile) // 2
    cols = pair(tables, 0, LANES, 2 * LANES)
    cols = (stacked((cols[0], cols[0])), cols[1])
    rows = tile // 2
    cos_rows = tables[6, :half, : 3 * rows]
    sin_rows = tables[6, half:period, : 3 * rows]

    def along_rows(wide):
        out = []
        for table, x in (
            (cos_rows, wide[:rows] + wide[rows:]),
            (sin_rows, wide[:rows] - wide[rows:]),
        ):
            high, low = split(x)
            out.append(dot(table, stacked((high, low, high))))
        return out

    total_re[...] = jnp.zeros((period, 2 * LANES), F32)
    total_im[...] = jnp.zeros((period, 2 * LANES), F32)

    for group, own in enumerate(spec):
        sources = []
        for i in range(BATCH):
            k = group * BATCH + i
            weighted = grid[...] * weights[k]
            sources += [weighted * field_re[k], weighted * field_im[k]]
        high, low = split(stacked(sources))
        both = dot(jnp.concatenate([high, low], axis=1), cols[0]) + dot(high, cols[1])
        for i in range(BATCH):
            k = group * BATCH + i
            real_cos, real_sin = halves(both[2 * i * tile : (2 * i + 1) * tile])
            imag_cos, imag_sin = halves(both[(2 * i + 1) * tile : (2 * i + 2) * tile])
            wide_re = jnp.concatenate([real_cos + imag_sin, real_cos - imag_sin], axis=1)
            wide_im = jnp.concatenate([imag_cos - real_sin, imag_cos + real_sin], axis=1)
            cos_re, sin_re = along_rows(wide_re)
            cos_im, sin_im = along_rows(wide_im)
            for start, sign in ((0, 1.0), (half, -1.0)):
                part = slice(start, start + half)
                wave_re = cos_re + sign * sin_im
                wave_im = cos_im - sign * sin_re
                own_re, own_im = own[0, i, part], own[1, i, part]
                total_re[part] += own_re * wave_re + own_im * wave_im
                total_im[part] += own_re * wave_im - own_im * wave_re

    pos_re, neg_re = total_re[:half], total_re[half:]
    pos_im, neg_im = total_im[:half], total_im[half:]
    back_rows = pair(tables, 4, period, period)
    back_rows = (back_rows[0], stacked(back_rows))
    for_re = jnp.concatenate([pos_re + neg_re, neg_im - pos_im], axis=0)
    for_im = jnp.concatenate([pos_im + neg_im, pos_re - neg_re], axis=0)
    re_pos, re_neg = halves(dot3_stacked(back_rows, split(for_re)))
    im_pos, im_neg = halves(dot3_stacked(back_rows, split(for_im)))
    last = jnp.concatenate([re_pos + re_neg, im_neg - im_pos], axis=1)
    framed = dot3(split(last), pair(tables, 2, 2 * LANES, period)) * (2.0 / (period * period))
    grad[...] = framed
    lower, _ = place_in_pair("ty")
    rim[...] = jnp.where(lower, framed[:radius], framed[radius + tile :])


VMEM = pl.BlockSpec(memory_space=pltpu.VMEM)
SMEM = pl.BlockSpec(memory_space=pltpu.SMEM)
ANY = pl.BlockSpec(memory_space=pl.ANY)


def shape(*dims):
    return jax.ShapeDtypeStruct(dims, F32)


def call(kernel, name, out_shape, in_specs, scratch=(), micros=1):
    return pl.pallas_call(
        kernel,
        out_shape=out_shape,
        in_specs=in_specs,
        out_specs=[VMEM] * len(out_shape),
        scratch_shapes=scratch,
        compiler_params=pltpu.CompilerParams(vmem_limit_bytes=10 * 1024 * 1024),
        cost_estimate=pl.CostEstimate(
            flops=micros * 10**9, bytes_accessed=2**20, transcendentals=0
        ),
        name=name,
    )


def gather_all(copies):
    return lax.all_to_all(copies, ("ty", "tx"), 0, 0, tiled=True)


def body(latent, kernels, socs_weights, dose_scale, inv_slope, edge_pixels, threshold_pick):
    tile = latent.shape[0]
    count, taps = kernels.shape[1], kernels.shape[-1]
    samples = edge_pixels.shape[1]
    radius = (taps - 1) // 2
    period = tile + 2 * radius
    half = period // 2
    tables = wave_tables(period, tile)
    last_tables = jnp.asarray(tables[[0, 1, 4, 5, 8, 9, 11]])
    tables = jnp.asarray(tables)
    token = shape(8, LANES)
    packed = shape(tile // 2, 2 * radius)
    devices = lax.axis_size("ty") * lax.axis_size("tx")

    spec = []

    def spectra(groups, after):
        *out, done = call(
            functools.partial(spectra_kernel, len(spec) * BATCH, groups),
            "spectra",
            [shape(2, BATCH, period, 2 * LANES)] * groups + [token],
            [VMEM] * 2 + [ANY],
            scratch=[pltpu.VMEM((period, LANES), F32)],
            micros=groups,
        )(kernels, tables, after)
        spec.extend(out)
        return done

    partner, outside = swap("tx", latent), swap_outside("tx", latent)
    transmit, done = call(
        own_kernel, "own", [shape(tile, tile), token], [VMEM], micros=4
    )(latent)
    done = spectra(1, done)
    band, done = call(
        band_kernel, "band", [shape(tile, period), token], [VMEM] * 3 + [ANY]
    )(transmit, partner, outside, done)
    partner = swap("ty", band)
    done = spectra(1, done)
    rim, done = call(
        relay_rows_kernel, "relay", [shape(radius, period), token], [VMEM, ANY]
    )(partner, done)
    rim = ring("ty", rim)
    spectra(count // BATCH - len(spec), done)

    field_re, field_im, sampled, copies = call(
        field_kernel,
        "field",
        [shape(count, tile, LANES)] * 2
        + [shape(1, 2 * samples), shape(devices, 1, 2 * samples)],
        [SMEM] + [VMEM] * (6 + len(spec)),
        scratch=[
            pltpu.VMEM((period, period), F32),
            pltpu.VMEM((4, half, 2 * LANES), F32),
        ],
        micros=7,
    )(socs_weights, band, partner, rim, edge_pixels, inv_slope, tables, *spec)

    gathered = gather_all(copies).reshape(devices, 2 * samples)
    grid, tail_mean = call(
        source_kernel,
        "source",
        [shape(tile, LANES), shape(1, 1)],
        [SMEM] * 3 + [VMEM] * 3,
        micros=2,
    )(socs_weights, dose_scale, threshold_pick, gathered, sampled, edge_pixels)
    grad, rim = call(
        gradient_kernel,
        "gradient",
        [shape(period, period), shape(radius, period)],
        [SMEM] + [VMEM] * (4 + len(spec)),
        scratch=[pltpu.VMEM((period, 2 * LANES), F32)] * 2,
        micros=6,
    )(socs_weights, grid, field_re, field_im, last_tables, *spec)

    rim = ring("ty", rim, back=True)
    (partner,) = call(fold_rows_kernel, "fold", [shape(tile, period)], [VMEM] * 2)(
        grad, rim
    )
    partner = swap("ty", partner)
    band, far = call(
        fold_band_kernel, "fold", [shape(tile, period), packed], [VMEM] * 2
    )(grad, partner)
    far = swap_outside("tx", far)
    (near,) = call(near_rim_kernel, "near", [packed], [VMEM])(band)
    near = swap("tx", near)
    (total,) = call(far_side_kernel, "far", [shape(tile, tile)], [VMEM] * 2)(band, far)
    (steering,) = call(finish_kernel, "finish", [shape(tile, tile)], [VMEM] * 3)(
        total, near, latent
    )
    return (steering, tail_mean.reshape(1))


def solution(mesh):
    placed = (P("ty", "tx"), P(), P(), P(), P("ty", "tx"), P("ty", "tx"), P())
    return jax.shard_map(
        body, mesh=mesh, in_specs=placed, out_specs=(P("ty", "tx"), P()), check_vma=False
    )
```

```python
import functools
import math

import jax
import jax.numpy as jnp
import ml_dtypes
import numpy as np
from jax import lax
from jax.experimental import pallas as pl
from jax.experimental.pallas import tpu as pltpu
from jax.sharding import PartitionSpec as P

STEEPNESS = 4.0
RESIST_LEVEL = 0.7
SOFTNESS = 0.25
LANES = 128
BATCH = 4
F32 = jnp.float32
BF16 = jnp.bfloat16


def split(x):
    high = x.astype(BF16)
    return high, (x - high.astype(F32)).astype(BF16)


def split3(x):
    first = x.astype(BF16)
    rest = x - first.astype(F32)
    second = rest.astype(BF16)
    return first, second, (rest - second.astype(F32)).astype(BF16)


def table_parts(table):
    parts = []
    for _ in range(3):
        parts.append(table.astype(ml_dtypes.bfloat16))
        table = table - parts[-1].astype(np.float64)
    return parts


def dot(a, b):
    return jnp.dot(a, b, preferred_element_type=F32)


def dot3(a, b):
    return dot(a[0], b[0]) + dot(a[0], b[1]) + dot(a[1], b[0])


def stacked(pair):
    return jnp.concatenate(pair, axis=0)


def dot6(a, b):
    small = dot(a[0], b[2]) + dot(a[1], b[1]) + dot(a[2], b[0])
    return small + (dot(a[0], b[1]) + dot(a[1], b[0])) + dot(a[0], b[0])


def dot3_stacked(a, b):
    high, both = a
    count = high.shape[0]
    tall = dot(both, b[0])
    return tall[:count] + tall[count:] + dot(high, b[1])


def waves(period, places):
    turn = (np.arange(period // 2) + 0.5) * (2.0 * math.pi / period)
    angle = turn[:, None] * places[None, :]
    return np.cos(angle), np.sin(angle)


def wave_table(period, places, by_lane=False):
    half = period // 2
    out = np.zeros((2 * LANES, 2 * LANES))
    for first, table in zip((0, LANES if by_lane else half), waves(period, places)):
        out[first : first + half, : len(places)] = table
    return out


def spectra_tables(period, last):
    taps = np.arange(last + 1)
    wide = wave_table(period, taps, True)
    tall = wave_table(period, taps)
    c1, c2, c3 = (part[:, :last].T for part in table_parts(wide))
    lanes = np.stack([np.concatenate(two) for two in ((c1, c1), (c2, c2), (c1, c3))])
    c1, c2, c3 = (part[:period, :last] for part in table_parts(tall))
    rows = [np.concatenate(two, axis=1) for two in ((c1, c1), (c2, c2), (c1, c3))]
    ends = np.zeros((period + 8, 2 * LANES), np.float32)
    ends[:period] = tall[:period, last : last + 1]
    ends[period] = wide[:, last]
    return lanes, np.concatenate(rows), ends


def field_tables(period, tile):
    half, rows = period // 2, tile // 2
    place = np.arange(period)
    wide = table_parts(wave_table(period, place, True))
    centred = table_parts(wave_table(period, place - (tile - 1) / 2))
    out = [part.T for part in wide] + centred + wide
    for table in waves(period, np.arange(rows) + 0.5):
        c1, c2, c3 = table_parts(table.T)
        slot = np.zeros((2 * LANES, 2 * LANES), ml_dtypes.bfloat16)
        for i, two in enumerate(((c1, c1), (c2, c2), (c1, c3))):
            slot[i * rows : (i + 1) * rows, :period] = np.concatenate(two, axis=1)
        out.append(slot)
    return np.stack(out)


def gradient_tables(period, tile):
    half, rows = period // 2, tile // 2
    place = np.arange(period)
    wide = table_parts(wave_table(period, place, True))[:2]
    centred = table_parts(wave_table(period, place - (tile - 1) / 2))[:2]
    slot = np.zeros((2 * LANES, 2 * LANES), ml_dtypes.bfloat16)
    for i, table in enumerate(waves(period, np.arange(rows) + 0.5)):
        high, low, _ = table_parts(table)
        slot[i * half : (i + 1) * half, : 3 * rows] = np.concatenate([high, high, low], axis=1)
    return np.stack([part.T for part in wide] + wide + [part.T for part in centred] + [slot])


def pair(tables, first, rows, cols):
    return tables[first, :rows, :cols], tables[first + 1, :rows, :cols]


def triple(tables, first, rows, cols):
    return [tables[first + i, :rows, :cols] for i in range(3)]


def halves(x):
    return x[:, :LANES], x[:, LANES:]


def place_in_pair(axis):
    index, count = lax.axis_index(axis), lax.axis_size(axis)
    lower = lax.rem(index, 2) == 0
    return lower, jnp.where(lower, index > 0, index < count - 1)


def swap(axis, x):
    return lax.ppermute(x, axis, [(i, i ^ 1) for i in range(lax.axis_size(axis))])


def swap_outside(axis, x):
    count = lax.axis_size(axis)
    pairs = [(0, 0), (count - 1, count - 1)]
    for low in range(1, count - 1, 2):
        pairs += [(low, low + 1), (low + 1, low)]
    return lax.ppermute(x, axis, pairs)


def ring(axis, x, back=False):
    count = lax.axis_size(axis)
    cycle = list(range(0, count, 2)) + list(range(count - 1, 0, -2))
    pairs = list(zip(cycle, cycle[1:] + cycle[:1]))
    return lax.ppermute(x, axis, [(b, a) if back else (a, b) for a, b in pairs])


def spectra_kernel(start, first_out, groups, kern, lanes, rows, ends, *rest):
    out, token = rest[-2:]
    period = out.shape[2]
    half = period // 2
    last = kern.shape[-1] - 1
    end_row = ends[period : period + 1]
    token[...] = jnp.zeros(token.shape, F32)

    def along_lanes(planes):
        main = stacked([plane[:last] for plane in planes])
        tail = stacked([plane[last:] for plane in planes])
        tail = jnp.concatenate([tail, jnp.zeros((-tail.shape[0] % 16, last + 1), F32)], axis=0)
        both = stacked((main, tail))
        x1, x2, x3 = split3(both[:, :last])
        most = jnp.concatenate([x1, x2], axis=1)
        out = dot(jnp.concatenate([x3, x1], axis=1), lanes[2]) + dot(most, lanes[1])
        out = out + dot(most, lanes[0]) + both[:, last:] * end_row
        first = len(planes) * last
        return [
            (out[i * last : (i + 1) * last], out[first + i : first + i + 1])
            for i in range(len(planes))
        ]

    def along_rows(wide, tail):
        x1, x2, x3 = split3(wide)
        tall = dot(rows[: 2 * period], stacked((x1, x2)))
        small = dot(rows[2 * period :], stacked((x3, x1)))
        return tall[:period] + (tall[period:] + small) + ends[:period] * tail

    def mixed(real, imag):
        real_cos, real_sin = halves(real)
        imag_cos, imag_sin = halves(imag)
        return (
            jnp.concatenate([real_cos - imag_sin, real_cos + imag_sin], axis=1),
            jnp.concatenate([real_sin + imag_cos, imag_cos - real_sin], axis=1),
        )

    for group in range(groups):
        first = start + group * BATCH
        planes = along_lanes([kern[c, first + k] for k in range(BATCH) for c in range(2)])
        for k in range(BATCH):
            to = first_out + group * BATCH + k
            (real, real_tail), (imag, imag_tail) = planes[2 * k : 2 * k + 2]
            wide_re, wide_im = mixed(real, imag)
            tail_re, tail_im = mixed(real_tail, imag_tail)
            tall_re = along_rows(wide_re, tail_re)
            tall_im = along_rows(wide_im, tail_im)
            out[0, to, :half] = tall_re[:half] - tall_im[half:]
            out[0, to, half:] = tall_re[:half] + tall_im[half:]
            out[1, to, :half] = tall_im[:half] + tall_re[half:]
            out[1, to, half:] = tall_im[:half] - tall_re[half:]


def pack(x):
    count = x.shape[0] // 2
    return jnp.concatenate([x[:count], x[count:]], axis=1)


def unpack(x):
    width = x.shape[1] // 2
    return jnp.concatenate([x[:, :width], x[:, width:]], axis=0)


def own_kernel(latent, transmit, token):
    transmit[...] = 0.5 * (1.0 + jnp.tanh(latent[...]))
    token[...] = jnp.zeros(token.shape, F32)


def band_kernel(middle, partner, outside, after, band, token):
    tile = middle.shape[0]
    radius = (band.shape[1] - tile) // 2
    lower, other = place_in_pair("tx")

    near = jnp.where(lower, partner[:, :radius], partner[:, tile - radius :])
    far = jnp.where(lower, outside[:, tile - radius :], outside[:, :radius])
    far = jnp.where(other, far, 0.0)
    band[:, :radius] = jnp.where(lower, far, near)
    band[:, radius : radius + tile] = middle[...]
    band[:, radius + tile :] = jnp.where(lower, near, far)
    token[...] = jnp.zeros(token.shape, F32)


def relay_rows_kernel(partner, after, rim, token):
    radius = rim.shape[0]
    tile = partner.shape[0]
    lower, _ = place_in_pair("ty")
    rim[...] = jnp.where(lower, partner[tile - radius :], partner[:radius])
    token[...] = jnp.zeros(token.shape, F32)


def fold_rows_kernel(grad, rim, out):
    radius = rim.shape[0]
    tile = out.shape[0]
    lower, _ = place_in_pair("ty")
    count, index = lax.axis_size("ty"), lax.axis_index("ty")
    comes = jnp.where(lower, index < count - 2, index > 1)
    outer = jnp.where(comes, rim[...], 0.0)
    top = jnp.where(lower, grad[radius + tile :], outer)
    bottom = jnp.where(lower, outer, grad[:radius])
    out[:radius] = top
    out[radius:] = jnp.zeros((tile - radius, out.shape[1]), F32)
    out[tile - radius :] += bottom


def fold_band_kernel(grad, partner, band, far):
    tile = band.shape[0]
    radius = far.shape[1] // 2
    lower, _ = place_in_pair("tx")
    band[...] = grad[radius : radius + tile] + partner[...]
    far[...] = jnp.where(lower, pack(band[:, :radius]), pack(band[:, radius + tile :]))


def near_rim_kernel(band, near):
    tile = band.shape[0]
    radius = near.shape[1] // 2
    lower, _ = place_in_pair("tx")
    near[...] = jnp.where(lower, pack(band[:, radius + tile :]), pack(band[:, :radius]))


def far_side_kernel(band, far, out):
    tile = out.shape[0]
    radius = (band.shape[1] - tile) // 2
    lower, other = place_in_pair("tx")
    outer = jnp.where(other, unpack(far[...]), 0.0)
    out[...] = band[:, radius : radius + tile]
    out[:, :radius] += jnp.where(lower, outer, 0.0)
    out[:, tile - radius :] += jnp.where(lower, 0.0, outer)


def finish_kernel(total, near, latent, steering):
    tile = latent.shape[0]
    radius = near.shape[1] // 2
    lower, _ = place_in_pair("tx")
    inner = unpack(near[...])
    steering[...] = total[...]
    steering[:, :radius] += jnp.where(lower, 0.0, inner)
    steering[:, tile - radius :] += jnp.where(lower, inner, 0.0)
    value = jnp.tanh(latent[...])
    steering[...] = steering[...] * 0.5 * (1.0 - value * value)


def total_weight(weights, kernels):
    total = weights[0]
    for k in range(1, kernels):
        total = total + weights[k]
    return jnp.full((1, 1), total, F32)


def sample_places(pixels, tile):
    row = ((pixels.astype(F32) + 0.5) * (1.0 / tile)).astype(jnp.int32)
    held = jnp.where(row < tile // 2, tile - 1 - row, row - tile // 2)
    return held, pixels - row * tile


def field_kernel(weights, band, partner, rim, pixels, slopes, tables, *rest):
    *spec, field_re, field_im, sampled, copies, framed, mask = rest
    kernels = weights.shape[0]
    period = band.shape[1]
    half = period // 2
    tile = field_re.shape[1]
    radius = rim.shape[0]
    lower, other = place_in_pair("ty")
    outer = jnp.where(other, rim[...], 0.0)
    framed[:radius] = jnp.where(lower, outer, partner[tile - radius :])
    framed[radius + tile :] = jnp.where(lower, partner[:radius], outer)
    framed[radius : radius + tile] = band[...]
    wide = dot6(split3(framed[...]), triple(tables, 0, period, 2 * LANES))
    tall = dot6(triple(tables, 3, period, period), split3(wide)) * (1.0 / (period * period))
    cos_cos, cos_sin = halves(tall[:half])
    sin_cos, sin_sin = halves(tall[half:])
    same, other = cos_cos - sin_sin, cos_cos + sin_sin
    joint, cross = sin_cos + cos_sin, sin_cos - cos_sin
    mask[0, :, :LANES], mask[0, :, LANES:] = same, other
    mask[1, :, :LANES], mask[1, :, LANES:] = -joint, -cross
    mask[2, :, :LANES], mask[2, :, LANES:] = other, same
    mask[3, :, :LANES], mask[3, :, LANES:] = cross, joint
    rows = tile // 2

    def lift(slot, x):
        x1, x2, x3 = split3(x)
        out = dot(tables[slot, :tile, :period], stacked((x1, x2)))
        small = dot(tables[slot, tile : tile + rows, :period], stacked((x3, x1)))
        return out[:rows] + (out[rows:] + small)

    across = triple(tables, 6, 2 * LANES, LANES)
    across = (across[0], jnp.concatenate(across[:2], axis=1), across[2])

    def lifted(own, k):
        pos_re, pos_im = own[0, k, :half], own[1, k, :half]
        neg_re, neg_im = own[0, k, half:], own[1, k, half:]
        up_re = mask[0] * pos_re - mask[1] * pos_im
        up_im = mask[0] * pos_im + mask[1] * pos_re
        down_re = mask[2] * neg_re - mask[3] * neg_im
        down_im = mask[2] * neg_im + mask[3] * neg_re
        even_re = lift(9, up_re + down_re)
        even_im = lift(9, up_im + down_im)
        odd_re = lift(10, up_im - down_im)
        odd_im = lift(10, up_re - down_re)
        re_pos, re_neg = halves(stacked((even_re - odd_re, even_re + odd_re)))
        im_pos, im_neg = halves(stacked((even_im + odd_im, even_im - odd_im)))
        rows_re = jnp.concatenate([re_pos + re_neg, im_neg - im_pos], axis=1)
        rows_im = jnp.concatenate([im_pos + im_neg, re_pos - re_neg], axis=1)
        return [rows_re, rows_im]

    intensity = jnp.zeros((tile, LANES), F32)
    places = [(own, k) for own in spec for k in range(own.shape[1])]
    for first in range(0, kernels, BATCH):
        lines = stacked([line for i in range(BATCH) for line in lifted(*places[first + i])])
        x1, x2, x3 = split3(lines)
        most, more = halves(dot(x1, across[1]))
        some, small = halves(dot(x2, across[1]))
        both = small + dot(x1, across[2]) + dot(x3, across[0]) + (more + some) + most
        for i in range(BATCH):
            real = both[2 * i * tile : (2 * i + 1) * tile]
            imag = both[(2 * i + 1) * tile : (2 * i + 2) * tile]
            field_re[first + i] = real
            field_im[first + i] = imag
            intensity = intensity + weights[first + i] * (real * real + imag * imag)
    intensity = intensity / total_weight(weights, kernels)
    samples = pixels.shape[1]
    row, col = sample_places(pixels[...], tile)
    in_col = lax.broadcasted_iota(jnp.int32, (LANES, samples), 0) == col
    one_hot = jnp.where(in_col, 1.0, 0.0).astype(BF16)
    high, rest = split(intensity)
    low = intensity - high.astype(F32) - rest.astype(F32)
    picked = dot(high, one_hot) + dot(rest, one_hot) + dot(low.astype(BF16), one_hot)
    in_row = lax.broadcasted_iota(jnp.int32, (tile, samples), 0) == row
    own = jnp.sum(jnp.where(in_row, picked, 0.0), axis=0, keepdims=True)
    sampled[...] = jnp.concatenate([own, slopes[...]], axis=1)
    copies[...] = jnp.broadcast_to(sampled[...][None], copies.shape)


def sigmoid(x):
    return 1.0 / (1.0 + jnp.exp(-x))


def errors(intensity, slope, dose):
    resist = 0.5 * jnp.tanh(0.5 * STEEPNESS * (dose * intensity - RESIST_LEVEL))
    offset = resist * slope
    return resist, offset, offset * offset


def source_kernel(weights, doses, pick, gathered, sampled, pixels, placed_sum, tail):
    kernels = weights.shape[0]
    tile = placed_sum.shape[0]
    samples = pixels.shape[1]
    devices = gathered.shape[0]
    corners = doses.shape[0]
    per_corner = devices * samples
    everyone, every_slope = gathered[:, :samples], gathered[:, samples:]
    pick_corner = pick[0] // per_corner
    remain = pick[0] - pick_corner * per_corner
    place = lax.broadcasted_iota(jnp.int32, (devices, samples), 0) * samples
    place = place + lax.broadcasted_iota(jnp.int32, (devices, samples), 1)
    _, _, picked = errors(everyone, every_slope, doses[pick_corner])
    threshold = jnp.sum(jnp.where(place == remain, picked, 0.0), keepdims=True)

    def corner(c, sums):
        _, _, error = errors(everyone, every_slope, doses[c])
        soft = sigmoid((error - threshold) * (1.0 / SOFTNESS))
        return sums[0] + soft, sums[1] + error * soft

    zero = jnp.zeros((devices, samples), F32)
    soft_sum, error_sum = lax.fori_loop(
        0, corners, corner, (zero, zero), unroll=8 if devices <= 32 else 1
    )
    soft_total = jnp.sum(soft_sum, keepdims=True)
    tail_mean = jnp.sum(error_sum, keepdims=True) / soft_total
    tail[...] = tail_mean

    own, slope = sampled[:, :samples], sampled[:, samples:]
    which = lax.broadcasted_iota(jnp.int32, (corners, samples), 0)
    dose = jnp.zeros((corners, samples), F32)
    for c in range(corners):
        dose = jnp.where(which == c, doses[c], dose)
    resist, offset, error = errors(own, slope, dose)
    soft = sigmoid((error - threshold) * (1.0 / SOFTNESS))
    slope_soft = soft * (1.0 - soft) * (1.0 / SOFTNESS)
    chain = 2.0 * STEEPNESS * offset * slope * dose * (0.25 - resist * resist)
    coefficient = (soft + (error - tail_mean) * slope_soft) * (corners * per_corner / soft_total)
    summed = jnp.sum(coefficient * chain, axis=0, keepdims=True)
    summed = summed / total_weight(weights, kernels)

    row, col = sample_places(pixels[...], tile)
    in_row = lax.broadcasted_iota(jnp.int32, (tile, samples), 0) == row
    in_col = lax.broadcasted_iota(jnp.int32, (LANES, samples), 0) == col
    one_hot = jnp.where(in_col, 1.0, 0.0).astype(BF16)
    placed = jnp.where(in_row, summed, 0.0)
    high, rest = split(placed)
    low = (placed - high.astype(F32) - rest.astype(F32)).astype(BF16)
    grid = jnp.zeros((tile, LANES), F32)
    for part in (high, rest, low):
        grid = grid + lax.dot_general(
            part, one_hot, (((1,), (1,)), ((), ())), preferred_element_type=F32
        )

    placed_sum[...] = grid


def gradient_kernel(weights, grid, field_re, field_im, tables, *rest):
    *spec, grad, rim, total_re, total_im = rest
    period = grad.shape[0]
    half = period // 2
    tile = field_re.shape[1]
    radius = (period - tile) // 2
    cols = pair(tables, 0, LANES, 2 * LANES)
    cols = (stacked((cols[0], cols[0])), cols[1])
    rows = tile // 2
    cos_rows = tables[6, :half, : 3 * rows]
    sin_rows = tables[6, half:period, : 3 * rows]

    def along_rows(wide):
        out = []
        for table, x in (
            (cos_rows, wide[:rows] + wide[rows:]),
            (sin_rows, wide[:rows] - wide[rows:]),
        ):
            high, low = split(x)
            out.append(dot(table, stacked((high, low, high))))
        return out

    total_re[...] = jnp.zeros((period, 2 * LANES), F32)
    total_im[...] = jnp.zeros((period, 2 * LANES), F32)

    places = [(own, k) for own in spec for k in range(own.shape[1])]
    for group in range(len(places) // BATCH):
        sources = []
        for i in range(BATCH):
            k = group * BATCH + i
            weighted = grid[...] * weights[k]
            sources += [weighted * field_re[k], weighted * field_im[k]]
        high, low = split(stacked(sources))
        both = dot(jnp.concatenate([high, low], axis=1), cols[0]) + dot(high, cols[1])
        for i in range(BATCH):
            own, at = places[group * BATCH + i]
            real_cos, real_sin = halves(both[2 * i * tile : (2 * i + 1) * tile])
            imag_cos, imag_sin = halves(both[(2 * i + 1) * tile : (2 * i + 2) * tile])
            wide_re = jnp.concatenate([real_cos + imag_sin, real_cos - imag_sin], axis=1)
            wide_im = jnp.concatenate([imag_cos - real_sin, imag_cos + real_sin], axis=1)
            cos_re, sin_re = along_rows(wide_re)
            cos_im, sin_im = along_rows(wide_im)
            for start, sign in ((0, 1.0), (half, -1.0)):
                part = slice(start, start + half)
                wave_re = cos_re + sign * sin_im
                wave_im = cos_im - sign * sin_re
                own_re, own_im = own[0, at, part], own[1, at, part]
                total_re[part] += own_re * wave_re + own_im * wave_im
                total_im[part] += own_re * wave_im - own_im * wave_re

    pos_re, neg_re = total_re[:half], total_re[half:]
    pos_im, neg_im = total_im[:half], total_im[half:]
    back_rows = pair(tables, 4, period, period)
    back_rows = (back_rows[0], stacked(back_rows))
    for_re = jnp.concatenate([pos_re + neg_re, neg_im - pos_im], axis=0)
    for_im = jnp.concatenate([pos_im + neg_im, pos_re - neg_re], axis=0)
    re_pos, re_neg = halves(dot3_stacked(back_rows, split(for_re)))
    im_pos, im_neg = halves(dot3_stacked(back_rows, split(for_im)))
    last = jnp.concatenate([re_pos + re_neg, im_neg - im_pos], axis=1)
    framed = dot3(split(last), pair(tables, 2, 2 * LANES, period)) * (2.0 / (period * period))
    grad[...] = framed
    lower, _ = place_in_pair("ty")
    rim[...] = jnp.where(lower, framed[:radius], framed[radius + tile :])


VMEM = pl.BlockSpec(memory_space=pltpu.VMEM)
SMEM = pl.BlockSpec(memory_space=pltpu.SMEM)
ANY = pl.BlockSpec(memory_space=pl.ANY)


def shape(*dims):
    return jax.ShapeDtypeStruct(dims, F32)


def call(kernel, name, out_shape, in_specs, scratch=(), aliases=None, micros=1):
    return pl.pallas_call(
        kernel,
        out_shape=out_shape,
        in_specs=in_specs,
        out_specs=[VMEM] * len(out_shape),
        scratch_shapes=scratch,
        input_output_aliases=aliases or {},
        compiler_params=pltpu.CompilerParams(vmem_limit_bytes=10 * 1024 * 1024),
        cost_estimate=pl.CostEstimate(
            flops=micros * 10**9, bytes_accessed=2**20, transcendentals=0
        ),
        name=name,
    )


def gather_all(copies):
    return lax.all_to_all(copies, ("ty", "tx"), 0, 0, tiled=True)


def body(latent, kernels, socs_weights, dose_scale, inv_slope, edge_pixels, threshold_pick):
    tile = latent.shape[0]
    count, taps = kernels.shape[1], kernels.shape[-1]
    samples = edge_pixels.shape[1]
    radius = (taps - 1) // 2
    period = tile + 2 * radius
    half = period // 2
    first_tables = [jnp.asarray(x) for x in spectra_tables(period, taps - 1)]
    tables = jnp.asarray(field_tables(period, tile))
    last_tables = jnp.asarray(gradient_tables(period, tile))
    token = shape(8, LANES)
    packed = shape(tile // 2, 2 * radius)
    devices = lax.axis_size("ty") * lax.axis_size("tx")

    def spectra(start, first_out, groups, size, after, into=()):
        return call(
            functools.partial(spectra_kernel, start, first_out, groups),
            "spectra",
            [shape(2, size, period, 2 * LANES), token],
            [VMEM] * 4 + [ANY] * (1 + len(into)),
            aliases={5: 0} if into else None,
            micros=groups,
        )(kernels, *first_tables, after, *into)

    transmit, done = call(
        own_kernel, "own", [shape(tile, tile), token], [VMEM], micros=3
    )(latent)
    partner, outside = swap("tx", transmit), swap_outside("tx", transmit)
    small, large = BATCH, count - BATCH
    spec_a, done = spectra(0, 0, 1, small, done)
    band, done = call(
        band_kernel, "band", [shape(tile, period), token], [VMEM] * 3 + [ANY]
    )(transmit, partner, outside, done)
    partner = swap("ty", band)
    spec_b, done = spectra(small, 0, 1, large, done)
    rim, done = call(
        relay_rows_kernel, "relay", [shape(radius, period), token], [VMEM, ANY]
    )(partner, done)
    rim = ring("ty", rim)
    groups = large // BATCH - 1
    spec_b, _ = spectra(2 * small, small, groups, large, done, (spec_b,))
    spec = [spec_a, spec_b]

    field_re, field_im, sampled, copies = call(
        field_kernel,
        "field",
        [shape(count, tile, LANES)] * 2
        + [shape(1, 2 * samples), shape(devices, 1, 2 * samples)],
        [SMEM] + [VMEM] * (6 + len(spec)),
        scratch=[
            pltpu.VMEM((period, period), F32),
            pltpu.VMEM((4, half, 2 * LANES), F32),
        ],
        micros=7,
    )(socs_weights, band, partner, rim, edge_pixels, inv_slope, tables, *spec)

    gathered = gather_all(copies).reshape(devices, 2 * samples)
    grid, tail_mean = call(
        source_kernel,
        "source",
        [shape(tile, LANES), shape(1, 1)],
        [SMEM] * 3 + [VMEM] * 3,
        micros=2,
    )(socs_weights, dose_scale, threshold_pick, gathered, sampled, edge_pixels)
    grad, rim = call(
        gradient_kernel,
        "gradient",
        [shape(period, period), shape(radius, period)],
        [SMEM] + [VMEM] * (4 + len(spec)),
        scratch=[pltpu.VMEM((period, 2 * LANES), F32)] * 2,
        micros=6,
    )(socs_weights, grid, field_re, field_im, last_tables, *spec)

    rim = ring("ty", rim, back=True)
    (partner,) = call(fold_rows_kernel, "fold", [shape(tile, period)], [VMEM] * 2)(
        grad, rim
    )
    partner = swap("ty", partner)
    band, far = call(
        fold_band_kernel, "fold", [shape(tile, period), packed], [VMEM] * 2
    )(grad, partner)
    far = swap_outside("tx", far)
    (near,) = call(near_rim_kernel, "near", [packed], [VMEM])(band)
    near = swap("tx", near)
    (total,) = call(far_side_kernel, "far", [shape(tile, tile)], [VMEM] * 2)(band, far)
    (steering,) = call(finish_kernel, "finish", [shape(tile, tile)], [VMEM] * 3)(
        total, near, latent
    )
    return (steering, tail_mean.reshape(1))


def solution(mesh):
    placed = (P("ty", "tx"), P(), P(), P(), P("ty", "tx"), P("ty", "tx"), P())
    return jax.shard_map(
        body, mesh=mesh, in_specs=placed, out_specs=(P("ty", "tx"), P()), check_vma=False
    )
```

```python
import functools
import math

import jax
import jax.numpy as jnp
import ml_dtypes
import numpy as np
from jax import lax
from jax.experimental import pallas as pl
from jax.experimental.pallas import tpu as pltpu
from jax.sharding import PartitionSpec as P

STEEPNESS = 4.0
RESIST_LEVEL = 0.7
SOFTNESS = 0.25
LANES = 128
BATCH = 4
F32 = jnp.float32
BF16 = jnp.bfloat16


def split(x):
    high = x.astype(BF16)
    return high, (x - high.astype(F32)).astype(BF16)


def split3(x):
    first = x.astype(BF16)
    rest = x - first.astype(F32)
    second = rest.astype(BF16)
    return first, second, (rest - second.astype(F32)).astype(BF16)


def table_parts(table):
    parts = []
    for _ in range(3):
        parts.append(table.astype(ml_dtypes.bfloat16))
        table = table - parts[-1].astype(np.float64)
    return parts


def dot(a, b):
    return jnp.dot(a, b, preferred_element_type=F32)


def dot3(a, b):
    return dot(a[0], b[0]) + dot(a[0], b[1]) + dot(a[1], b[0])


def stacked(pair):
    return jnp.concatenate(pair, axis=0)


def dot6(a, b):
    small = dot(a[0], b[2]) + dot(a[1], b[1]) + dot(a[2], b[0])
    return small + (dot(a[0], b[1]) + dot(a[1], b[0])) + dot(a[0], b[0])


def dot3_stacked(a, b):
    high, both = a
    count = high.shape[0]
    tall = dot(both, b[0])
    return tall[:count] + tall[count:] + dot(high, b[1])


def waves(period, places):
    turn = (np.arange(period // 2) + 0.5) * (2.0 * math.pi / period)
    angle = turn[:, None] * places[None, :]
    return np.cos(angle), np.sin(angle)


def wave_table(period, places, by_lane=False):
    half = period // 2
    out = np.zeros((2 * LANES, 2 * LANES))
    for first, table in zip((0, LANES if by_lane else half), waves(period, places)):
        out[first : first + half, : len(places)] = table
    return out


def spectra_tables(period, last):
    taps = np.arange(last + 1)
    wide = wave_table(period, taps, True)
    tall = wave_table(period, taps)
    c1, c2, c3 = (part[:, :last].T for part in table_parts(wide))
    lanes = np.stack([np.concatenate(two) for two in ((c1, c1), (c2, c2), (c1, c3))])
    c1, c2, c3 = (part[:period, :last] for part in table_parts(tall))
    rows = [np.concatenate(two, axis=1) for two in ((c1, c1), (c2, c2), (c1, c3))]
    ends = np.zeros((period + 8, 2 * LANES), np.float32)
    ends[:period] = tall[:period, last : last + 1]
    ends[period] = wide[:, last]
    return lanes, np.concatenate(rows), ends


def field_tables(period, tile):
    half, rows = period // 2, tile // 2
    place = np.arange(period)
    wide = table_parts(wave_table(period, place, True))
    centred = table_parts(wave_table(period, place - (tile - 1) / 2))
    out = [part.T for part in wide] + centred + wide
    for table in waves(period, np.arange(rows) + 0.5):
        c1, c2, c3 = table_parts(table.T)
        slot = np.zeros((2 * LANES, 2 * LANES), ml_dtypes.bfloat16)
        for i, two in enumerate(((c1, c1), (c2, c2), (c3, 0 * c3), (c1, 0 * c1))):
            slot[i * rows : (i + 1) * rows, :period] = np.concatenate(two, axis=1)
        out.append(slot)
    return np.stack(out)


def gradient_tables(period, tile):
    half, rows = period // 2, tile // 2
    place = np.arange(period)
    wide = table_parts(wave_table(period, place, True))[:2]
    centred = table_parts(wave_table(period, place - (tile - 1) / 2))[:2]
    slot = np.zeros((2 * LANES, 2 * LANES), ml_dtypes.bfloat16)
    for i, table in enumerate(waves(period, np.arange(rows) + 0.5)):
        high, low, _ = table_parts(table)
        slot[i * half : (i + 1) * half, : 3 * rows] = np.concatenate([high, high, low], axis=1)
    return np.stack([part.T for part in wide] + wide + [part.T for part in centred] + [slot])


def pair(tables, first, rows, cols):
    return tables[first, :rows, :cols], tables[first + 1, :rows, :cols]


def triple(tables, first, rows, cols):
    return [tables[first + i, :rows, :cols] for i in range(3)]


def halves(x):
    return x[:, :LANES], x[:, LANES:]


def place_in_pair(axis):
    index, count = lax.axis_index(axis), lax.axis_size(axis)
    lower = lax.rem(index, 2) == 0
    return lower, jnp.where(lower, index > 0, index < count - 1)


def swap(axis, x):
    return lax.ppermute(x, axis, [(i, i ^ 1) for i in range(lax.axis_size(axis))])


def swap_outside(axis, x):
    count = lax.axis_size(axis)
    pairs = [(0, 0), (count - 1, count - 1)]
    for low in range(1, count - 1, 2):
        pairs += [(low, low + 1), (low + 1, low)]
    return lax.ppermute(x, axis, pairs)


def ring(axis, x, back=False):
    count = lax.axis_size(axis)
    cycle = list(range(0, count, 2)) + list(range(count - 1, 0, -2))
    pairs = list(zip(cycle, cycle[1:] + cycle[:1]))
    return lax.ppermute(x, axis, [(b, a) if back else (a, b) for a, b in pairs])


def spectra_kernel(start, first_out, parts, kern, lanes, rows, ends, *rest):
    out, token = rest[-2:]
    period = out.shape[2]
    half = period // 2
    last = kern.shape[-1] - 1
    end_row = ends[period : period + 1]
    token[...] = jnp.zeros(token.shape, F32)

    def along_lanes(planes):
        main = stacked([plane[:last] for plane in planes])
        tail = stacked([plane[last:] for plane in planes])
        tail = jnp.concatenate([tail, jnp.zeros((-tail.shape[0] % 16, last + 1), F32)], axis=0)
        both = stacked((main, tail))
        x1, x2, x3 = split3(both[:, :last])
        most = jnp.concatenate([x1, x2], axis=1)
        out = dot(jnp.concatenate([x3, x1], axis=1), lanes[2]) + dot(most, lanes[1])
        out = out + dot(most, lanes[0]) + both[:, last:] * end_row
        first = len(planes) * last
        return [
            (out[i * last : (i + 1) * last], out[first + i : first + i + 1])
            for i in range(len(planes))
        ]

    def along_rows(wide, tail):
        x1, x2, x3 = split3(wide)
        tall = dot(rows[: 2 * period], stacked((x1, x2)))
        small = dot(rows[2 * period :], stacked((x3, x1)))
        return tall[:period] + (tall[period:] + small) + ends[:period] * tail

    def mixed(real, imag):
        real_cos, real_sin = halves(real)
        imag_cos, imag_sin = halves(imag)
        return (
            jnp.concatenate([real_cos - imag_sin, real_cos + imag_sin], axis=1),
            jnp.concatenate([real_sin + imag_cos, imag_cos - real_sin], axis=1),
        )

    planes = along_lanes([kern[c, start + k] for k in range(parts) for c in range(2)])
    for k in range(parts):
        to = first_out + k
        (real, real_tail), (imag, imag_tail) = planes[2 * k : 2 * k + 2]
        wide_re, wide_im = mixed(real, imag)
        tail_re, tail_im = mixed(real_tail, imag_tail)
        tall_re = along_rows(wide_re, tail_re)
        tall_im = along_rows(wide_im, tail_im)
        out[0, to, :half] = tall_re[:half] - tall_im[half:]
        out[0, to, half:] = tall_re[:half] + tall_im[half:]
        out[1, to, :half] = tall_im[:half] + tall_re[half:]
        out[1, to, half:] = tall_im[:half] - tall_re[half:]


def pack(x):
    count = x.shape[0] // 2
    return jnp.concatenate([x[:count], x[count:]], axis=1)


def unpack(x):
    width = x.shape[1] // 2
    return jnp.concatenate([x[:, :width], x[:, width:]], axis=0)


def own_kernel(latent, transmit, token):
    transmit[...] = 0.5 * (1.0 + jnp.tanh(latent[...]))
    token[...] = jnp.zeros(token.shape, F32)


def band_kernel(middle, partner, outside, after, band, token):
    tile = middle.shape[0]
    radius = (band.shape[1] - tile) // 2
    lower, other = place_in_pair("tx")

    near = jnp.where(lower, partner[:, :radius], partner[:, tile - radius :])
    far = jnp.where(lower, outside[:, tile - radius :], outside[:, :radius])
    far = jnp.where(other, far, 0.0)
    band[:, :radius] = jnp.where(lower, far, near)
    band[:, radius : radius + tile] = middle[...]
    band[:, radius + tile :] = jnp.where(lower, near, far)
    token[...] = jnp.zeros(token.shape, F32)


def relay_rows_kernel(partner, after, rim, token):
    radius = rim.shape[0]
    tile = partner.shape[0]
    lower, _ = place_in_pair("ty")
    rim[...] = jnp.where(lower, partner[tile - radius :], partner[:radius])
    token[...] = jnp.zeros(token.shape, F32)


def fold_rows_kernel(grad, rim, out):
    radius = rim.shape[0]
    tile = out.shape[0]
    lower, _ = place_in_pair("ty")
    count, index = lax.axis_size("ty"), lax.axis_index("ty")
    comes = jnp.where(lower, index < count - 2, index > 1)
    outer = jnp.where(comes, rim[...], 0.0)
    top = jnp.where(lower, grad[radius + tile :], outer)
    bottom = jnp.where(lower, outer, grad[:radius])
    out[:radius] = top
    out[radius:] = jnp.zeros((tile - radius, out.shape[1]), F32)
    out[tile - radius :] += bottom


def fold_band_kernel(grad, partner, band, far):
    tile = band.shape[0]
    radius = far.shape[1] // 2
    lower, _ = place_in_pair("tx")
    band[...] = grad[radius : radius + tile] + partner[...]
    far[...] = jnp.where(lower, pack(band[:, :radius]), pack(band[:, radius + tile :]))


def near_rim_kernel(band, near):
    tile = band.shape[0]
    radius = near.shape[1] // 2
    lower, _ = place_in_pair("tx")
    near[...] = jnp.where(lower, pack(band[:, radius + tile :]), pack(band[:, :radius]))


def far_side_kernel(band, far, out):
    tile = out.shape[0]
    radius = (band.shape[1] - tile) // 2
    lower, other = place_in_pair("tx")
    outer = jnp.where(other, unpack(far[...]), 0.0)
    out[...] = band[:, radius : radius + tile]
    out[:, :radius] += jnp.where(lower, outer, 0.0)
    out[:, tile - radius :] += jnp.where(lower, 0.0, outer)


def finish_kernel(total, near, latent, steering):
    tile = latent.shape[0]
    radius = near.shape[1] // 2
    lower, _ = place_in_pair("tx")
    inner = unpack(near[...])
    steering[...] = total[...]
    steering[:, :radius] += jnp.where(lower, 0.0, inner)
    steering[:, tile - radius :] += jnp.where(lower, inner, 0.0)
    value = jnp.tanh(latent[...])
    steering[...] = steering[...] * 0.5 * (1.0 - value * value)


def total_weight(weights, kernels):
    total = weights[0]
    for k in range(1, kernels):
        total = total + weights[k]
    return jnp.full((1, 1), total, F32)


def sample_places(pixels, tile):
    row = ((pixels.astype(F32) + 0.5) * (1.0 / tile)).astype(jnp.int32)
    held = jnp.where(row < tile // 2, tile - 1 - row, row - tile // 2)
    return held, pixels - row * tile


def field_kernel(weights, band, partner, rim, pixels, slopes, tables, *rest):
    *spec, field_re, field_im, sampled, copies, framed, mask = rest
    kernels = weights.shape[0]
    period = band.shape[1]
    half = period // 2
    tile = field_re.shape[1]
    radius = rim.shape[0]
    lower, other = place_in_pair("ty")
    outer = jnp.where(other, rim[...], 0.0)
    framed[:radius] = jnp.where(lower, outer, partner[tile - radius :])
    framed[radius + tile :] = jnp.where(lower, partner[:radius], outer)
    framed[radius : radius + tile] = band[...]
    wide = dot6(split3(framed[...]), triple(tables, 0, period, 2 * LANES))
    tall = dot6(triple(tables, 3, period, period), split3(wide)) * (1.0 / (period * period))
    cos_cos, cos_sin = halves(tall[:half])
    sin_cos, sin_sin = halves(tall[half:])
    same, other = cos_cos - sin_sin, cos_cos + sin_sin
    joint, cross = sin_cos + cos_sin, sin_cos - cos_sin
    mask[0, :, :LANES], mask[0, :, LANES:] = same, other
    mask[1, :, :LANES], mask[1, :, LANES:] = -joint, -cross
    mask[2, :, :LANES], mask[2, :, LANES:] = other, same
    mask[3, :, :LANES], mask[3, :, LANES:] = cross, joint
    rows = tile // 2

    def lift(slot, x):
        x1, x2, x3 = split3(x)
        out = dot(tables[slot, : 3 * rows, :period], stacked((x1, x2)))
        small = dot(tables[slot, 3 * rows : 4 * rows, :half], x3)
        return out[:rows] + (out[rows:tile] + (out[tile:] + small))

    across = triple(tables, 6, 2 * LANES, LANES)
    across = (across[0], jnp.concatenate(across[:2], axis=1), across[2])

    def lifted(own, k):
        pos_re, pos_im = own[0, k, :half], own[1, k, :half]
        neg_re, neg_im = own[0, k, half:], own[1, k, half:]
        up_re = mask[0] * pos_re - mask[1] * pos_im
        up_im = mask[0] * pos_im + mask[1] * pos_re
        down_re = mask[2] * neg_re - mask[3] * neg_im
        down_im = mask[2] * neg_im + mask[3] * neg_re
        even_re = lift(9, up_re + down_re)
        even_im = lift(9, up_im + down_im)
        odd_re = lift(10, up_im - down_im)
        odd_im = lift(10, up_re - down_re)
        re_pos, re_neg = halves(stacked((even_re - odd_re, even_re + odd_re)))
        im_pos, im_neg = halves(stacked((even_im + odd_im, even_im - odd_im)))
        rows_re = jnp.concatenate([re_pos + re_neg, im_neg - im_pos], axis=1)
        rows_im = jnp.concatenate([im_pos + im_neg, re_pos - re_neg], axis=1)
        return [rows_re, rows_im]

    intensity = jnp.zeros((tile, LANES), F32)
    places = [(own, k) for own in spec for k in range(own.shape[1])]
    for first in range(0, kernels, BATCH):
        lines = stacked([line for i in range(BATCH) for line in lifted(*places[first + i])])
        x1, x2, x3 = split3(lines)
        most, more = halves(dot(x1, across[1]))
        some, small = halves(dot(x2, across[1]))
        both = small + dot(x1, across[2]) + dot(x3, across[0]) + (more + some) + most
        for i in range(BATCH):
            real = both[2 * i * tile : (2 * i + 1) * tile]
            imag = both[(2 * i + 1) * tile : (2 * i + 2) * tile]
            field_re[first + i] = real
            field_im[first + i] = imag
            intensity = intensity + weights[first + i] * (real * real + imag * imag)
    intensity = intensity / total_weight(weights, kernels)
    samples = pixels.shape[1]
    row, col = sample_places(pixels[...], tile)
    in_col = lax.broadcasted_iota(jnp.int32, (LANES, samples), 0) == col
    one_hot = jnp.where(in_col, 1.0, 0.0).astype(BF16)
    high, rest = split(intensity)
    low = intensity - high.astype(F32) - rest.astype(F32)
    picked = dot(high, one_hot) + dot(rest, one_hot) + dot(low.astype(BF16), one_hot)
    in_row = lax.broadcasted_iota(jnp.int32, (tile, samples), 0) == row
    own = jnp.sum(jnp.where(in_row, picked, 0.0), axis=0, keepdims=True)
    sampled[...] = jnp.concatenate([own, slopes[...]], axis=1)
    copies[...] = jnp.broadcast_to(sampled[...][None], copies.shape)


def sigmoid(x):
    return 1.0 / (1.0 + jnp.exp(-x))


def errors(intensity, slope, dose):
    resist = 0.5 * jnp.tanh(0.5 * STEEPNESS * (dose * intensity - RESIST_LEVEL))
    offset = resist * slope
    return resist, offset, offset * offset


def source_kernel(weights, doses, pick, gathered, sampled, pixels, placed_sum, tail):
    kernels = weights.shape[0]
    tile = placed_sum.shape[0]
    samples = pixels.shape[1]
    devices = gathered.shape[0]
    corners = doses.shape[0]
    per_corner = devices * samples
    everyone, every_slope = gathered[:, :samples], gathered[:, samples:]
    pick_corner = pick[0] // per_corner
    remain = pick[0] - pick_corner * per_corner
    place = lax.broadcasted_iota(jnp.int32, (devices, samples), 0) * samples
    place = place + lax.broadcasted_iota(jnp.int32, (devices, samples), 1)
    _, _, picked = errors(everyone, every_slope, doses[pick_corner])
    threshold = jnp.sum(jnp.where(place == remain, picked, 0.0), keepdims=True)

    def corner(c, sums):
        _, _, error = errors(everyone, every_slope, doses[c])
        soft = sigmoid((error - threshold) * (1.0 / SOFTNESS))
        return sums[0] + soft, sums[1] + error * soft

    zero = jnp.zeros((devices, samples), F32)
    soft_sum, error_sum = lax.fori_loop(
        0, corners, corner, (zero, zero), unroll=8 if devices <= 32 else 1
    )
    soft_total = jnp.sum(soft_sum, keepdims=True)
    tail_mean = jnp.sum(error_sum, keepdims=True) / soft_total
    tail[...] = tail_mean

    own, slope = sampled[:, :samples], sampled[:, samples:]
    which = lax.broadcasted_iota(jnp.int32, (corners, samples), 0)
    dose = jnp.zeros((corners, samples), F32)
    for c in range(corners):
        dose = jnp.where(which == c, doses[c], dose)
    resist, offset, error = errors(own, slope, dose)
    soft = sigmoid((error - threshold) * (1.0 / SOFTNESS))
    slope_soft = soft * (1.0 - soft) * (1.0 / SOFTNESS)
    chain = 2.0 * STEEPNESS * offset * slope * dose * (0.25 - resist * resist)
    coefficient = (soft + (error - tail_mean) * slope_soft) * (corners * per_corner / soft_total)
    summed = jnp.sum(coefficient * chain, axis=0, keepdims=True)
    summed = summed / total_weight(weights, kernels)

    row, col = sample_places(pixels[...], tile)
    in_row = lax.broadcasted_iota(jnp.int32, (tile, samples), 0) == row
    in_col = lax.broadcasted_iota(jnp.int32, (LANES, samples), 0) == col
    one_hot = jnp.where(in_col, 1.0, 0.0).astype(BF16)
    placed = jnp.where(in_row, summed, 0.0)
    high, rest = split(placed)
    low = (placed - high.astype(F32) - rest.astype(F32)).astype(BF16)
    grid = jnp.zeros((tile, LANES), F32)
    for part in (high, rest, low):
        grid = grid + lax.dot_general(
            part, one_hot, (((1,), (1,)), ((), ())), preferred_element_type=F32
        )

    placed_sum[...] = grid


def gradient_kernel(weights, grid, field_re, field_im, tables, *rest):
    *spec, grad, rim, total_re, total_im = rest
    period = grad.shape[0]
    half = period // 2
    tile = field_re.shape[1]
    radius = (period - tile) // 2
    cols = pair(tables, 0, LANES, 2 * LANES)
    cols = (stacked((cols[0], cols[0])), cols[1])
    rows = tile // 2
    cos_rows = tables[6, :half, : 3 * rows]
    sin_rows = tables[6, half:period, : 3 * rows]

    def along_rows(wide):
        out = []
        for table, x in (
            (cos_rows, wide[:rows] + wide[rows:]),
            (sin_rows, wide[:rows] - wide[rows:]),
        ):
            high, low = split(x)
            out.append(dot(table, stacked((high, low, high))))
        return out

    total_re[...] = jnp.zeros((period, 2 * LANES), F32)
    total_im[...] = jnp.zeros((period, 2 * LANES), F32)

    places = [(own, k) for own in spec for k in range(own.shape[1])]
    for group in range(len(places) // BATCH):
        sources = []
        for i in range(BATCH):
            k = group * BATCH + i
            weighted = grid[...] * weights[k]
            sources += [weighted * field_re[k], weighted * field_im[k]]
        high, low = split(stacked(sources))
        both = dot(jnp.concatenate([high, low], axis=1), cols[0]) + dot(high, cols[1])
        for i in range(BATCH):
            own, at = places[group * BATCH + i]
            real_cos, real_sin = halves(both[2 * i * tile : (2 * i + 1) * tile])
            imag_cos, imag_sin = halves(both[(2 * i + 1) * tile : (2 * i + 2) * tile])
            wide_re = jnp.concatenate([real_cos + imag_sin, real_cos - imag_sin], axis=1)
            wide_im = jnp.concatenate([imag_cos - real_sin, imag_cos + real_sin], axis=1)
            cos_re, sin_re = along_rows(wide_re)
            cos_im, sin_im = along_rows(wide_im)
            for start, sign in ((0, 1.0), (half, -1.0)):
                part = slice(start, start + half)
                wave_re = cos_re + sign * sin_im
                wave_im = cos_im - sign * sin_re
                own_re, own_im = own[0, at, part], own[1, at, part]
                total_re[part] += own_re * wave_re + own_im * wave_im
                total_im[part] += own_re * wave_im - own_im * wave_re

    pos_re, neg_re = total_re[:half], total_re[half:]
    pos_im, neg_im = total_im[:half], total_im[half:]
    back_rows = pair(tables, 4, period, period)
    back_rows = (back_rows[0], stacked(back_rows))
    for_re = jnp.concatenate([pos_re + neg_re, neg_im - pos_im], axis=0)
    for_im = jnp.concatenate([pos_im + neg_im, pos_re - neg_re], axis=0)
    re_pos, re_neg = halves(dot3_stacked(back_rows, split(for_re)))
    im_pos, im_neg = halves(dot3_stacked(back_rows, split(for_im)))
    last = jnp.concatenate([re_pos + re_neg, im_neg - im_pos], axis=1)
    framed = dot3(split(last), pair(tables, 2, 2 * LANES, period)) * (2.0 / (period * period))
    grad[...] = framed
    lower, _ = place_in_pair("ty")
    rim[...] = jnp.where(lower, framed[:radius], framed[radius + tile :])


VMEM = pl.BlockSpec(memory_space=pltpu.VMEM)
SMEM = pl.BlockSpec(memory_space=pltpu.SMEM)
ANY = pl.BlockSpec(memory_space=pl.ANY)


def shape(*dims):
    return jax.ShapeDtypeStruct(dims, F32)


def call(kernel, name, out_shape, in_specs, scratch=(), aliases=None, micros=1):
    return pl.pallas_call(
        kernel,
        out_shape=out_shape,
        in_specs=in_specs,
        out_specs=[VMEM] * len(out_shape),
        scratch_shapes=scratch,
        input_output_aliases=aliases or {},
        compiler_params=pltpu.CompilerParams(vmem_limit_bytes=10 * 1024 * 1024),
        cost_estimate=pl.CostEstimate(
            flops=micros * 10**9, bytes_accessed=2**20, transcendentals=0
        ),
        name=name,
    )


def gather_all(copies):
    return lax.all_to_all(copies, ("ty", "tx"), 0, 0, tiled=True)


def body(latent, kernels, socs_weights, dose_scale, inv_slope, edge_pixels, threshold_pick):
    tile = latent.shape[0]
    count, taps = kernels.shape[1], kernels.shape[-1]
    samples = edge_pixels.shape[1]
    radius = (taps - 1) // 2
    period = tile + 2 * radius
    half = period // 2
    first_tables = [jnp.asarray(x) for x in spectra_tables(period, taps - 1)]
    tables = jnp.asarray(field_tables(period, tile))
    last_tables = jnp.asarray(gradient_tables(period, tile))
    token = shape(8, LANES)
    packed = shape(tile // 2, 2 * radius)
    devices = lax.axis_size("ty") * lax.axis_size("tx")

    def spectra(start, first_out, parts, size, after, into=()):
        return call(
            functools.partial(spectra_kernel, start, first_out, parts),
            "spectra",
            [shape(2, size, period, 2 * LANES), token],
            [VMEM] * 4 + [ANY] * (1 + len(into)),
            aliases={5: 0} if into else None,
            micros=parts // 2,
        )(kernels, *first_tables, after, *into)

    transmit, done = call(
        own_kernel, "own", [shape(tile, tile), token], [VMEM], micros=3
    )(latent)
    partner, outside = swap("tx", transmit), swap_outside("tx", transmit)
    small, few = count // 3, count // 6
    large = count - small
    spec_a, done = spectra(0, 0, small, small, done)
    band, done = call(
        band_kernel, "band", [shape(tile, period), token], [VMEM] * 3 + [ANY]
    )(transmit, partner, outside, done)
    partner = swap("ty", band)
    spec_b, done = spectra(small, 0, few, large, done)
    rim, done = call(
        relay_rows_kernel, "relay", [shape(radius, period), token], [VMEM, ANY]
    )(partner, done)
    rim = ring("ty", rim)
    spec_b, _ = spectra(small + few, few, large - few, large, done, (spec_b,))
    spec = [spec_a, spec_b]

    field_re, field_im, sampled, copies = call(
        field_kernel,
        "field",
        [shape(count, tile, LANES)] * 2
        + [shape(1, 2 * samples), shape(devices, 1, 2 * samples)],
        [SMEM] + [VMEM] * (6 + len(spec)),
        scratch=[
            pltpu.VMEM((period, period), F32),
            pltpu.VMEM((4, half, 2 * LANES), F32),
        ],
        micros=7,
    )(socs_weights, band, partner, rim, edge_pixels, inv_slope, tables, *spec)

    gathered = gather_all(copies).reshape(devices, 2 * samples)
    grid, tail_mean = call(
        source_kernel,
        "source",
        [shape(tile, LANES), shape(1, 1)],
        [SMEM] * 3 + [VMEM] * 3,
        micros=2,
    )(socs_weights, dose_scale, threshold_pick, gathered, sampled, edge_pixels)
    grad, rim = call(
        gradient_kernel,
        "gradient",
        [shape(period, period), shape(radius, period)],
        [SMEM] + [VMEM] * (4 + len(spec)),
        scratch=[pltpu.VMEM((period, 2 * LANES), F32)] * 2,
        micros=6,
    )(socs_weights, grid, field_re, field_im, last_tables, *spec)

    rim = ring("ty", rim, back=True)
    (partner,) = call(fold_rows_kernel, "fold", [shape(tile, period)], [VMEM] * 2)(
        grad, rim
    )
    partner = swap("ty", partner)
    band, far = call(
        fold_band_kernel, "fold", [shape(tile, period), packed], [VMEM] * 2
    )(grad, partner)
    far = swap_outside("tx", far)
    (near,) = call(near_rim_kernel, "near", [packed], [VMEM])(band)
    near = swap("tx", near)
    (total,) = call(far_side_kernel, "far", [shape(tile, tile)], [VMEM] * 2)(band, far)
    (steering,) = call(finish_kernel, "finish", [shape(tile, tile)], [VMEM] * 3)(
        total, near, latent
    )
    return (steering, tail_mean.reshape(1))


def solution(mesh):
    placed = (P("ty", "tx"), P(), P(), P(), P("ty", "tx"), P("ty", "tx"), P())
    return jax.shard_map(
        body, mesh=mesh, in_specs=placed, out_specs=(P("ty", "tx"), P()), check_vma=False
    )
```

```python
import functools
import math

import jax
import jax.numpy as jnp
import ml_dtypes
import numpy as np
from jax import lax
from jax.experimental import pallas as pl
from jax.experimental.pallas import tpu as pltpu
from jax.sharding import PartitionSpec as P

STEEPNESS = 4.0
RESIST_LEVEL = 0.7
SOFTNESS = 0.25
LANES = 128
BATCH = 4
F32 = jnp.float32
BF16 = jnp.bfloat16


def split(x):
    high = x.astype(BF16)
    return high, (x - high.astype(F32)).astype(BF16)


def split3(x):
    first = x.astype(BF16)
    rest = x - first.astype(F32)
    second = rest.astype(BF16)
    return first, second, (rest - second.astype(F32)).astype(BF16)


def table_parts(table):
    parts = []
    for _ in range(3):
        parts.append(table.astype(ml_dtypes.bfloat16))
        table = table - parts[-1].astype(np.float64)
    return parts


def dot(a, b):
    return jnp.dot(a, b, preferred_element_type=F32)


def dot3(a, b):
    return dot(a[0], b[0]) + dot(a[0], b[1]) + dot(a[1], b[0])


def stacked(pair):
    return jnp.concatenate(pair, axis=0)


def dot6(a, b):
    small = dot(a[0], b[2]) + dot(a[1], b[1]) + dot(a[2], b[0])
    return small + (dot(a[0], b[1]) + dot(a[1], b[0])) + dot(a[0], b[0])


def dot3_stacked(a, b):
    high, both = a
    count = high.shape[0]
    tall = dot(both, b[0])
    return tall[:count] + tall[count:] + dot(high, b[1])


def waves(period, places):
    turn = (np.arange(period // 2) + 0.5) * (2.0 * math.pi / period)
    angle = turn[:, None] * places[None, :]
    return np.cos(angle), np.sin(angle)


def wave_table(period, places, by_lane=False):
    half = period // 2
    out = np.zeros((2 * LANES, 2 * LANES))
    for first, table in zip((0, LANES if by_lane else half), waves(period, places)):
        out[first : first + half, : len(places)] = table
    return out


def spectra_tables(period, last):
    taps = np.arange(last + 1)
    wide = wave_table(period, taps, True)
    tall = wave_table(period, taps)
    c1, c2, c3 = (part[:, :last].T for part in table_parts(wide))
    lanes = np.stack([np.concatenate(two) for two in ((c1, c1), (c2, c2), (c1, c3))])
    c1, c2, c3 = (part[:period, :last] for part in table_parts(tall))
    rows = [np.concatenate(two, axis=1) for two in ((c1, c1), (c2, c2), (c1, c3))]
    ends = np.zeros((period + 8, 2 * LANES), np.float32)
    ends[:period] = tall[:period, last : last + 1]
    ends[period] = wide[:, last]
    return lanes, np.concatenate(rows), ends


def field_tables(period, tile):
    half, rows = period // 2, tile // 2
    place = np.arange(period)
    wide = table_parts(wave_table(period, place, True))
    centred = table_parts(wave_table(period, place - (tile - 1) / 2))
    out = [part.T for part in wide] + centred + wide
    for table in waves(period, np.arange(rows) + 0.5):
        c1, c2, c3 = table_parts(table.T)
        slot = np.zeros((2 * LANES, 2 * LANES), ml_dtypes.bfloat16)
        for i, two in enumerate(((c1, c1), (c2, c2), (c3, 0 * c3), (c1, 0 * c1))):
            slot[i * rows : (i + 1) * rows, :period] = np.concatenate(two, axis=1)
        out.append(slot)
    return np.stack(out)


def gradient_tables(period, tile):
    half, rows = period // 2, tile // 2
    place = np.arange(period)
    wide = table_parts(wave_table(period, place, True))[:2]
    centred = table_parts(wave_table(period, place - (tile - 1) / 2))[:2]
    slot = np.zeros((2 * LANES, 2 * LANES), ml_dtypes.bfloat16)
    for i, table in enumerate(waves(period, np.arange(rows) + 0.5)):
        high, low, _ = table_parts(table)
        slot[i * half : (i + 1) * half, : 3 * rows] = np.concatenate([high, high, low], axis=1)
    return np.stack([part.T for part in wide] + wide + [part.T for part in centred] + [slot])


def pair(tables, first, rows, cols):
    return tables[first, :rows, :cols], tables[first + 1, :rows, :cols]


def triple(tables, first, rows, cols):
    return [tables[first + i, :rows, :cols] for i in range(3)]


def halves(x):
    return x[:, :LANES], x[:, LANES:]


def place_in_pair(axis):
    index, count = lax.axis_index(axis), lax.axis_size(axis)
    lower = lax.rem(index, 2) == 0
    return lower, jnp.where(lower, index > 0, index < count - 1)


def swap(axis, x):
    return lax.ppermute(x, axis, [(i, i ^ 1) for i in range(lax.axis_size(axis))])


def swap_outside(axis, x):
    count = lax.axis_size(axis)
    pairs = [(0, 0), (count - 1, count - 1)]
    for low in range(1, count - 1, 2):
        pairs += [(low, low + 1), (low + 1, low)]
    return lax.ppermute(x, axis, pairs)


def ring(axis, x, back=False):
    count = lax.axis_size(axis)
    cycle = list(range(0, count, 2)) + list(range(count - 1, 0, -2))
    pairs = list(zip(cycle, cycle[1:] + cycle[:1]))
    return lax.ppermute(x, axis, [(b, a) if back else (a, b) for a, b in pairs])


def spectra_kernel(start, first_out, parts, kern, lanes, rows, ends, *rest):
    out, token = rest[-2:]
    period = out.shape[2]
    half = period // 2
    last = kern.shape[-1] - 1
    end_row = ends[period : period + 1]
    token[...] = jnp.zeros(token.shape, F32)

    def along_lanes(planes):
        main = stacked([plane[:last] for plane in planes])
        tail = stacked([plane[last:] for plane in planes])
        tail = jnp.concatenate([tail, jnp.zeros((-tail.shape[0] % 16, last + 1), F32)], axis=0)
        both = stacked((main, tail))
        x1, x2, x3 = split3(both[:, :last])
        most = jnp.concatenate([x1, x2], axis=1)
        out = dot(jnp.concatenate([x3, x1], axis=1), lanes[2]) + dot(most, lanes[1])
        out = out + dot(most, lanes[0]) + both[:, last:] * end_row
        first = len(planes) * last
        return [
            (out[i * last : (i + 1) * last], out[first + i : first + i + 1])
            for i in range(len(planes))
        ]

    def along_rows(wide, tail):
        x1, x2, x3 = split3(wide)
        tall = dot(rows[: 2 * period], stacked((x1, x2)))
        small = dot(rows[2 * period :], stacked((x3, x1)))
        return tall[:period] + (tall[period:] + small) + ends[:period] * tail

    def mixed(real, imag):
        real_cos, real_sin = halves(real)
        imag_cos, imag_sin = halves(imag)
        return (
            jnp.concatenate([real_cos - imag_sin, real_cos + imag_sin], axis=1),
            jnp.concatenate([real_sin + imag_cos, imag_cos - real_sin], axis=1),
        )

    planes = along_lanes([kern[c, start + k] for k in range(parts) for c in range(2)])
    for k in range(parts):
        to = first_out + k
        (real, real_tail), (imag, imag_tail) = planes[2 * k : 2 * k + 2]
        wide_re, wide_im = mixed(real, imag)
        tail_re, tail_im = mixed(real_tail, imag_tail)
        tall_re = along_rows(wide_re, tail_re)
        tall_im = along_rows(wide_im, tail_im)
        out[0, to, :half] = tall_re[:half] - tall_im[half:]
        out[0, to, half:] = tall_re[:half] + tall_im[half:]
        out[1, to, :half] = tall_im[:half] + tall_re[half:]
        out[1, to, half:] = tall_im[:half] - tall_re[half:]


def pack(x):
    count = x.shape[0] // 2
    return jnp.concatenate([x[:count], x[count:]], axis=1)


def unpack(x):
    width = x.shape[1] // 2
    return jnp.concatenate([x[:, :width], x[:, width:]], axis=0)


def own_kernel(latent, transmit, token):
    transmit[...] = 0.5 * (1.0 + jnp.tanh(latent[...]))
    token[...] = jnp.zeros(token.shape, F32)


def band_kernel(middle, partner, outside, after, band, token):
    tile = middle.shape[0]
    radius = (band.shape[1] - tile) // 2
    lower, other = place_in_pair("tx")

    near = jnp.where(lower, partner[:, :radius], partner[:, tile - radius :])
    near = 0.5 * (1.0 + jnp.tanh(near))
    far = jnp.where(lower, outside[:, tile - radius :], outside[:, :radius])
    far = jnp.where(other, far, 0.0)
    band[:, :radius] = jnp.where(lower, far, near)
    band[:, radius : radius + tile] = middle[...]
    band[:, radius + tile :] = jnp.where(lower, near, far)
    token[...] = jnp.zeros(token.shape, F32)


def relay_rows_kernel(partner, after, rim, token):
    radius = rim.shape[0]
    tile = partner.shape[0]
    lower, _ = place_in_pair("ty")
    rim[...] = jnp.where(lower, partner[tile - radius :], partner[:radius])
    token[...] = jnp.zeros(token.shape, F32)


def fold_rows_kernel(grad, rim, out):
    radius = rim.shape[0]
    tile = out.shape[0]
    lower, _ = place_in_pair("ty")
    count, index = lax.axis_size("ty"), lax.axis_index("ty")
    comes = jnp.where(lower, index < count - 2, index > 1)
    outer = jnp.where(comes, rim[...], 0.0)
    top = jnp.where(lower, grad[radius + tile :], outer)
    bottom = jnp.where(lower, outer, grad[:radius])
    out[:radius] = top
    out[radius:] = jnp.zeros((tile - radius, out.shape[1]), F32)
    out[tile - radius :] += bottom


def fold_band_kernel(grad, partner, band, far):
    tile = band.shape[0]
    radius = far.shape[1] // 2
    lower, _ = place_in_pair("tx")
    band[...] = grad[radius : radius + tile] + partner[...]
    far[...] = jnp.where(lower, pack(band[:, :radius]), pack(band[:, radius + tile :]))


def near_rim_kernel(band, near):
    tile = band.shape[0]
    radius = near.shape[1] // 2
    lower, _ = place_in_pair("tx")
    near[...] = jnp.where(lower, pack(band[:, radius + tile :]), pack(band[:, :radius]))


def far_side_kernel(band, far, out):
    tile = out.shape[0]
    radius = (band.shape[1] - tile) // 2
    lower, other = place_in_pair("tx")
    outer = jnp.where(other, unpack(far[...]), 0.0)
    out[...] = band[:, radius : radius + tile]
    out[:, :radius] += jnp.where(lower, outer, 0.0)
    out[:, tile - radius :] += jnp.where(lower, 0.0, outer)


def finish_kernel(total, near, latent, steering):
    tile = latent.shape[0]
    radius = near.shape[1] // 2
    lower, _ = place_in_pair("tx")
    inner = unpack(near[...])
    steering[...] = total[...]
    steering[:, :radius] += jnp.where(lower, 0.0, inner)
    steering[:, tile - radius :] += jnp.where(lower, inner, 0.0)
    value = jnp.tanh(latent[...])
    steering[...] = steering[...] * 0.5 * (1.0 - value * value)


def total_weight(weights, kernels):
    total = weights[0]
    for k in range(1, kernels):
        total = total + weights[k]
    return jnp.full((1, 1), total, F32)


def sample_places(pixels, tile):
    row = ((pixels.astype(F32) + 0.5) * (1.0 / tile)).astype(jnp.int32)
    held = jnp.where(row < tile // 2, tile - 1 - row, row - tile // 2)
    return held, pixels - row * tile


def field_kernel(weights, band, partner, rim, pixels, slopes, tables, *rest):
    *spec, field_re, field_im, sampled, copies, framed, mask = rest
    kernels = weights.shape[0]
    period = band.shape[1]
    half = period // 2
    tile = field_re.shape[1]
    radius = rim.shape[0]
    lower, other = place_in_pair("ty")
    outer = jnp.where(other, rim[...], 0.0)
    framed[:radius] = jnp.where(lower, outer, partner[tile - radius :])
    framed[radius + tile :] = jnp.where(lower, partner[:radius], outer)
    framed[radius : radius + tile] = band[...]
    wide = dot6(split3(framed[...]), triple(tables, 0, period, 2 * LANES))
    tall = dot6(triple(tables, 3, period, period), split3(wide)) * (1.0 / (period * period))
    cos_cos, cos_sin = halves(tall[:half])
    sin_cos, sin_sin = halves(tall[half:])
    same, other = cos_cos - sin_sin, cos_cos + sin_sin
    joint, cross = sin_cos + cos_sin, sin_cos - cos_sin
    mask[0, :, :LANES], mask[0, :, LANES:] = same, other
    mask[1, :, :LANES], mask[1, :, LANES:] = -joint, -cross
    mask[2, :, :LANES], mask[2, :, LANES:] = other, same
    mask[3, :, :LANES], mask[3, :, LANES:] = cross, joint
    rows = tile // 2

    def lift(slot, x):
        x1, x2, x3 = split3(x)
        out = dot(tables[slot, : 3 * rows, :period], stacked((x1, x2)))
        small = dot(tables[slot, 3 * rows : 4 * rows, :half], x3)
        return out[:rows] + (out[rows:tile] + (out[tile:] + small))

    across = triple(tables, 6, 2 * LANES, LANES)
    across = (across[0], jnp.concatenate(across[:2], axis=1), across[2])

    def lifted(own, k):
        pos_re, pos_im = own[0, k, :half], own[1, k, :half]
        neg_re, neg_im = own[0, k, half:], own[1, k, half:]
        up_re = mask[0] * pos_re - mask[1] * pos_im
        up_im = mask[0] * pos_im + mask[1] * pos_re
        down_re = mask[2] * neg_re - mask[3] * neg_im
        down_im = mask[2] * neg_im + mask[3] * neg_re
        even_re = lift(9, up_re + down_re)
        even_im = lift(9, up_im + down_im)
        odd_re = lift(10, up_im - down_im)
        odd_im = lift(10, up_re - down_re)
        re_pos, re_neg = halves(stacked((even_re - odd_re, even_re + odd_re)))
        im_pos, im_neg = halves(stacked((even_im + odd_im, even_im - odd_im)))
        rows_re = jnp.concatenate([re_pos + re_neg, im_neg - im_pos], axis=1)
        rows_im = jnp.concatenate([im_pos + im_neg, re_pos - re_neg], axis=1)
        return [rows_re, rows_im]

    intensity = jnp.zeros((tile, LANES), F32)
    places = [(own, k) for own in spec for k in range(own.shape[1])]
    for first in range(0, kernels, BATCH):
        lines = stacked([line for i in range(BATCH) for line in lifted(*places[first + i])])
        x1, x2, x3 = split3(lines)
        most, more = halves(dot(x1, across[1]))
        some, small = halves(dot(x2, across[1]))
        both = small + dot(x1, across[2]) + dot(x3, across[0]) + (more + some) + most
        for i in range(BATCH):
            real = both[2 * i * tile : (2 * i + 1) * tile]
            imag = both[(2 * i + 1) * tile : (2 * i + 2) * tile]
            field_re[first + i] = real
            field_im[first + i] = imag
            intensity = intensity + weights[first + i] * (real * real + imag * imag)
    intensity = intensity / total_weight(weights, kernels)
    samples = pixels.shape[1]
    row, col = sample_places(pixels[...], tile)
    in_col = lax.broadcasted_iota(jnp.int32, (LANES, samples), 0) == col
    one_hot = jnp.where(in_col, 1.0, 0.0).astype(BF16)
    high, rest = split(intensity)
    low = intensity - high.astype(F32) - rest.astype(F32)
    picked = dot(high, one_hot) + dot(rest, one_hot) + dot(low.astype(BF16), one_hot)
    in_row = lax.broadcasted_iota(jnp.int32, (tile, samples), 0) == row
    own = jnp.sum(jnp.where(in_row, picked, 0.0), axis=0, keepdims=True)
    sampled[...] = jnp.concatenate([own, slopes[...]], axis=1)
    copies[...] = jnp.broadcast_to(sampled[...][None], copies.shape)


def sigmoid(x):
    return 1.0 / (1.0 + jnp.exp(-x))


def errors(intensity, slope, dose):
    resist = 0.5 * jnp.tanh(0.5 * STEEPNESS * (dose * intensity - RESIST_LEVEL))
    offset = resist * slope
    return resist, offset, offset * offset


def own_samples_kernel(doses, sampled, pixels, own_error, chain, in_row, one_hot):
    corners, samples = own_error.shape
    tile = in_row.shape[0]
    own, slope = sampled[:, :samples], sampled[:, samples:]
    which = lax.broadcasted_iota(jnp.int32, (corners, samples), 0)
    dose = jnp.zeros((corners, samples), F32)
    for c in range(corners):
        dose = jnp.where(which == c, doses[c], dose)
    resist, offset, error = errors(own, slope, dose)
    own_error[...] = error
    chain[...] = 2.0 * STEEPNESS * offset * slope * dose * (0.25 - resist * resist)
    row, col = sample_places(pixels[...], tile)
    place = lax.broadcasted_iota(jnp.int32, (tile, samples), 0)
    in_row[...] = jnp.where(place == row, 1.0, 0.0)
    place = lax.broadcasted_iota(jnp.int32, (LANES, samples), 0)
    one_hot[...] = jnp.where(place == col, 1.0, 0.0).astype(BF16)


def source_kernel(
    weights, doses, pick, gathered, own_error, chain, in_row, one_hot, placed_sum, tail
):
    kernels = weights.shape[0]
    tile = placed_sum.shape[0]
    samples = own_error.shape[1]
    devices = gathered.shape[0]
    corners = doses.shape[0]
    per_corner = devices * samples
    everyone, every_slope = gathered[:, :samples], gathered[:, samples:]
    pick_corner = pick[0] // per_corner
    remain = pick[0] - pick_corner * per_corner
    place = lax.broadcasted_iota(jnp.int32, (devices, samples), 0) * samples
    place = place + lax.broadcasted_iota(jnp.int32, (devices, samples), 1)
    _, _, picked = errors(everyone, every_slope, doses[pick_corner])
    threshold = jnp.sum(jnp.where(place == remain, picked, 0.0), keepdims=True)

    def corner(c, sums):
        _, _, error = errors(everyone, every_slope, doses[c])
        soft = sigmoid((error - threshold) * (1.0 / SOFTNESS))
        return sums[0] + soft, sums[1] + error * soft

    zero = jnp.zeros((devices, samples), F32)
    soft_sum, error_sum = lax.fori_loop(
        0, corners, corner, (zero, zero), unroll=8 if devices <= 32 else 1
    )
    soft_total = jnp.sum(soft_sum, keepdims=True)
    tail_mean = jnp.sum(error_sum, keepdims=True) / soft_total
    tail[...] = tail_mean

    error = own_error[...]
    soft = sigmoid((error - threshold) * (1.0 / SOFTNESS))
    slope_soft = soft * (1.0 - soft) * (1.0 / SOFTNESS)
    coefficient = (soft + (error - tail_mean) * slope_soft) * (corners * per_corner / soft_total)
    summed = jnp.sum(coefficient * chain[...], axis=0, keepdims=True)
    summed = summed / total_weight(weights, kernels)

    placed = in_row[...] * summed
    high, rest = split(placed)
    low = (placed - high.astype(F32) - rest.astype(F32)).astype(BF16)
    grid = jnp.zeros((tile, LANES), F32)
    for part in (high, rest, low):
        grid = grid + lax.dot_general(
            part, one_hot[...], (((1,), (1,)), ((), ())), preferred_element_type=F32
        )

    placed_sum[...] = grid


def gradient_kernel(weights, grid, field_re, field_im, tables, *rest):
    *spec, grad, rim, total_re, total_im = rest
    period = grad.shape[0]
    half = period // 2
    tile = field_re.shape[1]
    radius = (period - tile) // 2
    cols = pair(tables, 0, LANES, 2 * LANES)
    cols = (stacked((cols[0], cols[0])), cols[1])
    rows = tile // 2
    cos_rows = tables[6, :half, : 3 * rows]
    sin_rows = tables[6, half:period, : 3 * rows]

    def along_rows(wide):
        out = []
        for table, x in (
            (cos_rows, wide[:rows] + wide[rows:]),
            (sin_rows, wide[:rows] - wide[rows:]),
        ):
            high, low = split(x)
            out.append(dot(table, stacked((high, low, high))))
        return out

    total_re[...] = jnp.zeros((period, 2 * LANES), F32)
    total_im[...] = jnp.zeros((period, 2 * LANES), F32)

    places = [(own, k) for own in spec for k in range(own.shape[1])]
    for group in range(len(places) // BATCH):
        sources = []
        for i in range(BATCH):
            k = group * BATCH + i
            weighted = grid[...] * weights[k]
            sources += [weighted * field_re[k], weighted * field_im[k]]
        high, low = split(stacked(sources))
        both = dot(jnp.concatenate([high, low], axis=1), cols[0]) + dot(high, cols[1])
        for i in range(BATCH):
            own, at = places[group * BATCH + i]
            real_cos, real_sin = halves(both[2 * i * tile : (2 * i + 1) * tile])
            imag_cos, imag_sin = halves(both[(2 * i + 1) * tile : (2 * i + 2) * tile])
            wide_re = jnp.concatenate([real_cos + imag_sin, real_cos - imag_sin], axis=1)
            wide_im = jnp.concatenate([imag_cos - real_sin, imag_cos + real_sin], axis=1)
            cos_re, sin_re = along_rows(wide_re)
            cos_im, sin_im = along_rows(wide_im)
            for start, sign in ((0, 1.0), (half, -1.0)):
                part = slice(start, start + half)
                wave_re = cos_re + sign * sin_im
                wave_im = cos_im - sign * sin_re
                own_re, own_im = own[0, at, part], own[1, at, part]
                total_re[part] += own_re * wave_re + own_im * wave_im
                total_im[part] += own_re * wave_im - own_im * wave_re

    pos_re, neg_re = total_re[:half], total_re[half:]
    pos_im, neg_im = total_im[:half], total_im[half:]
    back_rows = pair(tables, 4, period, period)
    back_rows = (back_rows[0], stacked(back_rows))
    for_re = jnp.concatenate([pos_re + neg_re, neg_im - pos_im], axis=0)
    for_im = jnp.concatenate([pos_im + neg_im, pos_re - neg_re], axis=0)
    re_pos, re_neg = halves(dot3_stacked(back_rows, split(for_re)))
    im_pos, im_neg = halves(dot3_stacked(back_rows, split(for_im)))
    last = jnp.concatenate([re_pos + re_neg, im_neg - im_pos], axis=1)
    framed = dot3(split(last), pair(tables, 2, 2 * LANES, period)) * (2.0 / (period * period))
    grad[...] = framed
    lower, _ = place_in_pair("ty")
    rim[...] = jnp.where(lower, framed[:radius], framed[radius + tile :])


VMEM = pl.BlockSpec(memory_space=pltpu.VMEM)
SMEM = pl.BlockSpec(memory_space=pltpu.SMEM)
ANY = pl.BlockSpec(memory_space=pl.ANY)


def shape(*dims):
    return jax.ShapeDtypeStruct(dims, F32)


def call(kernel, name, out_shape, in_specs, scratch=(), aliases=None, micros=1):
    return pl.pallas_call(
        kernel,
        out_shape=out_shape,
        in_specs=in_specs,
        out_specs=[VMEM] * len(out_shape),
        scratch_shapes=scratch,
        input_output_aliases=aliases or {},
        compiler_params=pltpu.CompilerParams(vmem_limit_bytes=10 * 1024 * 1024),
        cost_estimate=pl.CostEstimate(
            flops=micros * 10**9, bytes_accessed=2**20, transcendentals=0
        ),
        name=name,
    )


def gather_all(copies):
    return lax.all_to_all(copies, ("ty", "tx"), 0, 0, tiled=True)


def body(latent, kernels, socs_weights, dose_scale, inv_slope, edge_pixels, threshold_pick):
    tile = latent.shape[0]
    count, taps = kernels.shape[1], kernels.shape[-1]
    samples = edge_pixels.shape[1]
    radius = (taps - 1) // 2
    period = tile + 2 * radius
    half = period // 2
    first_tables = [jnp.asarray(x) for x in spectra_tables(period, taps - 1)]
    tables = jnp.asarray(field_tables(period, tile))
    last_tables = jnp.asarray(gradient_tables(period, tile))
    token = shape(8, LANES)
    packed = shape(tile // 2, 2 * radius)
    devices = lax.axis_size("ty") * lax.axis_size("tx")

    def spectra(start, first_out, parts, size, after, into=()):
        return call(
            functools.partial(spectra_kernel, start, first_out, parts),
            "spectra",
            [shape(2, size, period, 2 * LANES), token],
            [VMEM] * 4 + [ANY] * (1 + len(into)),
            aliases={5: 0} if into else None,
            micros=parts // 2,
        )(kernels, *first_tables, after, *into)

    partner = swap("tx", latent)
    transmit, done = call(
        own_kernel, "own", [shape(tile, tile), token], [VMEM], micros=3
    )(latent)
    outside = swap_outside("tx", transmit)
    small, few = count // 3, count // 6
    large = count - small
    spec_a, done = spectra(0, 0, small, small, done)
    band, done = call(
        band_kernel, "band", [shape(tile, period), token], [VMEM] * 3 + [ANY]
    )(transmit, partner, outside, done)
    partner = swap("ty", band)
    spec_b, done = spectra(small, 0, few, large, done)
    rim, done = call(
        relay_rows_kernel, "relay", [shape(radius, period), token], [VMEM, ANY]
    )(partner, done)
    rim = ring("ty", rim)
    spec_b, _ = spectra(small + few, few, large - few, large, done, (spec_b,))
    spec = [spec_a, spec_b]

    field_re, field_im, sampled, copies = call(
        field_kernel,
        "field",
        [shape(count, tile, LANES)] * 2
        + [shape(1, 2 * samples), shape(devices, 1, 2 * samples)],
        [SMEM] + [VMEM] * (6 + len(spec)),
        scratch=[
            pltpu.VMEM((period, period), F32),
            pltpu.VMEM((4, half, 2 * LANES), F32),
        ],
        micros=7,
    )(socs_weights, band, partner, rim, edge_pixels, inv_slope, tables, *spec)

    gathered = gather_all(copies).reshape(devices, 2 * samples)
    corners = dose_scale.shape[0]
    own = call(
        own_samples_kernel,
        "samples",
        [shape(corners, samples)] * 2
        + [shape(tile, samples), jax.ShapeDtypeStruct((LANES, samples), BF16)],
        [SMEM] + [VMEM] * 2,
        micros=2,
    )(dose_scale, sampled, edge_pixels)
    grid, tail_mean = call(
        source_kernel,
        "source",
        [shape(tile, LANES), shape(1, 1)],
        [SMEM] * 3 + [VMEM] * 5,
        micros=2,
    )(socs_weights, dose_scale, threshold_pick, gathered, *own)
    grad, rim = call(
        gradient_kernel,
        "gradient",
        [shape(period, period), shape(radius, period)],
        [SMEM] + [VMEM] * (4 + len(spec)),
        scratch=[pltpu.VMEM((period, 2 * LANES), F32)] * 2,
        micros=6,
    )(socs_weights, grid, field_re, field_im, last_tables, *spec)

    rim = ring("ty", rim, back=True)
    (partner,) = call(fold_rows_kernel, "fold", [shape(tile, period)], [VMEM] * 2)(
        grad, rim
    )
    partner = swap("ty", partner)
    band, far = call(
        fold_band_kernel, "fold", [shape(tile, period), packed], [VMEM] * 2
    )(grad, partner)
    far = swap_outside("tx", far)
    (near,) = call(near_rim_kernel, "near", [packed], [VMEM])(band)
    near = swap("tx", near)
    (total,) = call(far_side_kernel, "far", [shape(tile, tile)], [VMEM] * 2)(band, far)
    (steering,) = call(finish_kernel, "finish", [shape(tile, tile)], [VMEM] * 3)(
        total, near, latent
    )
    return (steering, tail_mean.reshape(1))


def solution(mesh):
    placed = (P("ty", "tx"), P(), P(), P(), P("ty", "tx"), P("ty", "tx"), P())
    return jax.shard_map(
        body, mesh=mesh, in_specs=placed, out_specs=(P("ty", "tx"), P()), check_vma=False
    )
```

```python
import functools
import math

import jax
import jax.numpy as jnp
import ml_dtypes
import numpy as np
from jax import lax
from jax.experimental import pallas as pl
from jax.experimental.pallas import tpu as pltpu
from jax.sharding import PartitionSpec as P

STEEPNESS = 4.0
RESIST_LEVEL = 0.7
SOFTNESS = 0.25
LANES = 128
BATCH = 4
F32 = jnp.float32
BF16 = jnp.bfloat16


def split(x):
    high = x.astype(BF16)
    return high, (x - high.astype(F32)).astype(BF16)


def split3(x):
    first = x.astype(BF16)
    rest = x - first.astype(F32)
    second = rest.astype(BF16)
    return first, second, (rest - second.astype(F32)).astype(BF16)


def table_parts(table):
    parts = []
    for _ in range(3):
        parts.append(table.astype(ml_dtypes.bfloat16))
        table = table - parts[-1].astype(np.float64)
    return parts


def dot(a, b):
    return jnp.dot(a, b, preferred_element_type=F32)


def dot3(a, b):
    return dot(a[0], b[0]) + dot(a[0], b[1]) + dot(a[1], b[0])


def stacked(pair):
    return jnp.concatenate(pair, axis=0)


def dot6(a, b):
    small = dot(a[0], b[2]) + dot(a[1], b[1]) + dot(a[2], b[0])
    return small + (dot(a[0], b[1]) + dot(a[1], b[0])) + dot(a[0], b[0])


def dot3_stacked(a, b):
    high, both = a
    count = high.shape[0]
    tall = dot(both, b[0])
    return tall[:count] + tall[count:] + dot(high, b[1])


def waves(period, places):
    turn = (np.arange(period // 2) + 0.5) * (2.0 * math.pi / period)
    angle = turn[:, None] * places[None, :]
    return np.cos(angle), np.sin(angle)


def wave_table(period, places, by_lane=False):
    half = period // 2
    out = np.zeros((2 * LANES, 2 * LANES))
    for first, table in zip((0, LANES if by_lane else half), waves(period, places)):
        out[first : first + half, : len(places)] = table
    return out


def spectra_tables(period, last):
    taps = np.arange(last + 1)
    wide = wave_table(period, taps, True)
    tall = wave_table(period, taps)
    c1, c2, c3 = (part[:, :last].T for part in table_parts(wide))
    lanes = np.stack([np.concatenate(two) for two in ((c1, c1), (c2, c2), (c1, c3))])
    c1, c2, c3 = (part[:period, :last] for part in table_parts(tall))
    rows = [np.concatenate(two, axis=1) for two in ((c1, c1), (c2, c2), (c1, c3))]
    ends = np.zeros((period + 8, 2 * LANES), np.float32)
    ends[:period] = tall[:period, last : last + 1]
    ends[period] = wide[:, last]
    return lanes, np.concatenate(rows), ends


def field_tables(period, tile):
    half, rows = period // 2, tile // 2
    place = np.arange(period)
    wide = table_parts(wave_table(period, place, True))
    centred = table_parts(wave_table(period, place - (tile - 1) / 2))
    out = [part.T for part in wide] + centred + wide
    for table in waves(period, np.arange(rows) + 0.5):
        c1, c2, c3 = table_parts(table.T)
        slot = np.zeros((2 * LANES, 2 * LANES), ml_dtypes.bfloat16)
        for i, two in enumerate(((c1, c1), (c2, c2), (c3, 0 * c3), (c1, 0 * c1))):
            slot[i * rows : (i + 1) * rows, :period] = np.concatenate(two, axis=1)
        out.append(slot)
    return np.stack(out)


def gradient_tables(period, tile):
    half, rows = period // 2, tile // 2
    place = np.arange(period)
    wide = table_parts(wave_table(period, place, True))[:2]
    centred = table_parts(wave_table(period, place - (tile - 1) / 2))[:2]
    slot = np.zeros((2 * LANES, 2 * LANES), ml_dtypes.bfloat16)
    for i, table in enumerate(waves(period, np.arange(rows) + 0.5)):
        high, low, _ = table_parts(table)
        slot[i * half : (i + 1) * half, : 3 * rows] = np.concatenate([high, high, low], axis=1)
    return np.stack([part.T for part in wide] + wide + [part.T for part in centred] + [slot])


def pair(tables, first, rows, cols):
    return tables[first, :rows, :cols], tables[first + 1, :rows, :cols]


def triple(tables, first, rows, cols):
    return [tables[first + i, :rows, :cols] for i in range(3)]


def halves(x):
    return x[:, :LANES], x[:, LANES:]


def place_in_pair(axis):
    index, count = lax.axis_index(axis), lax.axis_size(axis)
    lower = lax.rem(index, 2) == 0
    return lower, jnp.where(lower, index > 0, index < count - 1)


def swap(axis, x):
    return lax.ppermute(x, axis, [(i, i ^ 1) for i in range(lax.axis_size(axis))])


def swap_outside(axis, x):
    count = lax.axis_size(axis)
    pairs = [(0, 0), (count - 1, count - 1)]
    for low in range(1, count - 1, 2):
        pairs += [(low, low + 1), (low + 1, low)]
    return lax.ppermute(x, axis, pairs)


def ring(axis, x, back=False):
    count = lax.axis_size(axis)
    cycle = list(range(0, count, 2)) + list(range(count - 1, 0, -2))
    pairs = list(zip(cycle, cycle[1:] + cycle[:1]))
    return lax.ppermute(x, axis, [(b, a) if back else (a, b) for a, b in pairs])


def spectra_kernel(start, first_out, parts, kern, lanes, rows, ends, *rest):
    out, token = rest[-2:]
    period = out.shape[2]
    half = period // 2
    last = kern.shape[-1] - 1
    end_row = ends[period : period + 1]
    token[...] = jnp.zeros(token.shape, F32)

    def along_lanes(planes):
        main = stacked([plane[:last] for plane in planes])
        tail = stacked([plane[last:] for plane in planes])
        tail = jnp.concatenate([tail, jnp.zeros((-tail.shape[0] % 16, last + 1), F32)], axis=0)
        both = stacked((main, tail))
        x1, x2, x3 = split3(both[:, :last])
        most = jnp.concatenate([x1, x2], axis=1)
        out = dot(jnp.concatenate([x3, x1], axis=1), lanes[2]) + dot(most, lanes[1])
        out = out + dot(most, lanes[0]) + both[:, last:] * end_row
        first = len(planes) * last
        return [
            (out[i * last : (i + 1) * last], out[first + i : first + i + 1])
            for i in range(len(planes))
        ]

    def along_rows(wide, tail):
        x1, x2, x3 = split3(wide)
        tall = dot(rows[: 2 * period], stacked((x1, x2)))
        small = dot(rows[2 * period :], stacked((x3, x1)))
        return tall[:period] + (tall[period:] + small) + ends[:period] * tail

    def mixed(real, imag):
        real_cos, real_sin = halves(real)
        imag_cos, imag_sin = halves(imag)
        return (
            jnp.concatenate([real_cos - imag_sin, real_cos + imag_sin], axis=1),
            jnp.concatenate([real_sin + imag_cos, imag_cos - real_sin], axis=1),
        )

    planes = along_lanes([kern[c, start + k] for k in range(parts) for c in range(2)])
    for k in range(parts):
        to = first_out + k
        (real, real_tail), (imag, imag_tail) = planes[2 * k : 2 * k + 2]
        wide_re, wide_im = mixed(real, imag)
        tail_re, tail_im = mixed(real_tail, imag_tail)
        tall_re = along_rows(wide_re, tail_re)
        tall_im = along_rows(wide_im, tail_im)
        out[0, to, :half] = tall_re[:half] - tall_im[half:]
        out[0, to, half:] = tall_re[:half] + tall_im[half:]
        out[1, to, :half] = tall_im[:half] + tall_re[half:]
        out[1, to, half:] = tall_im[:half] - tall_re[half:]


def pack(x):
    count = x.shape[0] // 2
    return jnp.concatenate([x[:count], x[count:]], axis=1)


def unpack(x):
    width = x.shape[1] // 2
    return jnp.concatenate([x[:, :width], x[:, width:]], axis=0)


def own_kernel(latent, transmit, token):
    transmit[...] = 0.5 * (1.0 + jnp.tanh(latent[...]))
    token[...] = jnp.zeros(token.shape, F32)


def band_kernel(middle, partner, outside, after, band, token):
    tile = middle.shape[0]
    radius = (band.shape[1] - tile) // 2
    lower, other = place_in_pair("tx")

    near = jnp.where(lower, partner[:, :radius], partner[:, tile - radius :])
    far = jnp.where(lower, outside[:, tile - radius :], outside[:, :radius])
    far = jnp.where(other, far, 0.0)
    band[:, :radius] = jnp.where(lower, far, near)
    band[:, radius : radius + tile] = middle[...]
    band[:, radius + tile :] = jnp.where(lower, near, far)
    token[...] = jnp.zeros(token.shape, F32)


def relay_rows_kernel(partner, after, rim, token):
    radius = rim.shape[0]
    tile = partner.shape[0]
    lower, _ = place_in_pair("ty")
    rim[...] = jnp.where(lower, partner[tile - radius :], partner[:radius])
    token[...] = jnp.zeros(token.shape, F32)


def fold_rows_kernel(grad, rim, out):
    radius = rim.shape[0]
    tile = out.shape[0]
    lower, _ = place_in_pair("ty")
    count, index = lax.axis_size("ty"), lax.axis_index("ty")
    comes = jnp.where(lower, index < count - 2, index > 1)
    outer = jnp.where(comes, rim[...], 0.0)
    top = jnp.where(lower, grad[radius + tile :], outer)
    bottom = jnp.where(lower, outer, grad[:radius])
    out[:radius] = top
    out[radius:] = jnp.zeros((tile - radius, out.shape[1]), F32)
    out[tile - radius :] += bottom


def fold_band_kernel(grad, partner, band, far):
    tile = band.shape[0]
    radius = far.shape[1] // 2
    lower, _ = place_in_pair("tx")
    band[...] = grad[radius : radius + tile] + partner[...]
    far[...] = jnp.where(lower, pack(band[:, :radius]), pack(band[:, radius + tile :]))


def near_rim_kernel(band, near):
    tile = band.shape[0]
    radius = near.shape[1] // 2
    lower, _ = place_in_pair("tx")
    near[...] = jnp.where(lower, pack(band[:, radius + tile :]), pack(band[:, :radius]))


def far_side_kernel(band, far, out):
    tile = out.shape[0]
    radius = (band.shape[1] - tile) // 2
    lower, other = place_in_pair("tx")
    outer = jnp.where(other, unpack(far[...]), 0.0)
    out[...] = band[:, radius : radius + tile]
    out[:, :radius] += jnp.where(lower, outer, 0.0)
    out[:, tile - radius :] += jnp.where(lower, 0.0, outer)


def finish_kernel(total, near, latent, steering):
    tile = latent.shape[0]
    radius = near.shape[1] // 2
    lower, _ = place_in_pair("tx")
    inner = unpack(near[...])
    steering[...] = total[...]
    steering[:, :radius] += jnp.where(lower, 0.0, inner)
    steering[:, tile - radius :] += jnp.where(lower, inner, 0.0)
    value = jnp.tanh(latent[...])
    steering[...] = steering[...] * 0.5 * (1.0 - value * value)


def total_weight(weights, kernels):
    total = weights[0]
    for k in range(1, kernels):
        total = total + weights[k]
    return jnp.full((1, 1), total, F32)


def sample_places(pixels, tile):
    row = ((pixels.astype(F32) + 0.5) * (1.0 / tile)).astype(jnp.int32)
    held = jnp.where(row < tile // 2, tile - 1 - row, row - tile // 2)
    return held, pixels - row * tile


def field_kernel(weights, band, partner, rim, pixels, slopes, tables, *rest):
    *spec, field_re, field_im, sampled, copies, framed, mask = rest
    kernels = weights.shape[0]
    period = band.shape[1]
    half = period // 2
    tile = field_re.shape[1]
    radius = rim.shape[0]
    lower, other = place_in_pair("ty")
    outer = jnp.where(other, rim[...], 0.0)
    framed[:radius] = jnp.where(lower, outer, partner[tile - radius :])
    framed[radius + tile :] = jnp.where(lower, partner[:radius], outer)
    framed[radius : radius + tile] = band[...]
    wide = dot6(split3(framed[...]), triple(tables, 0, period, 2 * LANES))
    tall = dot6(triple(tables, 3, period, period), split3(wide)) * (1.0 / (period * period))
    cos_cos, cos_sin = halves(tall[:half])
    sin_cos, sin_sin = halves(tall[half:])
    same, other = cos_cos - sin_sin, cos_cos + sin_sin
    joint, cross = sin_cos + cos_sin, sin_cos - cos_sin
    mask[0, :, :LANES], mask[0, :, LANES:] = same, other
    mask[1, :, :LANES], mask[1, :, LANES:] = -joint, -cross
    mask[2, :, :LANES], mask[2, :, LANES:] = other, same
    mask[3, :, :LANES], mask[3, :, LANES:] = cross, joint
    rows = tile // 2

    def lift(slot, x):
        x1, x2, x3 = split3(x)
        out = dot(tables[slot, : 3 * rows, :period], stacked((x1, x2)))
        small = dot(tables[slot, 3 * rows : 4 * rows, :half], x3)
        return out[:rows] + (out[rows:tile] + (out[tile:] + small))

    across = triple(tables, 6, 2 * LANES, LANES)
    across = (across[0], jnp.concatenate(across[:2], axis=1), across[2])

    def lifted(own, k):
        pos_re, pos_im = own[0, k, :half], own[1, k, :half]
        neg_re, neg_im = own[0, k, half:], own[1, k, half:]
        up_re = mask[0] * pos_re - mask[1] * pos_im
        up_im = mask[0] * pos_im + mask[1] * pos_re
        down_re = mask[2] * neg_re - mask[3] * neg_im
        down_im = mask[2] * neg_im + mask[3] * neg_re
        even_re = lift(9, up_re + down_re)
        even_im = lift(9, up_im + down_im)
        odd_re = lift(10, up_im - down_im)
        odd_im = lift(10, up_re - down_re)
        re_pos, re_neg = halves(stacked((even_re - odd_re, even_re + odd_re)))
        im_pos, im_neg = halves(stacked((even_im + odd_im, even_im - odd_im)))
        rows_re = jnp.concatenate([re_pos + re_neg, im_neg - im_pos], axis=1)
        rows_im = jnp.concatenate([im_pos + im_neg, re_pos - re_neg], axis=1)
        return [rows_re, rows_im]

    intensity = jnp.zeros((tile, LANES), F32)
    places = [(own, k) for own in spec for k in range(own.shape[1])]
    for first in range(0, kernels, BATCH):
        lines = stacked([line for i in range(BATCH) for line in lifted(*places[first + i])])
        x1, x2, x3 = split3(lines)
        most, more = halves(dot(x1, across[1]))
        some, small = halves(dot(x2, across[1]))
        both = small + dot(x1, across[2]) + dot(x3, across[0]) + (more + some) + most
        for i in range(BATCH):
            real = both[2 * i * tile : (2 * i + 1) * tile]
            imag = both[(2 * i + 1) * tile : (2 * i + 2) * tile]
            field_re[first + i] = real
            field_im[first + i] = imag
            intensity = intensity + weights[first + i] * (real * real + imag * imag)
    intensity = intensity / total_weight(weights, kernels)
    samples = pixels.shape[1]
    row, col = sample_places(pixels[...], tile)
    in_col = lax.broadcasted_iota(jnp.int32, (LANES, samples), 0) == col
    one_hot = jnp.where(in_col, 1.0, 0.0).astype(BF16)
    high, rest = split(intensity)
    low = intensity - high.astype(F32) - rest.astype(F32)
    picked = dot(high, one_hot) + dot(rest, one_hot) + dot(low.astype(BF16), one_hot)
    in_row = lax.broadcasted_iota(jnp.int32, (tile, samples), 0) == row
    own = jnp.sum(jnp.where(in_row, picked, 0.0), axis=0, keepdims=True)
    sampled[...] = jnp.concatenate([own, slopes[...]], axis=1)
    copies[...] = jnp.broadcast_to(sampled[...][None], copies.shape)


def sigmoid(x):
    return 1.0 / (1.0 + jnp.exp(-x))


def errors(intensity, slope, dose):
    resist = 0.5 * jnp.tanh(0.5 * STEEPNESS * (dose * intensity - RESIST_LEVEL))
    offset = resist * slope
    return resist, offset, offset * offset


def own_samples_kernel(doses, sampled, pixels, own_error, chain, in_row, one_hot):
    corners, samples = own_error.shape
    tile = in_row.shape[0]
    own, slope = sampled[:, :samples], sampled[:, samples:]
    which = lax.broadcasted_iota(jnp.int32, (corners, samples), 0)
    dose = jnp.zeros((corners, samples), F32)
    for c in range(corners):
        dose = jnp.where(which == c, doses[c], dose)
    resist, offset, error = errors(own, slope, dose)
    own_error[...] = error
    chain[...] = 2.0 * STEEPNESS * offset * slope * dose * (0.25 - resist * resist)
    row, col = sample_places(pixels[...], tile)
    place = lax.broadcasted_iota(jnp.int32, (tile, samples), 0)
    in_row[...] = jnp.where(place == row, 1.0, 0.0)
    place = lax.broadcasted_iota(jnp.int32, (LANES, samples), 0)
    one_hot[...] = jnp.where(place == col, 1.0, 0.0).T.astype(BF16)


def source_kernel(
    weights, doses, pick, gathered, own_error, chain, in_row, one_hot, placed_sum, tail
):
    kernels = weights.shape[0]
    tile = placed_sum.shape[0]
    samples = own_error.shape[1]
    devices = gathered.shape[0]
    corners = doses.shape[0]
    per_corner = devices * samples
    everyone, every_slope = gathered[:, :samples], gathered[:, samples:]
    pick_corner = pick[0] // per_corner
    remain = pick[0] - pick_corner * per_corner
    place = lax.broadcasted_iota(jnp.int32, (devices, samples), 0) * samples
    place = place + lax.broadcasted_iota(jnp.int32, (devices, samples), 1)
    _, _, picked = errors(everyone, every_slope, doses[pick_corner])
    threshold = jnp.sum(jnp.where(place == remain, picked, 0.0), keepdims=True)

    def corner(c, sums):
        _, _, error = errors(everyone, every_slope, doses[c])
        soft = sigmoid((error - threshold) * (1.0 / SOFTNESS))
        return sums[0] + soft, sums[1] + error * soft

    zero = jnp.zeros((devices, samples), F32)
    soft_sum, error_sum = lax.fori_loop(
        0, corners, corner, (zero, zero), unroll=8 if devices <= 32 else 1
    )
    soft_total = jnp.sum(soft_sum, keepdims=True)
    tail_mean = jnp.sum(error_sum, keepdims=True) / soft_total
    tail[...] = tail_mean

    error = own_error[...]
    soft = sigmoid((error - threshold) * (1.0 / SOFTNESS))
    slope_soft = soft * (1.0 - soft) * (1.0 / SOFTNESS)
    coefficient = (soft + (error - tail_mean) * slope_soft) * (corners * per_corner / soft_total)
    summed = jnp.sum(coefficient * chain[...], axis=0, keepdims=True)
    summed = summed / total_weight(weights, kernels)

    placed = in_row[...] * summed
    tall = dot(stacked(split3(placed)), one_hot[...])
    grid = tall[:tile] + (tall[tile : 2 * tile] + tall[2 * tile :])
    placed_sum[...] = grid


def add_waves(first, weights, grid, field_re, field_im, tables, own, total_re, total_im):
    period = total_re.shape[0]
    half = period // 2
    tile = field_re.shape[1]
    cols = pair(tables, 0, LANES, 2 * LANES)
    cols = (stacked((cols[0], cols[0])), cols[1])
    rows = tile // 2
    cos_rows = tables[6, :half, : 3 * rows]
    sin_rows = tables[6, half:period, : 3 * rows]

    def along_rows(wide):
        out = []
        for table, x in (
            (cos_rows, wide[:rows] + wide[rows:]),
            (sin_rows, wide[:rows] - wide[rows:]),
        ):
            high, low = split(x)
            out.append(dot(table, stacked((high, low, high))))
        return out

    for start in range(0, own.shape[1], BATCH):
        sources = []
        for at in range(start, start + BATCH):
            weighted = grid[...] * weights[first + at]
            sources += [weighted * field_re[first + at], weighted * field_im[first + at]]
        high, low = split(stacked(sources))
        both = dot(jnp.concatenate([high, low], axis=1), cols[0]) + dot(high, cols[1])
        for i in range(BATCH):
            at = start + i
            real_cos, real_sin = halves(both[2 * i * tile : (2 * i + 1) * tile])
            imag_cos, imag_sin = halves(both[(2 * i + 1) * tile : (2 * i + 2) * tile])
            wide_re = jnp.concatenate([real_cos + imag_sin, real_cos - imag_sin], axis=1)
            wide_im = jnp.concatenate([imag_cos - real_sin, imag_cos + real_sin], axis=1)
            cos_re, sin_re = along_rows(wide_re)
            cos_im, sin_im = along_rows(wide_im)
            for begin, sign in ((0, 1.0), (half, -1.0)):
                part = slice(begin, begin + half)
                wave_re = cos_re + sign * sin_im
                wave_im = cos_im - sign * sin_re
                own_re, own_im = own[0, at, part], own[1, at, part]
                total_re[part] += own_re * wave_re + own_im * wave_im
                total_im[part] += own_re * wave_im - own_im * wave_re


def first_waves_kernel(weights, grid, field_re, field_im, tables, own, total_re, total_im):
    total_re[...] = jnp.zeros(total_re.shape, F32)
    total_im[...] = jnp.zeros(total_im.shape, F32)
    add_waves(0, weights, grid, field_re, field_im, tables, own, total_re, total_im)


def gradient_kernel(
    first, weights, grid, field_re, field_im, tables, own, sum_re, sum_im,
    grad, rim, total_re, total_im,
):
    period = grad.shape[0]
    half = period // 2
    tile = field_re.shape[1]
    radius = (period - tile) // 2
    total_re[...] = sum_re[...]
    total_im[...] = sum_im[...]
    add_waves(first, weights, grid, field_re, field_im, tables, own, total_re, total_im)
    pos_re, neg_re = total_re[:half], total_re[half:]
    pos_im, neg_im = total_im[:half], total_im[half:]
    back_rows = pair(tables, 4, period, period)
    back_rows = (back_rows[0], stacked(back_rows))
    for_re = jnp.concatenate([pos_re + neg_re, neg_im - pos_im], axis=0)
    for_im = jnp.concatenate([pos_im + neg_im, pos_re - neg_re], axis=0)
    re_pos, re_neg = halves(dot3_stacked(back_rows, split(for_re)))
    im_pos, im_neg = halves(dot3_stacked(back_rows, split(for_im)))
    last = jnp.concatenate([re_pos + re_neg, im_neg - im_pos], axis=1)
    framed = dot3(split(last), pair(tables, 2, 2 * LANES, period)) * (2.0 / (period * period))
    grad[...] = framed
    lower, _ = place_in_pair("ty")
    rim[...] = jnp.where(lower, framed[:radius], framed[radius + tile :])


VMEM = pl.BlockSpec(memory_space=pltpu.VMEM)
SMEM = pl.BlockSpec(memory_space=pltpu.SMEM)
ANY = pl.BlockSpec(memory_space=pl.ANY)


def shape(*dims):
    return jax.ShapeDtypeStruct(dims, F32)


def call(kernel, name, out_shape, in_specs, scratch=(), aliases=None, micros=1):
    return pl.pallas_call(
        kernel,
        out_shape=out_shape,
        in_specs=in_specs,
        out_specs=[VMEM] * len(out_shape),
        scratch_shapes=scratch,
        input_output_aliases=aliases or {},
        compiler_params=pltpu.CompilerParams(vmem_limit_bytes=10 * 1024 * 1024),
        cost_estimate=pl.CostEstimate(
            flops=micros * 10**9, bytes_accessed=2**20, transcendentals=0
        ),
        name=name,
    )


def gather_all(copies):
    return lax.all_to_all(copies, ("ty", "tx"), 0, 0, tiled=True)


def body(latent, kernels, socs_weights, dose_scale, inv_slope, edge_pixels, threshold_pick):
    tile = latent.shape[0]
    count, taps = kernels.shape[1], kernels.shape[-1]
    samples = edge_pixels.shape[1]
    radius = (taps - 1) // 2
    period = tile + 2 * radius
    half = period // 2
    first_tables = [jnp.asarray(x) for x in spectra_tables(period, taps - 1)]
    tables = jnp.asarray(field_tables(period, tile))
    last_tables = jnp.asarray(gradient_tables(period, tile))
    token = shape(8, LANES)
    packed = shape(tile // 2, 2 * radius)
    devices = lax.axis_size("ty") * lax.axis_size("tx")

    def spectra(start, first_out, parts, size, after, into=()):
        return call(
            functools.partial(spectra_kernel, start, first_out, parts),
            "spectra",
            [shape(2, size, period, 2 * LANES), token],
            [VMEM] * 4 + [ANY] * (1 + len(into)),
            aliases={5: 0} if into else None,
            micros=parts // 2,
        )(kernels, *first_tables, after, *into)

    transmit, done = call(
        own_kernel, "own", [shape(tile, tile), token], [VMEM], micros=3
    )(latent)
    partner, outside = swap("tx", transmit), swap_outside("tx", transmit)
    small, few = count // 3, count // 6
    large = count - small
    spec_a, done = spectra(0, 0, small, small, done)
    band, done = call(
        band_kernel, "band", [shape(tile, period), token], [VMEM] * 3 + [ANY]
    )(transmit, partner, outside, done)
    partner = swap("ty", band)
    spec_b, done = spectra(small, 0, few, large, done)
    rim, done = call(
        relay_rows_kernel, "relay", [shape(radius, period), token], [VMEM, ANY]
    )(partner, done)
    rim = ring("ty", rim)
    spec_b, _ = spectra(small + few, few, large - few, large, done, (spec_b,))
    spec = [spec_a, spec_b]

    field_re, field_im, sampled, copies = call(
        field_kernel,
        "field",
        [shape(count, tile, LANES)] * 2
        + [shape(1, 2 * samples), shape(devices, 1, 2 * samples)],
        [SMEM] + [VMEM] * (6 + len(spec)),
        scratch=[
            pltpu.VMEM((period, period), F32),
            pltpu.VMEM((4, half, 2 * LANES), F32),
        ],
        micros=7,
    )(socs_weights, band, partner, rim, edge_pixels, inv_slope, tables, *spec)

    gathered = gather_all(copies).reshape(devices, 2 * samples)
    corners = dose_scale.shape[0]
    own = call(
        own_samples_kernel,
        "samples",
        [shape(corners, samples)] * 2
        + [shape(tile, samples), jax.ShapeDtypeStruct((samples, LANES), BF16)],
        [SMEM] + [VMEM] * 2,
        micros=2,
    )(dose_scale, sampled, edge_pixels)
    grid, tail_mean = call(
        source_kernel,
        "source",
        [shape(tile, LANES), shape(1, 1)],
        [SMEM] * 3 + [VMEM] * 5,
        micros=2,
    )(socs_weights, dose_scale, threshold_pick, gathered, *own)
    known = (socs_weights, grid, field_re, field_im, last_tables)
    sums = call(
        first_waves_kernel,
        "waves",
        [shape(period, 2 * LANES)] * 2,
        [SMEM] + [VMEM] * 5,
        micros=2,
    )(*known, spec_a)
    grad, rim = call(
        functools.partial(gradient_kernel, small),
        "gradient",
        [shape(period, period), shape(radius, period)],
        [SMEM] + [VMEM] * 7,
        scratch=[pltpu.VMEM((period, 2 * LANES), F32)] * 2,
        micros=5,
    )(*known, spec_b, *sums)

    rim = ring("ty", rim, back=True)
    (partner,) = call(fold_rows_kernel, "fold", [shape(tile, period)], [VMEM] * 2)(
        grad, rim
    )
    partner = swap("ty", partner)
    band, far = call(
        fold_band_kernel, "fold", [shape(tile, period), packed], [VMEM] * 2
    )(grad, partner)
    far = swap_outside("tx", far)
    (near,) = call(near_rim_kernel, "near", [packed], [VMEM])(band)
    near = swap("tx", near)
    (total,) = call(far_side_kernel, "far", [shape(tile, tile)], [VMEM] * 2)(band, far)
    (steering,) = call(finish_kernel, "finish", [shape(tile, tile)], [VMEM] * 3)(
        total, near, latent
    )
    return (steering, tail_mean.reshape(1))


def solution(mesh):
    placed = (P("ty", "tx"), P(), P(), P(), P("ty", "tx"), P("ty", "tx"), P())
    return jax.shard_map(
        body, mesh=mesh, in_specs=placed, out_specs=(P("ty", "tx"), P()), check_vma=False
    )
```

```python
import functools
import math

import jax
import jax.numpy as jnp
import ml_dtypes
import numpy as np
from jax import lax
from jax.experimental import pallas as pl
from jax.experimental.pallas import tpu as pltpu
from jax.sharding import PartitionSpec as P

STEEPNESS = 4.0
RESIST_LEVEL = 0.7
SOFTNESS = 0.25
LANES = 128
BATCH = 6
F32 = jnp.float32
BF16 = jnp.bfloat16


def split(x):
    high = x.astype(BF16)
    return high, (x - high.astype(F32)).astype(BF16)


def split3(x):
    first = x.astype(BF16)
    rest = x - first.astype(F32)
    second = rest.astype(BF16)
    return first, second, (rest - second.astype(F32)).astype(BF16)


def table_parts(table):
    parts = []
    for _ in range(3):
        parts.append(table.astype(ml_dtypes.bfloat16))
        table = table - parts[-1].astype(np.float64)
    return parts


def dot(a, b):
    return jnp.dot(a, b, preferred_element_type=F32)


def dot3(a, b):
    return dot(a[0], b[0]) + dot(a[0], b[1]) + dot(a[1], b[0])


def stacked(pair):
    return jnp.concatenate(pair, axis=0)


def dot6(a, b):
    small = dot(a[0], b[2]) + dot(a[1], b[1]) + dot(a[2], b[0])
    return small + (dot(a[0], b[1]) + dot(a[1], b[0])) + dot(a[0], b[0])


def dot3_stacked(a, b):
    high, both = a
    count = high.shape[0]
    tall = dot(both, b[0])
    return tall[:count] + tall[count:] + dot(high, b[1])


def waves(period, places):
    turn = (np.arange(period // 2) + 0.5) * (2.0 * math.pi / period)
    angle = turn[:, None] * places[None, :]
    return np.cos(angle), np.sin(angle)


def wave_table(period, places, by_lane=False):
    half = period // 2
    out = np.zeros((2 * LANES, 2 * LANES))
    for first, table in zip((0, LANES if by_lane else half), waves(period, places)):
        out[first : first + half, : len(places)] = table
    return out


def spectra_tables(period, last):
    taps = np.arange(last + 1)
    wide = wave_table(period, taps, True)
    tall = wave_table(period, taps)
    c1, c2, c3 = (part[:, :last].T for part in table_parts(wide))
    lanes = np.stack([np.concatenate(two) for two in ((c1, c1), (c2, c2), (c1, c3))])
    c1, c2, c3 = (part[:period, :last] for part in table_parts(tall))
    rows = [np.concatenate(two, axis=1) for two in ((c1, c1), (c2, c2), (c1, c3))]
    ends = np.zeros((period + 8, 2 * LANES), np.float32)
    ends[:period] = tall[:period, last : last + 1]
    ends[period] = wide[:, last]
    return lanes, np.concatenate(rows), ends


def field_tables(period, tile):
    half, rows = period // 2, tile // 2
    place = np.arange(period)
    wide = table_parts(wave_table(period, place, True))
    centred = table_parts(wave_table(period, place - (tile - 1) / 2))
    out = [part.T for part in wide] + centred + wide
    for table in waves(period, np.arange(rows) + 0.5):
        c1, c2, c3 = table_parts(table.T)
        slot = np.zeros((2 * LANES, 2 * LANES), ml_dtypes.bfloat16)
        for i, two in enumerate(((c1, c1), (c2, c2), (c3, 0 * c3), (c1, 0 * c1))):
            slot[i * rows : (i + 1) * rows, :period] = np.concatenate(two, axis=1)
        out.append(slot)
    return np.stack(out)


def gradient_tables(period, tile):
    half, rows = period // 2, tile // 2
    place = np.arange(period)
    wide = table_parts(wave_table(period, place, True))[:2]
    centred = table_parts(wave_table(period, place - (tile - 1) / 2))[:2]
    slot = np.zeros((2 * LANES, 2 * LANES), ml_dtypes.bfloat16)
    for i, table in enumerate(waves(period, np.arange(rows) + 0.5)):
        high, low, _ = table_parts(table)
        slot[i * half : (i + 1) * half, : 3 * rows] = np.concatenate([high, high, low], axis=1)
    return np.stack([part.T for part in wide] + wide + [part.T for part in centred] + [slot])


def pair(tables, first, rows, cols):
    return tables[first, :rows, :cols], tables[first + 1, :rows, :cols]


def triple(tables, first, rows, cols):
    return [tables[first + i, :rows, :cols] for i in range(3)]


def halves(x):
    return x[:, :LANES], x[:, LANES:]


def place_in_pair(axis):
    index, count = lax.axis_index(axis), lax.axis_size(axis)
    lower = lax.rem(index, 2) == 0
    return lower, jnp.where(lower, index > 0, index < count - 1)


def swap(axis, x):
    return lax.ppermute(x, axis, [(i, i ^ 1) for i in range(lax.axis_size(axis))])


def swap_outside(axis, x):
    count = lax.axis_size(axis)
    pairs = [(0, 0), (count - 1, count - 1)]
    for low in range(1, count - 1, 2):
        pairs += [(low, low + 1), (low + 1, low)]
    return lax.ppermute(x, axis, pairs)


def ring(axis, x, back=False):
    count = lax.axis_size(axis)
    cycle = list(range(0, count, 2)) + list(range(count - 1, 0, -2))
    pairs = list(zip(cycle, cycle[1:] + cycle[:1]))
    return lax.ppermute(x, axis, [(b, a) if back else (a, b) for a, b in pairs])


def spectra_kernel(start, first_out, parts, kern, lanes, rows, ends, *rest):
    out, token = rest[-2:]
    period = out.shape[2]
    half = period // 2
    last = kern.shape[-1] - 1
    end_row = ends[period : period + 1]
    token[...] = jnp.zeros(token.shape, F32)

    def along_lanes(planes):
        main = stacked([plane[:last] for plane in planes])
        tail = stacked([plane[last:] for plane in planes])
        tail = jnp.concatenate([tail, jnp.zeros((-tail.shape[0] % 16, last + 1), F32)], axis=0)
        both = stacked((main, tail))
        x1, x2, x3 = split3(both[:, :last])
        most = jnp.concatenate([x1, x2], axis=1)
        out = dot(jnp.concatenate([x3, x1], axis=1), lanes[2]) + dot(most, lanes[1])
        out = out + dot(most, lanes[0]) + both[:, last:] * end_row
        first = len(planes) * last
        return [
            (out[i * last : (i + 1) * last], out[first + i : first + i + 1])
            for i in range(len(planes))
        ]

    def along_rows(wide, tail):
        x1, x2, x3 = split3(wide)
        tall = dot(rows[: 2 * period], stacked((x1, x2)))
        small = dot(rows[2 * period :], stacked((x3, x1)))
        return tall[:period] + (tall[period:] + small) + ends[:period] * tail

    def mixed(real, imag):
        real_cos, real_sin = halves(real)
        imag_cos, imag_sin = halves(imag)
        return (
            jnp.concatenate([real_cos - imag_sin, real_cos + imag_sin], axis=1),
            jnp.concatenate([real_sin + imag_cos, imag_cos - real_sin], axis=1),
        )

    planes = along_lanes([kern[c, start + k] for k in range(parts) for c in range(2)])
    for k in range(parts):
        to = first_out + k
        (real, real_tail), (imag, imag_tail) = planes[2 * k : 2 * k + 2]
        wide_re, wide_im = mixed(real, imag)
        tail_re, tail_im = mixed(real_tail, imag_tail)
        tall_re = along_rows(wide_re, tail_re)
        tall_im = along_rows(wide_im, tail_im)
        out[0, to, :half] = tall_re[:half] - tall_im[half:]
        out[0, to, half:] = tall_re[:half] + tall_im[half:]
        out[1, to, :half] = tall_im[:half] + tall_re[half:]
        out[1, to, half:] = tall_im[:half] - tall_re[half:]


def pack(x):
    count = x.shape[0] // 2
    return jnp.concatenate([x[:count], x[count:]], axis=1)


def unpack(x):
    width = x.shape[1] // 2
    return jnp.concatenate([x[:, :width], x[:, width:]], axis=0)


def own_kernel(latent, transmit, token):
    transmit[...] = 0.5 * (1.0 + jnp.tanh(latent[...]))
    token[...] = jnp.zeros(token.shape, F32)


def band_kernel(middle, partner, outside, after, band, token):
    tile = middle.shape[0]
    radius = (band.shape[1] - tile) // 2
    lower, other = place_in_pair("tx")

    near = jnp.where(lower, partner[:, :radius], partner[:, tile - radius :])
    far = jnp.where(lower, outside[:, tile - radius :], outside[:, :radius])
    far = jnp.where(other, far, 0.0)
    band[:, :radius] = jnp.where(lower, far, near)
    band[:, radius : radius + tile] = middle[...]
    band[:, radius + tile :] = jnp.where(lower, near, far)
    token[...] = jnp.zeros(token.shape, F32)


def relay_rows_kernel(partner, after, rim, token):
    radius = rim.shape[0]
    tile = partner.shape[0]
    lower, _ = place_in_pair("ty")
    rim[...] = jnp.where(lower, partner[tile - radius :], partner[:radius])
    token[...] = jnp.zeros(token.shape, F32)


def fold_rows_kernel(grad, rim, out):
    radius = rim.shape[0]
    tile = out.shape[0]
    lower, _ = place_in_pair("ty")
    count, index = lax.axis_size("ty"), lax.axis_index("ty")
    comes = jnp.where(lower, index < count - 2, index > 1)
    outer = jnp.where(comes, rim[...], 0.0)
    top = jnp.where(lower, grad[radius + tile :], outer)
    bottom = jnp.where(lower, outer, grad[:radius])
    out[:radius] = top
    out[radius:] = jnp.zeros((tile - radius, out.shape[1]), F32)
    out[tile - radius :] += bottom


def fold_band_kernel(grad, partner, band, far):
    tile = band.shape[0]
    radius = far.shape[1] // 2
    lower, _ = place_in_pair("tx")
    band[...] = grad[radius : radius + tile] + partner[...]
    far[...] = jnp.where(lower, pack(band[:, :radius]), pack(band[:, radius + tile :]))


def near_rim_kernel(band, near):
    tile = band.shape[0]
    radius = near.shape[1] // 2
    lower, _ = place_in_pair("tx")
    near[...] = jnp.where(lower, pack(band[:, radius + tile :]), pack(band[:, :radius]))


def far_side_kernel(band, far, out):
    tile = out.shape[0]
    radius = (band.shape[1] - tile) // 2
    lower, other = place_in_pair("tx")
    outer = jnp.where(other, unpack(far[...]), 0.0)
    out[...] = band[:, radius : radius + tile]
    out[:, :radius] += jnp.where(lower, outer, 0.0)
    out[:, tile - radius :] += jnp.where(lower, 0.0, outer)


def finish_kernel(total, near, latent, steering):
    tile = latent.shape[0]
    radius = near.shape[1] // 2
    lower, _ = place_in_pair("tx")
    inner = unpack(near[...])
    steering[...] = total[...]
    steering[:, :radius] += jnp.where(lower, 0.0, inner)
    steering[:, tile - radius :] += jnp.where(lower, inner, 0.0)
    value = jnp.tanh(latent[...])
    steering[...] = steering[...] * 0.5 * (1.0 - value * value)


def total_weight(weights, kernels):
    total = weights[0]
    for k in range(1, kernels):
        total = total + weights[k]
    return jnp.full((1, 1), total, F32)


def sample_places(pixels, tile):
    row = ((pixels.astype(F32) + 0.5) * (1.0 / tile)).astype(jnp.int32)
    held = jnp.where(row < tile // 2, tile - 1 - row, row - tile // 2)
    return held, pixels - row * tile


def field_kernel(weights, band, partner, rim, pixels, slopes, tables, *rest):
    *spec, field_re, field_im, sampled, copies, framed, mask = rest
    kernels = weights.shape[0]
    period = band.shape[1]
    half = period // 2
    tile = field_re.shape[1]
    radius = rim.shape[0]
    lower, other = place_in_pair("ty")
    outer = jnp.where(other, rim[...], 0.0)
    framed[:radius] = jnp.where(lower, outer, partner[tile - radius :])
    framed[radius + tile :] = jnp.where(lower, partner[:radius], outer)
    framed[radius : radius + tile] = band[...]
    wide = dot6(split3(framed[...]), triple(tables, 0, period, 2 * LANES))
    tall = dot6(triple(tables, 3, period, period), split3(wide)) * (1.0 / (period * period))
    cos_cos, cos_sin = halves(tall[:half])
    sin_cos, sin_sin = halves(tall[half:])
    same, other = cos_cos - sin_sin, cos_cos + sin_sin
    joint, cross = sin_cos + cos_sin, sin_cos - cos_sin
    mask[0, :, :LANES], mask[0, :, LANES:] = same, other
    mask[1, :, :LANES], mask[1, :, LANES:] = -joint, -cross
    mask[2, :, :LANES], mask[2, :, LANES:] = other, same
    mask[3, :, :LANES], mask[3, :, LANES:] = cross, joint
    rows = tile // 2

    def lift(slot, x):
        x1, x2, x3 = split3(x)
        out = dot(tables[slot, : 3 * rows, :period], stacked((x1, x2)))
        small = dot(tables[slot, 3 * rows : 4 * rows, :half], x3)
        return out[:rows] + (out[rows:tile] + (out[tile:] + small))

    across = triple(tables, 6, 2 * LANES, LANES)
    across = (across[0], jnp.concatenate(across[:2], axis=1), across[2])

    def lifted(own, k):
        pos_re, pos_im = own[0, k, :half], own[1, k, :half]
        neg_re, neg_im = own[0, k, half:], own[1, k, half:]
        up_re = mask[0] * pos_re - mask[1] * pos_im
        up_im = mask[0] * pos_im + mask[1] * pos_re
        down_re = mask[2] * neg_re - mask[3] * neg_im
        down_im = mask[2] * neg_im + mask[3] * neg_re
        even_re = lift(9, up_re + down_re)
        even_im = lift(9, up_im + down_im)
        odd_re = lift(10, up_im - down_im)
        odd_im = lift(10, up_re - down_re)
        re_pos, re_neg = halves(stacked((even_re - odd_re, even_re + odd_re)))
        im_pos, im_neg = halves(stacked((even_im + odd_im, even_im - odd_im)))
        rows_re = jnp.concatenate([re_pos + re_neg, im_neg - im_pos], axis=1)
        rows_im = jnp.concatenate([im_pos + im_neg, re_pos - re_neg], axis=1)
        return [rows_re, rows_im]

    intensity = jnp.zeros((tile, LANES), F32)
    places = [(own, k) for own in spec for k in range(own.shape[1])]
    for first in range(0, kernels, BATCH):
        lines = stacked([line for i in range(BATCH) for line in lifted(*places[first + i])])
        x1, x2, x3 = split3(lines)
        leading = dot(stacked((x1, x2)), across[1])
        most, more = halves(leading[: x1.shape[0]])
        some, small = halves(leading[x1.shape[0] :])
        both = small + dot(x1, across[2]) + dot(x3, across[0]) + (more + some) + most
        for i in range(BATCH):
            real = both[2 * i * tile : (2 * i + 1) * tile]
            imag = both[(2 * i + 1) * tile : (2 * i + 2) * tile]
            field_re[first + i] = real
            field_im[first + i] = imag
            intensity = intensity + weights[first + i] * (real * real + imag * imag)
    intensity = intensity / total_weight(weights, kernels)
    samples = pixels.shape[1]
    row, col = sample_places(pixels[...], tile)
    in_col = lax.broadcasted_iota(jnp.int32, (LANES, samples), 0) == col
    one_hot = jnp.where(in_col, 1.0, 0.0).astype(BF16)
    high, rest = split(intensity)
    low = intensity - high.astype(F32) - rest.astype(F32)
    picked = dot(high, one_hot) + dot(rest, one_hot) + dot(low.astype(BF16), one_hot)
    in_row = lax.broadcasted_iota(jnp.int32, (tile, samples), 0) == row
    own = jnp.sum(jnp.where(in_row, picked, 0.0), axis=0, keepdims=True)
    sampled[...] = jnp.concatenate([own, slopes[...]], axis=1)
    copies[...] = jnp.broadcast_to(sampled[...][None], copies.shape)


def sigmoid(x):
    return 1.0 / (1.0 + jnp.exp(-x))


def errors(intensity, slope, dose):
    resist = 0.5 * jnp.tanh(0.5 * STEEPNESS * (dose * intensity - RESIST_LEVEL))
    offset = resist * slope
    return resist, offset, offset * offset


def source_kernel(weights, doses, pick, gathered, sampled, pixels, placed_sum, tail):
    kernels = weights.shape[0]
    tile = placed_sum.shape[0]
    samples = pixels.shape[1]
    devices = gathered.shape[0]
    corners = doses.shape[0]
    per_corner = devices * samples
    everyone, every_slope = gathered[:, :samples], gathered[:, samples:]
    pick_corner = pick[0] // per_corner
    remain = pick[0] - pick_corner * per_corner
    place = lax.broadcasted_iota(jnp.int32, (devices, samples), 0) * samples
    place = place + lax.broadcasted_iota(jnp.int32, (devices, samples), 1)
    _, _, picked = errors(everyone, every_slope, doses[pick_corner])
    threshold = jnp.sum(jnp.where(place == remain, picked, 0.0), keepdims=True)

    def corner(c, sums):
        _, _, error = errors(everyone, every_slope, doses[c])
        soft = sigmoid((error - threshold) * (1.0 / SOFTNESS))
        return sums[0] + soft, sums[1] + error * soft

    zero = jnp.zeros((devices, samples), F32)
    soft_sum, error_sum = lax.fori_loop(
        0, corners, corner, (zero, zero), unroll=8 if devices <= 32 else 1
    )
    soft_total = jnp.sum(soft_sum, keepdims=True)
    tail_mean = jnp.sum(error_sum, keepdims=True) / soft_total
    tail[...] = tail_mean

    own, slope = sampled[:, :samples], sampled[:, samples:]
    which = lax.broadcasted_iota(jnp.int32, (corners, samples), 0)
    dose = jnp.zeros((corners, samples), F32)
    for c in range(corners):
        dose = jnp.where(which == c, doses[c], dose)
    resist, offset, error = errors(own, slope, dose)
    soft = sigmoid((error - threshold) * (1.0 / SOFTNESS))
    slope_soft = soft * (1.0 - soft) * (1.0 / SOFTNESS)
    chain = 2.0 * STEEPNESS * offset * slope * dose * (0.25 - resist * resist)
    coefficient = (soft + (error - tail_mean) * slope_soft) * (corners * per_corner / soft_total)
    summed = jnp.sum(coefficient * chain, axis=0, keepdims=True)
    summed = summed / total_weight(weights, kernels)

    row, col = sample_places(pixels[...], tile)
    in_row = lax.broadcasted_iota(jnp.int32, (tile, samples), 0) == row
    in_col = lax.broadcasted_iota(jnp.int32, (LANES, samples), 0) == col
    one_hot = jnp.where(in_col, 1.0, 0.0).astype(BF16)
    placed = jnp.where(in_row, summed, 0.0)
    high, rest = split(placed)
    low = (placed - high.astype(F32) - rest.astype(F32)).astype(BF16)
    grid = jnp.zeros((tile, LANES), F32)
    for part in (high, rest, low):
        grid = grid + lax.dot_general(
            part, one_hot, (((1,), (1,)), ((), ())), preferred_element_type=F32
        )

    placed_sum[...] = grid


def gradient_kernel(weights, grid, field_re, field_im, tables, *rest):
    *spec, grad, rim, total_re, total_im = rest
    period = grad.shape[0]
    half = period // 2
    tile = field_re.shape[1]
    radius = (period - tile) // 2
    cols = pair(tables, 0, LANES, 2 * LANES)
    cols = (stacked((cols[0], cols[0])), cols[1])
    rows = tile // 2
    cos_rows = tables[6, :half, : 3 * rows]
    sin_rows = tables[6, half:period, : 3 * rows]

    def along_rows(wide):
        out = []
        for table, x in (
            (cos_rows, wide[:rows] + wide[rows:]),
            (sin_rows, wide[:rows] - wide[rows:]),
        ):
            high, low = split(x)
            out.append(dot(table, stacked((high, low, high))))
        return out

    total_re[...] = jnp.zeros((period, 2 * LANES), F32)
    total_im[...] = jnp.zeros((period, 2 * LANES), F32)

    places = [(own, k) for own in spec for k in range(own.shape[1])]
    for group in range(len(places) // BATCH):
        sources = []
        for i in range(BATCH):
            k = group * BATCH + i
            weighted = grid[...] * weights[k]
            sources += [weighted * field_re[k], weighted * field_im[k]]
        high, low = split(stacked(sources))
        both = dot(jnp.concatenate([high, low], axis=1), cols[0]) + dot(high, cols[1])
        for i in range(BATCH):
            own, at = places[group * BATCH + i]
            real_cos, real_sin = halves(both[2 * i * tile : (2 * i + 1) * tile])
            imag_cos, imag_sin = halves(both[(2 * i + 1) * tile : (2 * i + 2) * tile])
            wide_re = jnp.concatenate([real_cos + imag_sin, real_cos - imag_sin], axis=1)
            wide_im = jnp.concatenate([imag_cos - real_sin, imag_cos + real_sin], axis=1)
            cos_re, sin_re = along_rows(wide_re)
            cos_im, sin_im = along_rows(wide_im)
            for start, sign in ((0, 1.0), (half, -1.0)):
                part = slice(start, start + half)
                wave_re = cos_re + sign * sin_im
                wave_im = cos_im - sign * sin_re
                own_re, own_im = own[0, at, part], own[1, at, part]
                total_re[part] += own_re * wave_re + own_im * wave_im
                total_im[part] += own_re * wave_im - own_im * wave_re

    pos_re, neg_re = total_re[:half], total_re[half:]
    pos_im, neg_im = total_im[:half], total_im[half:]
    back_rows = pair(tables, 4, period, period)
    back_rows = (back_rows[0], stacked(back_rows))
    for_re = jnp.concatenate([pos_re + neg_re, neg_im - pos_im], axis=0)
    for_im = jnp.concatenate([pos_im + neg_im, pos_re - neg_re], axis=0)
    re_pos, re_neg = halves(dot3_stacked(back_rows, split(for_re)))
    im_pos, im_neg = halves(dot3_stacked(back_rows, split(for_im)))
    last = jnp.concatenate([re_pos + re_neg, im_neg - im_pos], axis=1)
    framed = dot3(split(last), pair(tables, 2, 2 * LANES, period)) * (2.0 / (period * period))
    grad[...] = framed
    lower, _ = place_in_pair("ty")
    rim[...] = jnp.where(lower, framed[:radius], framed[radius + tile :])


VMEM = pl.BlockSpec(memory_space=pltpu.VMEM)
SMEM = pl.BlockSpec(memory_space=pltpu.SMEM)
ANY = pl.BlockSpec(memory_space=pl.ANY)


def shape(*dims):
    return jax.ShapeDtypeStruct(dims, F32)


def call(kernel, name, out_shape, in_specs, scratch=(), aliases=None, micros=1):
    return pl.pallas_call(
        kernel,
        out_shape=out_shape,
        in_specs=in_specs,
        out_specs=[VMEM] * len(out_shape),
        scratch_shapes=scratch,
        input_output_aliases=aliases or {},
        compiler_params=pltpu.CompilerParams(vmem_limit_bytes=10 * 1024 * 1024),
        cost_estimate=pl.CostEstimate(
            flops=micros * 10**9, bytes_accessed=2**20, transcendentals=0
        ),
        name=name,
    )


def gather_all(copies):
    return lax.all_to_all(copies, ("ty", "tx"), 0, 0, tiled=True)


def body(latent, kernels, socs_weights, dose_scale, inv_slope, edge_pixels, threshold_pick):
    tile = latent.shape[0]
    count, taps = kernels.shape[1], kernels.shape[-1]
    samples = edge_pixels.shape[1]
    radius = (taps - 1) // 2
    period = tile + 2 * radius
    half = period // 2
    first_tables = [jnp.asarray(x) for x in spectra_tables(period, taps - 1)]
    tables = jnp.asarray(field_tables(period, tile))
    last_tables = jnp.asarray(gradient_tables(period, tile))
    token = shape(8, LANES)
    packed = shape(tile // 2, 2 * radius)
    devices = lax.axis_size("ty") * lax.axis_size("tx")

    def spectra(start, first_out, parts, size, after, into=()):
        return call(
            functools.partial(spectra_kernel, start, first_out, parts),
            "spectra",
            [shape(2, size, period, 2 * LANES), token],
            [VMEM] * 4 + [ANY] * (1 + len(into)),
            aliases={5: 0} if into else None,
            micros=parts // 2,
        )(kernels, *first_tables, after, *into)

    transmit, done = call(
        own_kernel, "own", [shape(tile, tile), token], [VMEM], micros=3
    )(latent)
    partner, outside = swap("tx", transmit), swap_outside("tx", transmit)
    small, few = count // 3, count // 6
    large = count - small
    spec_a, done = spectra(0, 0, small, small, done)
    band, done = call(
        band_kernel, "band", [shape(tile, period), token], [VMEM] * 3 + [ANY]
    )(transmit, partner, outside, done)
    partner = swap("ty", band)
    spec_b, done = spectra(small, 0, few, large, done)
    rim, done = call(
        relay_rows_kernel, "relay", [shape(radius, period), token], [VMEM, ANY]
    )(partner, done)
    rim = ring("ty", rim)
    spec_b, _ = spectra(small + few, few, large - few, large, done, (spec_b,))
    spec = [spec_a, spec_b]

    field_re, field_im, sampled, copies = call(
        field_kernel,
        "field",
        [shape(count, tile, LANES)] * 2
        + [shape(1, 2 * samples), shape(devices, 1, 2 * samples)],
        [SMEM] + [VMEM] * (6 + len(spec)),
        scratch=[
            pltpu.VMEM((period, period), F32),
            pltpu.VMEM((4, half, 2 * LANES), F32),
        ],
        micros=7,
    )(socs_weights, band, partner, rim, edge_pixels, inv_slope, tables, *spec)

    gathered = gather_all(copies).reshape(devices, 2 * samples)
    grid, tail_mean = call(
        source_kernel,
        "source",
        [shape(tile, LANES), shape(1, 1)],
        [SMEM] * 3 + [VMEM] * 3,
        micros=2,
    )(socs_weights, dose_scale, threshold_pick, gathered, sampled, edge_pixels)
    grad, rim = call(
        gradient_kernel,
        "gradient",
        [shape(period, period), shape(radius, period)],
        [SMEM] + [VMEM] * (4 + len(spec)),
        scratch=[pltpu.VMEM((period, 2 * LANES), F32)] * 2,
        micros=6,
    )(socs_weights, grid, field_re, field_im, last_tables, *spec)

    rim = ring("ty", rim, back=True)
    (partner,) = call(fold_rows_kernel, "fold", [shape(tile, period)], [VMEM] * 2)(
        grad, rim
    )
    partner = swap("ty", partner)
    band, far = call(
        fold_band_kernel, "fold", [shape(tile, period), packed], [VMEM] * 2
    )(grad, partner)
    far = swap_outside("tx", far)
    (near,) = call(near_rim_kernel, "near", [packed], [VMEM])(band)
    near = swap("tx", near)
    (total,) = call(far_side_kernel, "far", [shape(tile, tile)], [VMEM] * 2)(band, far)
    (steering,) = call(finish_kernel, "finish", [shape(tile, tile)], [VMEM] * 3)(
        total, near, latent
    )
    return (steering, tail_mean.reshape(1))


def solution(mesh):
    placed = (P("ty", "tx"), P(), P(), P(), P("ty", "tx"), P("ty", "tx"), P())
    return jax.shard_map(
        body, mesh=mesh, in_specs=placed, out_specs=(P("ty", "tx"), P()), check_vma=False
    )
```

```python
import functools
import math

import jax
import jax.numpy as jnp
import ml_dtypes
import numpy as np
from jax import lax
from jax.experimental import pallas as pl
from jax.experimental.pallas import tpu as pltpu
from jax.sharding import PartitionSpec as P

STEEPNESS = 4.0
RESIST_LEVEL = 0.7
SOFTNESS = 0.25
LANES = 128
BATCH = 4
FIELD_BATCH = 2
F32 = jnp.float32
BF16 = jnp.bfloat16


def split(x):
    high = x.astype(BF16)
    return high, (x - high.astype(F32)).astype(BF16)


def split3(x):
    first = x.astype(BF16)
    rest = x - first.astype(F32)
    second = rest.astype(BF16)
    return first, second, (rest - second.astype(F32)).astype(BF16)


def table_parts(table):
    parts = []
    for _ in range(3):
        parts.append(table.astype(ml_dtypes.bfloat16))
        table = table - parts[-1].astype(np.float64)
    return parts


def dot(a, b):
    return jnp.dot(a, b, preferred_element_type=F32)


def dot3(a, b):
    return dot(a[0], b[0]) + dot(a[0], b[1]) + dot(a[1], b[0])


def stacked(pair):
    return jnp.concatenate(pair, axis=0)


def dot6(a, b):
    small = dot(a[0], b[2]) + dot(a[1], b[1]) + dot(a[2], b[0])
    return small + (dot(a[0], b[1]) + dot(a[1], b[0])) + dot(a[0], b[0])


def dot3_stacked(a, b):
    high, both = a
    count = high.shape[0]
    tall = dot(both, b[0])
    return tall[:count] + tall[count:] + dot(high, b[1])


def waves(period, places):
    turn = (np.arange(period // 2) + 0.5) * (2.0 * math.pi / period)
    angle = turn[:, None] * places[None, :]
    return np.cos(angle), np.sin(angle)


def wave_table(period, places, by_lane=False):
    half = period // 2
    out = np.zeros((2 * LANES, 2 * LANES))
    for first, table in zip((0, LANES if by_lane else half), waves(period, places)):
        out[first : first + half, : len(places)] = table
    return out


def spectra_tables(period, last):
    taps = np.arange(last + 1)
    wide = wave_table(period, taps, True)
    tall = wave_table(period, taps)
    c1, c2, c3 = (part[:, :last].T for part in table_parts(wide))
    lanes = np.stack([np.concatenate(two) for two in ((c1, c1), (c2, c2), (c1, c3))])
    c1, c2, c3 = (part[:period, :last] for part in table_parts(tall))
    rows = [np.concatenate(two, axis=1) for two in ((c1, c1), (c2, c2), (c1, c3))]
    ends = np.zeros((period + 8, 2 * LANES), np.float32)
    ends[:period] = tall[:period, last : last + 1]
    ends[period] = wide[:, last]
    return lanes, np.concatenate(rows), ends


def field_tables(period, tile):
    half, rows = period // 2, tile // 2
    place = np.arange(period)
    wide = table_parts(wave_table(period, place, True))
    centred = table_parts(wave_table(period, place - (tile - 1) / 2))
    out = [part.T for part in wide] + centred + wide
    for table in waves(period, np.arange(rows) + 0.5):
        c1, c2, c3 = table_parts(table.T)
        slot = np.zeros((2 * LANES, 2 * LANES), ml_dtypes.bfloat16)
        for i, two in enumerate(((c1, c1), (c2, c2), (c3, 0 * c3), (c1, 0 * c1))):
            slot[i * rows : (i + 1) * rows, :period] = np.concatenate(two, axis=1)
        out.append(slot)
    return np.stack(out)


def gradient_tables(period, tile):
    half, rows = period // 2, tile // 2
    place = np.arange(period)
    wide = table_parts(wave_table(period, place, True))[:2]
    centred = table_parts(wave_table(period, place - (tile - 1) / 2))[:2]
    slot = np.zeros((2 * LANES, 2 * LANES), ml_dtypes.bfloat16)
    for i, table in enumerate(waves(period, np.arange(rows) + 0.5)):
        high, low, _ = table_parts(table)
        slot[i * half : (i + 1) * half, : 3 * rows] = np.concatenate([high, high, low], axis=1)
    return np.stack([part.T for part in wide] + wide + [part.T for part in centred] + [slot])


def pair(tables, first, rows, cols):
    return tables[first, :rows, :cols], tables[first + 1, :rows, :cols]


def triple(tables, first, rows, cols):
    return [tables[first + i, :rows, :cols] for i in range(3)]


def halves(x):
    return x[:, :LANES], x[:, LANES:]


def place_in_pair(axis):
    index, count = lax.axis_index(axis), lax.axis_size(axis)
    lower = lax.rem(index, 2) == 0
    return lower, jnp.where(lower, index > 0, index < count - 1)


def swap(axis, x):
    return lax.ppermute(x, axis, [(i, i ^ 1) for i in range(lax.axis_size(axis))])


def swap_outside(axis, x):
    count = lax.axis_size(axis)
    pairs = [(0, 0), (count - 1, count - 1)]
    for low in range(1, count - 1, 2):
        pairs += [(low, low + 1), (low + 1, low)]
    return lax.ppermute(x, axis, pairs)


def ring(axis, x, back=False):
    count = lax.axis_size(axis)
    cycle = list(range(0, count, 2)) + list(range(count - 1, 0, -2))
    pairs = list(zip(cycle, cycle[1:] + cycle[:1]))
    return lax.ppermute(x, axis, [(b, a) if back else (a, b) for a, b in pairs])


def spectra_kernel(start, first_out, parts, kern, lanes, rows, ends, *rest):
    out, token = rest[-2:]
    period = out.shape[2]
    half = period // 2
    last = kern.shape[-1] - 1
    end_row = ends[period : period + 1]
    token[...] = jnp.zeros(token.shape, F32)

    def along_lanes(planes):
        main = stacked([plane[:last] for plane in planes])
        tail = stacked([plane[last:] for plane in planes])
        tail = jnp.concatenate([tail, jnp.zeros((-tail.shape[0] % 16, last + 1), F32)], axis=0)
        both = stacked((main, tail))
        x1, x2, x3 = split3(both[:, :last])
        most = jnp.concatenate([x1, x2], axis=1)
        out = dot(jnp.concatenate([x3, x1], axis=1), lanes[2]) + dot(most, lanes[1])
        out = out + dot(most, lanes[0]) + both[:, last:] * end_row
        first = len(planes) * last
        return [
            (out[i * last : (i + 1) * last], out[first + i : first + i + 1])
            for i in range(len(planes))
        ]

    def along_rows(wide, tail):
        x1, x2, x3 = split3(wide)
        tall = dot(rows[: 2 * period], stacked((x1, x2)))
        small = dot(rows[2 * period :], stacked((x3, x1)))
        return tall[:period] + (tall[period:] + small) + ends[:period] * tail

    def mixed(real, imag):
        real_cos, real_sin = halves(real)
        imag_cos, imag_sin = halves(imag)
        return (
            jnp.concatenate([real_cos - imag_sin, real_cos + imag_sin], axis=1),
            jnp.concatenate([real_sin + imag_cos, imag_cos - real_sin], axis=1),
        )

    planes = along_lanes([kern[c, start + k] for k in range(parts) for c in range(2)])
    for k in range(parts):
        to = first_out + k
        (real, real_tail), (imag, imag_tail) = planes[2 * k : 2 * k + 2]
        wide_re, wide_im = mixed(real, imag)
        tail_re, tail_im = mixed(real_tail, imag_tail)
        tall_re = along_rows(wide_re, tail_re)
        tall_im = along_rows(wide_im, tail_im)
        out[0, to, :half] = tall_re[:half] - tall_im[half:]
        out[0, to, half:] = tall_re[:half] + tall_im[half:]
        out[1, to, :half] = tall_im[:half] + tall_re[half:]
        out[1, to, half:] = tall_im[:half] - tall_re[half:]


def pack(x):
    count = x.shape[0] // 2
    return jnp.concatenate([x[:count], x[count:]], axis=1)


def unpack(x):
    width = x.shape[1] // 2
    return jnp.concatenate([x[:, :width], x[:, width:]], axis=0)


def own_kernel(latent, transmit, token):
    transmit[...] = 0.5 * (1.0 + jnp.tanh(latent[...]))
    token[...] = jnp.zeros(token.shape, F32)


def band_kernel(middle, partner, outside, after, band, token):
    tile = middle.shape[0]
    radius = (band.shape[1] - tile) // 2
    lower, other = place_in_pair("tx")

    near = jnp.where(lower, partner[:, :radius], partner[:, tile - radius :])
    far = jnp.where(lower, outside[:, tile - radius :], outside[:, :radius])
    far = jnp.where(other, far, 0.0)
    band[:, :radius] = jnp.where(lower, far, near)
    band[:, radius : radius + tile] = middle[...]
    band[:, radius + tile :] = jnp.where(lower, near, far)
    token[...] = jnp.zeros(token.shape, F32)


def relay_rows_kernel(partner, after, rim, token):
    radius = rim.shape[0]
    tile = partner.shape[0]
    lower, _ = place_in_pair("ty")
    rim[...] = jnp.where(lower, partner[tile - radius :], partner[:radius])
    token[...] = jnp.zeros(token.shape, F32)


def fold_rows_kernel(grad, rim, out):
    radius = rim.shape[0]
    tile = out.shape[0]
    lower, _ = place_in_pair("ty")
    count, index = lax.axis_size("ty"), lax.axis_index("ty")
    comes = jnp.where(lower, index < count - 2, index > 1)
    outer = jnp.where(comes, rim[...], 0.0)
    top = jnp.where(lower, grad[radius + tile :], outer)
    bottom = jnp.where(lower, outer, grad[:radius])
    out[:radius] = top
    out[radius:] = jnp.zeros((tile - radius, out.shape[1]), F32)
    out[tile - radius :] += bottom


def fold_band_kernel(grad, partner, band, far):
    tile = band.shape[0]
    radius = far.shape[1] // 2
    lower, _ = place_in_pair("tx")
    band[...] = grad[radius : radius + tile] + partner[...]
    far[...] = jnp.where(lower, pack(band[:, :radius]), pack(band[:, radius + tile :]))


def near_rim_kernel(band, near):
    tile = band.shape[0]
    radius = near.shape[1] // 2
    lower, _ = place_in_pair("tx")
    near[...] = jnp.where(lower, pack(band[:, radius + tile :]), pack(band[:, :radius]))


def far_side_kernel(band, far, out):
    tile = out.shape[0]
    radius = (band.shape[1] - tile) // 2
    lower, other = place_in_pair("tx")
    outer = jnp.where(other, unpack(far[...]), 0.0)
    out[...] = band[:, radius : radius + tile]
    out[:, :radius] += jnp.where(lower, outer, 0.0)
    out[:, tile - radius :] += jnp.where(lower, 0.0, outer)


def finish_kernel(total, near, latent, steering):
    tile = latent.shape[0]
    radius = near.shape[1] // 2
    lower, _ = place_in_pair("tx")
    inner = unpack(near[...])
    steering[...] = total[...]
    steering[:, :radius] += jnp.where(lower, 0.0, inner)
    steering[:, tile - radius :] += jnp.where(lower, inner, 0.0)
    value = jnp.tanh(latent[...])
    steering[...] = steering[...] * 0.5 * (1.0 - value * value)


def total_weight(weights, kernels):
    total = weights[0]
    for k in range(1, kernels):
        total = total + weights[k]
    return jnp.full((1, 1), total, F32)


def sample_places(pixels, tile):
    row = ((pixels.astype(F32) + 0.5) * (1.0 / tile)).astype(jnp.int32)
    held = jnp.where(row < tile // 2, tile - 1 - row, row - tile // 2)
    return held, pixels - row * tile


def field_kernel(weights, band, partner, rim, pixels, slopes, tables, *rest):
    *spec, field_re, field_im, sampled, copies, framed, mask = rest
    kernels = weights.shape[0]
    period = band.shape[1]
    half = period // 2
    tile = field_re.shape[1]
    radius = rim.shape[0]
    lower, other = place_in_pair("ty")
    outer = jnp.where(other, rim[...], 0.0)
    framed[:radius] = jnp.where(lower, outer, partner[tile - radius :])
    framed[radius + tile :] = jnp.where(lower, partner[:radius], outer)
    framed[radius : radius + tile] = band[...]
    wide = dot6(split3(framed[...]), triple(tables, 0, period, 2 * LANES))
    tall = dot6(triple(tables, 3, period, period), split3(wide)) * (1.0 / (period * period))
    cos_cos, cos_sin = halves(tall[:half])
    sin_cos, sin_sin = halves(tall[half:])
    same, other = cos_cos - sin_sin, cos_cos + sin_sin
    joint, cross = sin_cos + cos_sin, sin_cos - cos_sin
    mask[0, :, :LANES], mask[0, :, LANES:] = same, other
    mask[1, :, :LANES], mask[1, :, LANES:] = -joint, -cross
    mask[2, :, :LANES], mask[2, :, LANES:] = other, same
    mask[3, :, :LANES], mask[3, :, LANES:] = cross, joint
    rows = tile // 2

    def lift(slot, x):
        x1, x2, x3 = split3(x)
        out = dot(tables[slot, : 3 * rows, :period], stacked((x1, x2)))
        small = dot(tables[slot, 3 * rows : 4 * rows, :half], x3)
        return out[:rows] + (out[rows:tile] + (out[tile:] + small))

    across = triple(tables, 6, 2 * LANES, LANES)
    across = (across[0], jnp.concatenate(across[:2], axis=1), across[2])

    def lifted(own, k):
        pos_re, pos_im = own[0, k, :half], own[1, k, :half]
        neg_re, neg_im = own[0, k, half:], own[1, k, half:]
        up_re = mask[0] * pos_re - mask[1] * pos_im
        up_im = mask[0] * pos_im + mask[1] * pos_re
        down_re = mask[2] * neg_re - mask[3] * neg_im
        down_im = mask[2] * neg_im + mask[3] * neg_re
        even_re = lift(9, up_re + down_re)
        even_im = lift(9, up_im + down_im)
        odd_re = lift(10, up_im - down_im)
        odd_im = lift(10, up_re - down_re)
        re_pos, re_neg = halves(stacked((even_re - odd_re, even_re + odd_re)))
        im_pos, im_neg = halves(stacked((even_im + odd_im, even_im - odd_im)))
        rows_re = jnp.concatenate([re_pos + re_neg, im_neg - im_pos], axis=1)
        rows_im = jnp.concatenate([im_pos + im_neg, re_pos - re_neg], axis=1)
        return [rows_re, rows_im]

    intensity = jnp.zeros((tile, LANES), F32)
    places = [(own, k) for own in spec for k in range(own.shape[1])]
    for first in range(0, kernels, FIELD_BATCH):
        lines = stacked([line for i in range(FIELD_BATCH) for line in lifted(*places[first + i])])
        x1, x2, x3 = split3(lines)
        most, more = halves(dot(x1, across[1]))
        some, small = halves(dot(x2, across[1]))
        both = small + dot(x1, across[2]) + dot(x3, across[0]) + (more + some) + most
        for i in range(FIELD_BATCH):
            real = both[2 * i * tile : (2 * i + 1) * tile]
            imag = both[(2 * i + 1) * tile : (2 * i + 2) * tile]
            field_re[first + i] = real
            field_im[first + i] = imag
            intensity = intensity + weights[first + i] * (real * real + imag * imag)
    intensity = intensity / total_weight(weights, kernels)
    samples = pixels.shape[1]
    row, col = sample_places(pixels[...], tile)
    in_col = lax.broadcasted_iota(jnp.int32, (LANES, samples), 0) == col
    one_hot = jnp.where(in_col, 1.0, 0.0).astype(BF16)
    high, rest = split(intensity)
    low = intensity - high.astype(F32) - rest.astype(F32)
    picked = dot(high, one_hot) + dot(rest, one_hot) + dot(low.astype(BF16), one_hot)
    in_row = lax.broadcasted_iota(jnp.int32, (tile, samples), 0) == row
    own = jnp.sum(jnp.where(in_row, picked, 0.0), axis=0, keepdims=True)
    sampled[...] = jnp.concatenate([own, slopes[...]], axis=1)
    copies[...] = jnp.broadcast_to(sampled[...][None], copies.shape)


def sigmoid(x):
    return 1.0 / (1.0 + jnp.exp(-x))


def errors(intensity, slope, dose):
    resist = 0.5 * jnp.tanh(0.5 * STEEPNESS * (dose * intensity - RESIST_LEVEL))
    offset = resist * slope
    return resist, offset, offset * offset


def source_kernel(weights, doses, pick, gathered, sampled, pixels, placed_sum, tail):
    kernels = weights.shape[0]
    tile = placed_sum.shape[0]
    samples = pixels.shape[1]
    devices = gathered.shape[0]
    corners = doses.shape[0]
    per_corner = devices * samples
    everyone, every_slope = gathered[:, :samples], gathered[:, samples:]
    pick_corner = pick[0] // per_corner
    remain = pick[0] - pick_corner * per_corner
    place = lax.broadcasted_iota(jnp.int32, (devices, samples), 0) * samples
    place = place + lax.broadcasted_iota(jnp.int32, (devices, samples), 1)
    _, _, picked = errors(everyone, every_slope, doses[pick_corner])
    threshold = jnp.sum(jnp.where(place == remain, picked, 0.0), keepdims=True)

    def corner(c, sums):
        _, _, error = errors(everyone, every_slope, doses[c])
        soft = sigmoid((error - threshold) * (1.0 / SOFTNESS))
        return sums[0] + soft, sums[1] + error * soft

    zero = jnp.zeros((devices, samples), F32)
    soft_sum, error_sum = lax.fori_loop(
        0, corners, corner, (zero, zero), unroll=8 if devices <= 32 else 1
    )
    soft_total = jnp.sum(soft_sum, keepdims=True)
    tail_mean = jnp.sum(error_sum, keepdims=True) / soft_total
    tail[...] = tail_mean

    own, slope = sampled[:, :samples], sampled[:, samples:]
    which = lax.broadcasted_iota(jnp.int32, (corners, samples), 0)
    dose = jnp.zeros((corners, samples), F32)
    for c in range(corners):
        dose = jnp.where(which == c, doses[c], dose)
    resist, offset, error = errors(own, slope, dose)
    soft = sigmoid((error - threshold) * (1.0 / SOFTNESS))
    slope_soft = soft * (1.0 - soft) * (1.0 / SOFTNESS)
    chain = 2.0 * STEEPNESS * offset * slope * dose * (0.25 - resist * resist)
    coefficient = (soft + (error - tail_mean) * slope_soft) * (corners * per_corner / soft_total)
    summed = jnp.sum(coefficient * chain, axis=0, keepdims=True)
    summed = summed / total_weight(weights, kernels)

    row, col = sample_places(pixels[...], tile)
    in_row = lax.broadcasted_iota(jnp.int32, (tile, samples), 0) == row
    in_col = lax.broadcasted_iota(jnp.int32, (LANES, samples), 0) == col
    one_hot = jnp.where(in_col, 1.0, 0.0).astype(BF16)
    placed = jnp.where(in_row, summed, 0.0)
    high, rest = split(placed)
    low = (placed - high.astype(F32) - rest.astype(F32)).astype(BF16)
    grid = jnp.zeros((tile, LANES), F32)
    for part in (high, rest, low):
        grid = grid + lax.dot_general(
            part, one_hot, (((1,), (1,)), ((), ())), preferred_element_type=F32
        )

    placed_sum[...] = grid


def gradient_kernel(weights, grid, field_re, field_im, tables, *rest):
    *spec, grad, rim, total_re, total_im = rest
    period = grad.shape[0]
    half = period // 2
    tile = field_re.shape[1]
    radius = (period - tile) // 2
    cols = pair(tables, 0, LANES, 2 * LANES)
    cols = (stacked((cols[0], cols[0])), cols[1])
    rows = tile // 2
    cos_rows = tables[6, :half, : 3 * rows]
    sin_rows = tables[6, half:period, : 3 * rows]

    def along_rows(wide):
        out = []
        for table, x in (
            (cos_rows, wide[:rows] + wide[rows:]),
            (sin_rows, wide[:rows] - wide[rows:]),
        ):
            high, low = split(x)
            out.append(dot(table, stacked((high, low, high))))
        return out

    total_re[...] = jnp.zeros((period, 2 * LANES), F32)
    total_im[...] = jnp.zeros((period, 2 * LANES), F32)

    places = [(own, k) for own in spec for k in range(own.shape[1])]
    for group in range(len(places) // BATCH):
        sources = []
        for i in range(BATCH):
            k = group * BATCH + i
            weighted = grid[...] * weights[k]
            sources += [weighted * field_re[k], weighted * field_im[k]]
        high, low = split(stacked(sources))
        both = dot(jnp.concatenate([high, low], axis=1), cols[0]) + dot(high, cols[1])
        for i in range(BATCH):
            own, at = places[group * BATCH + i]
            real_cos, real_sin = halves(both[2 * i * tile : (2 * i + 1) * tile])
            imag_cos, imag_sin = halves(both[(2 * i + 1) * tile : (2 * i + 2) * tile])
            wide_re = jnp.concatenate([real_cos + imag_sin, real_cos - imag_sin], axis=1)
            wide_im = jnp.concatenate([imag_cos - real_sin, imag_cos + real_sin], axis=1)
            cos_re, sin_re = along_rows(wide_re)
            cos_im, sin_im = along_rows(wide_im)
            for start, sign in ((0, 1.0), (half, -1.0)):
                part = slice(start, start + half)
                wave_re = cos_re + sign * sin_im
                wave_im = cos_im - sign * sin_re
                own_re, own_im = own[0, at, part], own[1, at, part]
                total_re[part] += own_re * wave_re + own_im * wave_im
                total_im[part] += own_re * wave_im - own_im * wave_re

    pos_re, neg_re = total_re[:half], total_re[half:]
    pos_im, neg_im = total_im[:half], total_im[half:]
    back_rows = pair(tables, 4, period, period)
    back_rows = (back_rows[0], stacked(back_rows))
    for_re = jnp.concatenate([pos_re + neg_re, neg_im - pos_im], axis=0)
    for_im = jnp.concatenate([pos_im + neg_im, pos_re - neg_re], axis=0)
    re_pos, re_neg = halves(dot3_stacked(back_rows, split(for_re)))
    im_pos, im_neg = halves(dot3_stacked(back_rows, split(for_im)))
    last = jnp.concatenate([re_pos + re_neg, im_neg - im_pos], axis=1)
    framed = dot3(split(last), pair(tables, 2, 2 * LANES, period)) * (2.0 / (period * period))
    grad[...] = framed
    lower, _ = place_in_pair("ty")
    rim[...] = jnp.where(lower, framed[:radius], framed[radius + tile :])


VMEM = pl.BlockSpec(memory_space=pltpu.VMEM)
SMEM = pl.BlockSpec(memory_space=pltpu.SMEM)
ANY = pl.BlockSpec(memory_space=pl.ANY)


def shape(*dims):
    return jax.ShapeDtypeStruct(dims, F32)


def call(kernel, name, out_shape, in_specs, scratch=(), aliases=None, micros=1):
    return pl.pallas_call(
        kernel,
        out_shape=out_shape,
        in_specs=in_specs,
        out_specs=[VMEM] * len(out_shape),
        scratch_shapes=scratch,
        input_output_aliases=aliases or {},
        compiler_params=pltpu.CompilerParams(vmem_limit_bytes=10 * 1024 * 1024),
        cost_estimate=pl.CostEstimate(
            flops=micros * 10**9, bytes_accessed=2**20, transcendentals=0
        ),
        name=name,
    )


def gather_all(copies):
    return lax.all_to_all(copies, ("ty", "tx"), 0, 0, tiled=True)


def body(latent, kernels, socs_weights, dose_scale, inv_slope, edge_pixels, threshold_pick):
    tile = latent.shape[0]
    count, taps = kernels.shape[1], kernels.shape[-1]
    samples = edge_pixels.shape[1]
    radius = (taps - 1) // 2
    period = tile + 2 * radius
    half = period // 2
    first_tables = [jnp.asarray(x) for x in spectra_tables(period, taps - 1)]
    tables = jnp.asarray(field_tables(period, tile))
    last_tables = jnp.asarray(gradient_tables(period, tile))
    token = shape(8, LANES)
    packed = shape(tile // 2, 2 * radius)
    devices = lax.axis_size("ty") * lax.axis_size("tx")

    def spectra(start, first_out, parts, size, after, into=()):
        return call(
            functools.partial(spectra_kernel, start, first_out, parts),
            "spectra",
            [shape(2, size, period, 2 * LANES), token],
            [VMEM] * 4 + [ANY] * (1 + len(into)),
            aliases={5: 0} if into else None,
            micros=parts // 2,
        )(kernels, *first_tables, after, *into)

    transmit, done = call(
        own_kernel, "own", [shape(tile, tile), token], [VMEM], micros=3
    )(latent)
    partner, outside = swap("tx", transmit), swap_outside("tx", transmit)
    small, few = count // 3, count // 6
    large = count - small
    spec_a, done = spectra(0, 0, small, small, done)
    band, done = call(
        band_kernel, "band", [shape(tile, period), token], [VMEM] * 3 + [ANY]
    )(transmit, partner, outside, done)
    partner = swap("ty", band)
    spec_b, done = spectra(small, 0, few, large, done)
    rim, done = call(
        relay_rows_kernel, "relay", [shape(radius, period), token], [VMEM, ANY]
    )(partner, done)
    rim = ring("ty", rim)
    spec_b, _ = spectra(small + few, few, large - few, large, done, (spec_b,))
    spec = [spec_a, spec_b]

    field_re, field_im, sampled, copies = call(
        field_kernel,
        "field",
        [shape(count, tile, LANES)] * 2
        + [shape(1, 2 * samples), shape(devices, 1, 2 * samples)],
        [SMEM] + [VMEM] * (6 + len(spec)),
        scratch=[
            pltpu.VMEM((period, period), F32),
            pltpu.VMEM((4, half, 2 * LANES), F32),
        ],
        micros=7,
    )(socs_weights, band, partner, rim, edge_pixels, inv_slope, tables, *spec)

    gathered = gather_all(copies).reshape(devices, 2 * samples)
    grid, tail_mean = call(
        source_kernel,
        "source",
        [shape(tile, LANES), shape(1, 1)],
        [SMEM] * 3 + [VMEM] * 3,
        micros=2,
    )(socs_weights, dose_scale, threshold_pick, gathered, sampled, edge_pixels)
    grad, rim = call(
        gradient_kernel,
        "gradient",
        [shape(period, period), shape(radius, period)],
        [SMEM] + [VMEM] * (4 + len(spec)),
        scratch=[pltpu.VMEM((period, 2 * LANES), F32)] * 2,
        micros=6,
    )(socs_weights, grid, field_re, field_im, last_tables, *spec)

    rim = ring("ty", rim, back=True)
    (partner,) = call(fold_rows_kernel, "fold", [shape(tile, period)], [VMEM] * 2)(
        grad, rim
    )
    partner = swap("ty", partner)
    band, far = call(
        fold_band_kernel, "fold", [shape(tile, period), packed], [VMEM] * 2
    )(grad, partner)
    far = swap_outside("tx", far)
    (near,) = call(near_rim_kernel, "near", [packed], [VMEM])(band)
    near = swap("tx", near)
    (total,) = call(far_side_kernel, "far", [shape(tile, tile)], [VMEM] * 2)(band, far)
    (steering,) = call(finish_kernel, "finish", [shape(tile, tile)], [VMEM] * 3)(
        total, near, latent
    )
    return (steering, tail_mean.reshape(1))


def solution(mesh):
    placed = (P("ty", "tx"), P(), P(), P(), P("ty", "tx"), P("ty", "tx"), P())
    return jax.shard_map(
        body, mesh=mesh, in_specs=placed, out_specs=(P("ty", "tx"), P()), check_vma=False
    )
```
